32 devices in a mesh: row: 8 (over y, x, core), col: 4 (over z).
Axes of the slice: x: 2, y: 2, z: 4, core: 2. Of those that a mesh axis runs over, the one named last changes fastest.
Arguments:
- amplitudes: bfloat16 [8192, 8192], P('row', 'col'), may hold values from -6 to 6
- integrals: bfloat16 [8192, 1024], P('col', 'row'), may hold values from -0.0625 to 0.0625
- tile_mask: int32 [64, 64], P('row', 'col'), may hold values 0 or 1
Outputs:
- residual: bfloat16 [8192, 1024], P('row', 'col')
The draws below stay inside these ranges and needn't reach their ends.
All inputs are finite; a program needn't handle non-finite values. No bound on the sum of `tile_mask` on one device may be relied on, other than what follows from the above.
Results may differ from the reference program's by a relative error of at most 0.001.
Values may be sent and summed in bfloat16 or wider, within the bound.
No kernel may reach another device: no remote copies, remote signals or barrier semaphores. Data moves between devices by JAX's collectives and lax.ppermute only.
A program may use at most 64 MiB of HBM per device.

```python
import jax
import jax.numpy as jnp

TILE = 128
AB_COLS = 1024
MT = 64
KT = 64
MROWS = 8192
KDIM = 8192


def place_ends(array, stream_key, smallest, high):
    longest = array.shape.index(max(array.shape))
    spots = []
    for shift in (0, 1):
        where = [jax.random.randint(jax.random.fold_in(stream_key, axis), (), 0, length) for axis, length in enumerate(array.shape)]
        where[longest] = (where[longest] + shift) % array.shape[longest]
        spots.append(tuple(where))
    return array.at[spots[0]].set(smallest).at[spots[1]].set(high)


def shard_levels(key, shape, split, low, largest):
    def one(dim, parts):
        heights = jax.random.uniform(jax.random.fold_in(jax.random.fold_in(key, 6), dim), (parts,), jnp.float32, low / len(split), largest / len(split))
        return jnp.repeat(jnp.exp(heights), shape[dim] // parts).reshape((-1,) + (1,) * (len(shape) - dim - 1))

    gain = one(*split[0])
    for cut in split[1:]:
        gain = gain * one(*cut)
    return gain


def gaussian(rng, dims, deviation, limit, cuts=(), held_as=jnp.bfloat16):
    values = jax.random.normal(rng, dims, jnp.float32) * deviation
    if len(cuts) > 0:
        values = shard_levels(rng, dims, cuts, -0.22, 0.18) * values
    return jnp.clip(values, min=-limit, max=limit).astype(held_as)


def setup_inputs(seed: int = 0) -> dict:
    arg_keys = jax.random.split(jax.random.key(seed), 4)
    amplitudes = gaussian(arg_keys[0], (MROWS, KDIM), 1.0, 6.0, ((0, 8), (1, 4)))
    integrals = gaussian(arg_keys[1], (KDIM, AB_COLS), KDIM ** -0.5, 0.0625, ((0, 4), (1, 8)))
    tile_mask = place_ends((jax.random.randint(arg_keys[2], (MT, KT), 0, 2) < 1).astype(jnp.int32), jax.random.fold_in(arg_keys[2], 1), 0, 1)
    return dict(amplitudes=amplitudes, integrals=integrals, tile_mask=tile_mask)


def reference(amplitudes, integrals, tile_mask):
    tiles_m, tiles_k = tile_mask.shape
    blocks = amplitudes.reshape(tiles_m, TILE, tiles_k, TILE)
    weights = tile_mask.astype(amplitudes.dtype)[:, None, :, None]
    masked = (blocks * weights).reshape(amplitudes.shape)
    return jnp.dot(masked, integrals, preferred_element_type=jnp.float32).astype(jnp.bfloat16)
```

```python
import functools

import jax
import jax.numpy as jnp
from jax import lax
from jax.experimental import pallas as pl
from jax.experimental.pallas import tpu as pltpu
from jax.sharding import PartitionSpec as P

TILE = 128
CODE_ROWS = 16
LEVELS = 32767.0
STEPS_PER_OCTAVE = 64.0
BLOCK_ROWS = 256


def apply_mask(amplitudes, tile_mask):
    tiles_m, tiles_k = tile_mask.shape
    tile_rows = amplitudes.shape[0] // tiles_m
    tile_cols = amplitudes.shape[1] // tiles_k
    blocks = amplitudes.reshape(tiles_m, tile_rows, tiles_k, tile_cols)
    weights = tile_mask.astype(amplitudes.dtype)[:, None, :, None]
    return (blocks * weights).reshape(amplitudes.shape)


def general(amplitudes, integrals, tile_mask):
    masked = apply_mask(amplitudes, tile_mask)
    partial_sums = jnp.dot(
        masked,
        lax.all_gather(integrals, "row", axis=1, tiled=True),
        preferred_element_type=jnp.float32,
    )
    summed = lax.psum_scatter(partial_sums, "col", scatter_dimension=1, tiled=True)
    return summed.astype(jnp.bfloat16)


def decode(ref, step, rows):
    groups = BLOCK_ROWS // TILE
    levels = ref[pl.ds(step * BLOCK_ROWS, BLOCK_ROWS), :].astype(jnp.int32).astype(jnp.float32)
    codes = ref[pl.ds(rows, CODE_ROWS), :].astype(jnp.int32).astype(jnp.float32)
    pieces = []
    which = lax.broadcasted_iota(jnp.int32, codes.shape, 0)
    for g in range(groups):
        code = jnp.sum(jnp.where(which == step * groups + g, codes, 0.0), axis=0, keepdims=True)
        unit = jnp.exp2(code / STEPS_PER_OCTAVE) / LEVELS
        pieces.append(levels[g * TILE : (g + 1) * TILE] * unit)
    return jnp.concatenate(pieces, axis=0)


def encode(acc, step, out_ref, code_ref, rows):
    groups = BLOCK_ROWS // TILE
    pieces = []
    for g in range(groups):
        part = acc[g * TILE : (g + 1) * TILE]
        largest = jnp.max(jnp.abs(part), axis=0, keepdims=True)
        code = jnp.ceil(jnp.log(jnp.maximum(largest, 1e-30)) * (STEPS_PER_OCTAVE / 0.6931471805599453))
        scaled = jnp.round(part * (jnp.exp2(-code / STEPS_PER_OCTAVE) * LEVELS))
        pieces.append(jnp.clip(scaled, -LEVELS, LEVELS).astype(jnp.int32))
        code_ref[pl.ds(step * groups + g, 1), :] = code
    out_ref[pl.ds(pl.multiple_of(step * BLOCK_ROWS, BLOCK_ROWS), BLOCK_ROWS), :] = jnp.concatenate(pieces, axis=0).astype(jnp.int16)

    @pl.when(step == pl.num_programs(0) - 1)
    def _():
        out_ref[pl.ds(rows, CODE_ROWS), :] = code_ref[...].astype(jnp.int32).astype(jnp.int16)


def kernel(arrived, last, rows, chunk_ref, a_ref, b_ref, *refs):
    step = pl.program_id(0)
    b = jnp.concatenate([b_ref[0], b_ref[1]], axis=1)
    acc = jnp.dot(a_ref[...], b, preferred_element_type=jnp.float32)
    for i in range(arrived):
        acc = acc + decode(refs[i], step, rows)
    if last:
        refs[arrived][...] = acc.astype(jnp.bfloat16)
    else:
        encode(acc, step, refs[arrived], refs[arrived + 1], rows)


def chunk_sums(chunk, masked, gathered, arrived=(), last=False):
    rows, depth = masked.shape
    width = gathered.shape[2] * 2
    packed = (rows + CODE_ROWS, width)
    if last:
        out_spec = pl.BlockSpec((BLOCK_ROWS, width), lambda i, c: (i, 0))
        out_shape = jax.ShapeDtypeStruct((rows, width), jnp.bfloat16)
        scratch = []
    else:
        out_spec = pl.BlockSpec(packed, lambda i, c: (0, 0))
        out_shape = jax.ShapeDtypeStruct(packed, jnp.int16)
        scratch = [pltpu.VMEM((CODE_ROWS, width), jnp.float32)]
    return pl.pallas_call(
        functools.partial(kernel, len(arrived), last, rows),
        out_shape=out_shape,
        grid_spec=pltpu.PrefetchScalarGridSpec(
            num_scalar_prefetch=1,
            grid=(rows // BLOCK_ROWS,),
            in_specs=[
                pl.BlockSpec((BLOCK_ROWS, depth), lambda i, c: (i, 0)),
                pl.BlockSpec((2, depth, width // 2), lambda i, c: (c[0], 0, 0)),
            ]
            + [pl.BlockSpec(packed, lambda i, c: (0, 0))] * len(arrived),
            out_specs=out_spec,
            scratch_shapes=scratch,
        ),
        compiler_params=pltpu.CompilerParams(vmem_limit_bytes=32 * 1024 * 1024),
        cost_estimate=pl.CostEstimate(
            flops=2 * rows * depth * width,
            bytes_accessed=2 * (rows * depth + depth * width + rows * width * (1 + len(arrived))),
            transcendentals=0,
        ),
    )(chunk, masked, gathered, *arrived)


def line_of_four(amplitudes, integrals, tile_mask):
    at = lax.axis_index("col")
    masked = apply_mask(amplitudes, tile_mask)
    gathered = lax.all_gather(integrals, "row", axis=0, tiled=False)

    def pick(*chunks):
        return jnp.asarray(chunks, jnp.int32)[at].reshape(1)

    def sums(chunk, arrived=(), last=False):
        return chunk_sums(chunk, masked, gathered, arrived, last)

    def send(block, pairs):
        return lax.ppermute(block, "col", pairs)

    first = send(sums(pick(3, 0, 3, 0)), [(0, 1), (1, 0), (2, 3), (3, 2)])
    second = send(sums(pick(2, 2, 1, 1)), [(0, 1), (3, 2)])
    third = send(sums(pick(1, 1, 2, 2)), [(0, 1), (3, 2)])
    far = send(sums(pick(3, 3, 0, 0), (first,)), [(1, 3), (2, 0)])
    near = send(sums(pick(2, 2, 1, 1), (second,)), [(1, 2), (2, 1)])
    outer = (at == 0) | (at == 3)
    one = jnp.where(outer, first, third)
    two = jnp.where(outer, far, near)
    return sums(pick(0, 1, 2, 3), (one, two), last=True)


def solution(mesh):
    body = line_of_four if mesh.shape["col"] == 4 and mesh.shape["row"] == 8 else general
    placed = (P("row", "col"), P("col", "row"), P("row", "col"))
    return jax.shard_map(
        body, mesh=mesh, in_specs=placed, out_specs=P("row", "col"), check_vma=False
    )
```

```python
import functools

import jax
import jax.numpy as jnp
from jax import lax
from jax.experimental import pallas as pl
from jax.experimental.pallas import tpu as pltpu
from jax.sharding import PartitionSpec as P

TILE = 128
CODE_ROWS = 16
LEVELS = 32767.0
STEPS_PER_OCTAVE = 64.0
BLOCK_ROWS = 256


def apply_mask(amplitudes, tile_mask):
    tiles_m, tiles_k = tile_mask.shape
    tile_rows = amplitudes.shape[0] // tiles_m
    tile_cols = amplitudes.shape[1] // tiles_k
    blocks = amplitudes.reshape(tiles_m, tile_rows, tiles_k, tile_cols)
    weights = tile_mask.astype(amplitudes.dtype)[:, None, :, None]
    return (blocks * weights).reshape(amplitudes.shape)


def general(amplitudes, integrals, tile_mask):
    masked = apply_mask(amplitudes, tile_mask)
    partial_sums = jnp.dot(
        masked,
        lax.all_gather(integrals, "row", axis=1, tiled=True),
        preferred_element_type=jnp.float32,
    )
    summed = lax.psum_scatter(partial_sums, "col", scatter_dimension=1, tiled=True)
    return summed.astype(jnp.bfloat16)


def decode(ref, step, rows, weight):
    groups = BLOCK_ROWS // TILE
    start = pl.multiple_of(step * BLOCK_ROWS, BLOCK_ROWS)
    levels = ref[pl.ds(start, BLOCK_ROWS), :].astype(jnp.int32).astype(jnp.float32)
    codes = ref[pl.ds(rows, CODE_ROWS), :].astype(jnp.int32).astype(jnp.float32)
    pieces = []
    which = lax.broadcasted_iota(jnp.int32, codes.shape, 0)
    for g in range(groups):
        code = jnp.sum(jnp.where(which == step * groups + g, codes, 0.0), axis=0, keepdims=True)
        unit = jnp.exp2(code / STEPS_PER_OCTAVE) * (weight / LEVELS)
        pieces.append(levels[g * TILE : (g + 1) * TILE] * unit)
    return jnp.concatenate(pieces, axis=0)


def encode(acc, step, out_ref, code_ref, rows):
    groups = BLOCK_ROWS // TILE
    pieces = []
    for g in range(groups):
        part = acc[g * TILE : (g + 1) * TILE]
        largest = jnp.max(jnp.abs(part), axis=0, keepdims=True)
        code = jnp.ceil(jnp.log(jnp.maximum(largest, 1e-30)) * (STEPS_PER_OCTAVE / 0.6931471805599453))
        scaled = jnp.round(part * (jnp.exp2(-code / STEPS_PER_OCTAVE) * LEVELS))
        pieces.append(jnp.clip(scaled, -LEVELS, LEVELS).astype(jnp.int32))
        code_ref[pl.ds(step * groups + g, 1), :] = code
    start = pl.multiple_of(step * BLOCK_ROWS, BLOCK_ROWS)
    out_ref[pl.ds(start, BLOCK_ROWS), :] = jnp.concatenate(pieces, axis=0).astype(jnp.int16)

    @pl.when(step == pl.num_programs(0) - 1)
    def _():
        out_ref[pl.ds(rows, CODE_ROWS), :] = code_ref[...].astype(jnp.int32).astype(jnp.int16)


def fetch(piece, chosen, core, own, mine, other, b, sems):
    half = b.shape[0] // 2

    def whole(ref):
        copy = pltpu.make_async_copy(ref, b, sems.at[0])
        copy.start()
        copy.wait()

    @pl.when((chosen == 0) & (core == piece))
    def _():
        whole(own[0])

    @pl.when((chosen == 0) & (core != piece))
    def _():
        whole(own[1])

    for j in range(3):

        @pl.when(chosen == j + 1)
        def _():
            here = pl.ds(pl.multiple_of(core * half, half), half)
            there = pl.ds(pl.multiple_of((1 - core) * half, half), half)
            near = pltpu.make_async_copy(mine[j], b.at[here], sems.at[0])
            far = pltpu.make_async_copy(other[j], b.at[there], sems.at[1])
            near.start()
            far.start()
            near.wait()
            far.wait()


def kernel(weights, beside, rows, piece, slot, facts, a_ref, *refs):
    arrived = len(weights)
    own, mine, other, refs = refs[:2], refs[2:5], refs[5:8], refs[8:]
    step = pl.program_id(0)
    blocks, refs = refs[:arrived], refs[arrived:]
    if beside:
        left_ref, refs = refs[0], refs[1:]
    out_ref, b, sems = refs[:3]

    @pl.when(step == 0)
    def _():
        fetch(piece, facts[slot] ^ facts[CHIP], facts[CORE], own, mine, other, b, sems)

    acc = jnp.dot(a_ref[...], b[...], preferred_element_type=jnp.float32)
    for i in range(arrived):
        acc = acc + decode(blocks[i], step, rows, facts[weights[i]].astype(jnp.float32))
    if out_ref.dtype != jnp.int16:
        acc = acc.astype(jnp.bfloat16)
        out_ref[...] = jnp.concatenate([left_ref[...], acc], axis=1) if beside else acc
    else:
        encode(acc, step, out_ref, refs[3], rows)


def chunk_sums(piece, slot, weights, facts, masked, columns, arrived=(), last=False, left=None):
    rows, depth = masked.shape
    width = columns[0].shape[1]
    packed = (rows + CODE_ROWS, width)
    scratch = [pltpu.VMEM((depth, width), masked.dtype), pltpu.SemaphoreType.DMA((2,))]
    beside = () if left is None else (left,)
    if last:
        total = width * (1 + len(beside))
        out_spec = pl.BlockSpec((BLOCK_ROWS, total), lambda i, c: (i, 0))
        out_shape = jax.ShapeDtypeStruct((rows, total), jnp.bfloat16)
    else:
        out_spec = pl.BlockSpec(packed, lambda i, c: (0, 0))
        out_shape = jax.ShapeDtypeStruct(packed, jnp.int16)
        scratch.append(pltpu.VMEM((CODE_ROWS, width), jnp.float32))
    return pl.pallas_call(
        functools.partial(kernel, weights, len(beside), rows, piece, slot),
        out_shape=out_shape,
        grid_spec=pltpu.PrefetchScalarGridSpec(
            num_scalar_prefetch=1,
            grid=(rows // BLOCK_ROWS,),
            in_specs=[pl.BlockSpec((BLOCK_ROWS, depth), lambda i, c: (i, 0))]
            + [pl.BlockSpec(memory_space=pl.ANY)] * len(columns)
            + [pl.BlockSpec(packed, lambda i, c: (0, 0))] * len(arrived)
            + [pl.BlockSpec((BLOCK_ROWS, width), lambda i, c: (i, 0))] * len(beside),
            out_specs=out_spec,
            scratch_shapes=scratch,
        ),
        compiler_params=pltpu.CompilerParams(vmem_limit_bytes=24 * 1024 * 1024),
        cost_estimate=pl.CostEstimate(flops=0, bytes_accessed=0, transcendentals=0),
    )(facts, masked, *columns, *arrived, *beside)


PLAN = (
    (3, 2, 3, 1, 2, 2, 1, 2, 0, 1, 1, 0),
    (0, 0, 0, 3, 2, 3, 0, 2, 1, 1, 0, 1),
    (3, 3, 3, 0, 1, 0, 3, 1, 2, 1, 0, 1),
    (0, 1, 0, 2, 1, 1, 2, 1, 3, 1, 1, 0),
)
ALWAYS, OUTER, INNER, CORE, CHIP = 9, 10, 11, 12, 13


def line_of_four(amplitudes, integrals, tile_mask):
    row = lax.axis_index("row")
    core, chip = row % 2, row // 2
    planned = lax.dynamic_slice_in_dim(jnp.asarray(PLAN, jnp.int32), lax.axis_index("col"), 1)[0]
    facts = jnp.concatenate([planned, jnp.stack([core, chip]).astype(jnp.int32)])
    masked = apply_mask(amplitudes, tile_mask)
    depth = integrals.shape[0]
    half = depth // 2

    def across(block, bit):
        return lax.ppermute(block, "row", [(i, i ^ bit) for i in range(8)])

    twin = across(integrals, 1)
    gathered = []
    for piece in range(2):
        low = integrals if piece == 0 else twin
        high = twin if piece == 0 else integrals
        mine = jnp.where(core == 0, low[:half], high[half:])
        pieces = [across(mine, bit) for bit in (2, 4, 6)]
        gathered.append((integrals, twin, *pieces, *[across(x, 1) for x in pieces]))

    latest = []

    def sums(after, piece, slot, arrived=(), weights=(), **kw):
        told = lax.optimization_barrier((facts, *latest, *after))[0]
        out = chunk_sums(piece, slot, weights, told, masked, gathered[piece], arrived, **kw)
        latest[:] = [out]
        return out

    def send(pairs, after, *what, **kw):
        return lax.ppermute(sums(after, *what, **kw), "col", pairs)

    swap = [(0, 1), (1, 0), (2, 3), (3, 2)]
    jump = [(0, 1), (1, 3), (2, 0), (3, 2)]
    middle = [(0, 0), (1, 2), (2, 1), (3, 3)]
    one = send(swap, (), 0, 0)
    two = send(swap, (), 0, 1)
    three = send(swap, (one,), 1, 2)
    four = send(jump, (two,), 0, 3, (one,), (INNER,))
    near_a = send(middle, (), 0, 4, (two,), (INNER,))
    five = send(jump, (three,), 1, 5, (three,), (INNER,))
    six = send(swap, (four,), 1, 6)
    ends = (OUTER, ALWAYS, INNER)
    left = sums((), 0, 8, (two, four, near_a), ends, last=True)
    near_b = send(middle, (five,), 1, 7, (five,), (INNER,))
    return sums((), 1, 8, (five, six, near_b), ends, last=True, left=left)


def solution(mesh):
    body = line_of_four if mesh.shape["col"] == 4 and mesh.shape["row"] == 8 else general
    placed = (P("row", "col"), P("col", "row"), P("row", "col"))
    return jax.shard_map(
        body, mesh=mesh, in_specs=placed, out_specs=P("row", "col"), check_vma=False
    )
```

```python
import functools

import jax
import jax.numpy as jnp
from jax import lax
from jax.experimental import pallas as pl
from jax.experimental.pallas import tpu as pltpu
from jax.sharding import PartitionSpec as P

TILE = 128
CODE_ROWS = 16
LEVELS = 32767.0
STEPS_PER_OCTAVE = 64.0
BLOCK_ROWS = 256
ADD_ROWS = 512


def apply_mask(amplitudes, tile_mask):
    tiles_m, tiles_k = tile_mask.shape
    tile_rows = amplitudes.shape[0] // tiles_m
    tile_cols = amplitudes.shape[1] // tiles_k
    blocks = amplitudes.reshape(tiles_m, tile_rows, tiles_k, tile_cols)
    weights = tile_mask.astype(amplitudes.dtype)[:, None, :, None]
    return (blocks * weights).reshape(amplitudes.shape)


def general(amplitudes, integrals, tile_mask):
    masked = apply_mask(amplitudes, tile_mask)
    partial_sums = jnp.dot(
        masked,
        lax.all_gather(integrals, "row", axis=1, tiled=True),
        preferred_element_type=jnp.float32,
    )
    summed = lax.psum_scatter(partial_sums, "col", scatter_dimension=1, tiled=True)
    return summed.astype(jnp.bfloat16)


def decode(ref, step, rows, block_rows, weight):
    groups = block_rows // TILE
    start = pl.multiple_of(step * block_rows, block_rows)
    levels = ref[pl.ds(start, block_rows), :].astype(jnp.int32).astype(jnp.float32)
    codes = ref[pl.ds(rows, CODE_ROWS), :].astype(jnp.int32).astype(jnp.float32)
    pieces = []
    which = lax.broadcasted_iota(jnp.int32, codes.shape, 0)
    for g in range(groups):
        code = jnp.sum(jnp.where(which == step * groups + g, codes, 0.0), axis=0, keepdims=True)
        unit = jnp.exp2(code / STEPS_PER_OCTAVE) * (weight / LEVELS)
        pieces.append(levels[g * TILE : (g + 1) * TILE] * unit)
    return jnp.concatenate(pieces, axis=0)


def encode(acc, step, out_ref, code_ref, rows):
    block_rows = acc.shape[0]
    groups = block_rows // TILE
    pieces = []
    for g in range(groups):
        part = acc[g * TILE : (g + 1) * TILE]
        largest = jnp.max(jnp.abs(part), axis=0, keepdims=True)
        code = jnp.ceil(jnp.log(jnp.maximum(largest, 1e-30)) * (STEPS_PER_OCTAVE / 0.6931471805599453))
        scaled = jnp.round(part * (jnp.exp2(-code / STEPS_PER_OCTAVE) * LEVELS))
        pieces.append(jnp.clip(scaled, -LEVELS, LEVELS).astype(jnp.int32))
        code_ref[pl.ds(step * groups + g, 1), :] = code
    start = pl.multiple_of(step * block_rows, block_rows)
    out_ref[pl.ds(start, block_rows), :] = jnp.concatenate(pieces, axis=0).astype(jnp.int16)

    @pl.when(step == pl.num_programs(0) - 1)
    def _():
        out_ref[pl.ds(rows, CODE_ROWS), :] = code_ref[...].astype(jnp.int32).astype(jnp.int16)


def fetch(chosen, core, own, mine, other, b, columns, sems):
    half = b.shape[0] // 2

    @pl.when(chosen == 0)
    def _():
        copy = pltpu.make_async_copy(own, b.at[:, columns], sems.at[0])
        copy.start()
        copy.wait()

    for j in range(3):

        @pl.when(chosen == j + 1)
        def _():
            here = pl.ds(pl.multiple_of(core * half, half), half)
            there = pl.ds(pl.multiple_of((1 - core) * half, half), half)
            near = pltpu.make_async_copy(mine[j], b.at[here, columns], sems.at[0])
            far = pltpu.make_async_copy(other[j], b.at[there, columns], sems.at[1])
            near.start()
            far.start()
            near.wait()
            far.wait()


def multiply_kernel(slots, kinds, rows, width, facts, a_ref, *refs):
    own, mine, other, refs = refs[0], refs[1:4], refs[4:7], refs[7:]
    count = sum(len(kind) for kind in kinds)
    outs, refs = list(refs[:count]), refs[count:]
    b, sems, codes = refs[0], refs[1], list(refs[2:])
    step = pl.program_id(0)

    @pl.when(step == 0)
    def _():
        for j, slot in enumerate(slots):
            fetch(facts[slot] ^ facts[CHIP], facts[CORE], own, mine, other, b, pl.ds(j * width, width), sems)

    acc = jnp.dot(a_ref[...], b[...], preferred_element_type=jnp.float32)
    for j, kind in enumerate(kinds):
        part = acc[:, j * width : (j + 1) * width]
        for form in kind:
            out_ref = outs.pop(0)
            if form == "coded":
                encode(part, step, out_ref, codes.pop(0), rows)
            else:
                out_ref[...] = part


def multiply(facts, masked, columns, slots, kinds):
    rows, depth = masked.shape
    width = columns[0].shape[1]
    packed = (rows + CODE_ROWS, width)
    forms = [form for kind in kinds for form in kind]
    coded = (pl.BlockSpec(packed, lambda i, c: (0, 0)), jax.ShapeDtypeStruct(packed, jnp.int16))
    plain = (pl.BlockSpec((BLOCK_ROWS, width), lambda i, c: (i, 0)), jax.ShapeDtypeStruct((rows, width), jnp.float32))
    outs = [coded if form == "coded" else plain for form in forms]
    return pl.pallas_call(
        functools.partial(multiply_kernel, slots, kinds, rows, width),
        out_shape=[shape for _, shape in outs],
        grid_spec=pltpu.PrefetchScalarGridSpec(
            num_scalar_prefetch=1,
            grid=(rows // BLOCK_ROWS,),
            in_specs=[pl.BlockSpec((BLOCK_ROWS, depth), lambda i, c: (i, 0))]
            + [pl.BlockSpec(memory_space=pl.ANY)] * len(columns),
            out_specs=[spec for spec, _ in outs],
            scratch_shapes=[pltpu.VMEM((depth, width * len(slots)), masked.dtype), pltpu.SemaphoreType.DMA((2,))]
            + [pltpu.VMEM((CODE_ROWS, width), jnp.float32)] * forms.count("coded"),
        ),
        compiler_params=pltpu.CompilerParams(vmem_limit_bytes=24 * 1024 * 1024),
        cost_estimate=pl.CostEstimate(flops=0, bytes_accessed=0, transcendentals=0),
    )(facts, masked, *columns)


def add_kernel(weights, beside, rows, facts, own_ref, *refs):
    step = pl.program_id(0)
    blocks, refs = refs[: len(weights)], refs[len(weights) :]
    acc = own_ref[...]
    for weight, block in zip(weights, blocks):
        acc = acc + decode(block, step, rows, acc.shape[0], facts[weight].astype(jnp.float32))
    out_ref = refs[beside]
    if out_ref.dtype == jnp.int16:
        encode(acc, step, out_ref, refs[beside + 1], rows)
    else:
        acc = acc.astype(out_ref.dtype)
        out_ref[...] = jnp.concatenate([refs[0][...], acc], axis=1) if beside else acc


def add(facts, own, arrived, weights, last=False, left=None):
    rows, width = own.shape
    packed = (rows + CODE_ROWS, width)
    beside = () if left is None else (left,)
    plain = pl.BlockSpec((ADD_ROWS, width), lambda i, c: (i, 0))
    if last:
        total = width * (1 + len(beside))
        out_spec = pl.BlockSpec((ADD_ROWS, total), lambda i, c: (i, 0))
        out_shape = jax.ShapeDtypeStruct((rows, total), jnp.bfloat16)
        scratch = []
    else:
        out_spec = pl.BlockSpec(packed, lambda i, c: (0, 0))
        out_shape = jax.ShapeDtypeStruct(packed, jnp.int16)
        scratch = [pltpu.VMEM((CODE_ROWS, width), jnp.float32)]
    return pl.pallas_call(
        functools.partial(add_kernel, weights, len(beside), rows),
        out_shape=out_shape,
        grid_spec=pltpu.PrefetchScalarGridSpec(
            num_scalar_prefetch=1,
            grid=(rows // ADD_ROWS,),
            in_specs=[plain]
            + [pl.BlockSpec(packed, lambda i, c: (0, 0))] * len(arrived)
            + [plain] * len(beside),
            out_specs=out_spec,
            scratch_shapes=scratch,
        ),
        compiler_params=pltpu.CompilerParams(vmem_limit_bytes=16 * 1024 * 1024),
        cost_estimate=pl.CostEstimate(flops=0, bytes_accessed=0, transcendentals=0),
    )(facts, own, *arrived, *beside)


PLAN = (
    (3, 2, 1, 2, 1, 0, 1, 1, 0),
    (2, 0, 3, 3, 0, 1, 1, 0, 1),
    (1, 3, 0, 0, 3, 2, 1, 0, 1),
    (0, 1, 2, 1, 2, 3, 1, 1, 0),
)
FIRST, SECOND_A, THIRD_A, SECOND_B, THIRD_B, HERE, ALWAYS, OUTER, INNER, CORE, CHIP = range(11)


def line_of_four(amplitudes, integrals, tile_mask):
    row = lax.axis_index("row")
    core, chip = row % 2, row // 2
    half = integrals.shape[0] // 2

    def after(value, *others):
        return lax.optimization_barrier((value, *others))[0]

    def across(block, bit):
        return lax.ppermute(block, "row", [(i, i ^ bit) for i in range(8)])

    def choose(low, high):
        return jnp.where(core == 0, low, high)

    def along(block, pairs):
        return lax.ppermute(block, "col", pairs)

    twin = across(integrals, 1)
    mine_a = choose(integrals[:half], twin[half:])
    own, pair, tile_mask, plan = lax.optimization_barrier(
        (integrals, twin, tile_mask, jnp.asarray(PLAN, jnp.int32), mine_a)
    )[:4]
    masked = apply_mask(amplitudes, tile_mask)
    planned = lax.dynamic_slice_in_dim(plan, lax.axis_index("col"), 1)[0]
    facts = jnp.concatenate([planned, jnp.stack([core, chip]).astype(jnp.int32)])
    mine_b = choose(pair[:half], own[half:])
    own, pair = lax.optimization_barrier((own, pair, mine_b))[:2]
    whole_a, whole_b = choose(own, pair), choose(pair, own)

    got_a = [across(mine_a, bit) for bit in (2, 4, 6)]
    ready = (masked, facts, whole_a, whole_b)
    swapped_a = [across(after(x, *ready), 1) for x in got_a]
    columns_a = (whole_a, *got_a, *swapped_a)
    got_b = [across(after(mine_b, got_a[0]), bit) for bit in (2, 4, 6)]

    swap = [(0, 1), (1, 0), (2, 3), (3, 2)]
    jump = [(0, 1), (1, 3), (2, 0), (3, 2)]
    middle = [(0, 0), (1, 2), (2, 1), (3, 3)]
    ends = (OUTER, ALWAYS, INNER)
    coded, plain = ("coded",), ("plain",)
    out_one, first_a = multiply(facts, masked, columns_a, (FIRST,), (coded + plain,))
    one = along(out_one, swap)
    out_two, third_a, here_a = multiply(
        after(facts, out_one), masked, columns_a, (SECOND_A, THIRD_A, HERE), (coded, plain, plain)
    )
    two = along(out_two, swap)
    swapped_b = [across(after(x, out_two), 1) for x in got_b]
    columns_b = (whole_b, *got_b, *swapped_b)
    out_three, first_b, second_b, out_six, here_b = multiply(
        after(facts, out_two, one), masked, columns_b,
        (FIRST, SECOND_B, THIRD_B, HERE), (coded + plain, plain, coded, plain),
    )
    three = along(out_three, swap)
    out_four = add(after(facts, out_three, two), third_a, (one,), (INNER,))
    four = along(out_four, jump)
    out_near = add(after(facts, out_four), first_a, (two,), (INNER,))
    near_a = along(out_near, middle)
    out_five = add(after(facts, out_near), second_b, (three,), (INNER,))
    five = along(out_five, jump)
    six = along(after(out_six, out_five, four), swap)
    left = add(after(facts, out_five, four), here_a, (two, four, near_a), ends, last=True)
    out_near_b = add(after(facts, left), first_b, (five,), (INNER,))
    near_b = along(out_near_b, middle)
    return add(after(facts, out_near_b), here_b, (five, six, near_b), ends, last=True, left=left)


def solution(mesh):
    body = line_of_four if mesh.shape["col"] == 4 and mesh.shape["row"] == 8 else general
    placed = (P("row", "col"), P("col", "row"), P("row", "col"))
    return jax.shard_map(
        body, mesh=mesh, in_specs=placed, out_specs=P("row", "col"), check_vma=False
    )
```

```python
import functools

import jax
import jax.numpy as jnp
from jax import lax
from jax.experimental import pallas as pl
from jax.experimental.pallas import tpu as pltpu
from jax.sharding import PartitionSpec as P

TILE = 128
CODE_ROWS = 16
LEVELS = 32767.0
STEPS_PER_OCTAVE = 64.0
BLOCK_ROWS = 256
ADD_ROWS = 512


def apply_mask(amplitudes, tile_mask):
    tiles_m, tiles_k = tile_mask.shape
    tile_rows = amplitudes.shape[0] // tiles_m
    tile_cols = amplitudes.shape[1] // tiles_k
    blocks = amplitudes.reshape(tiles_m, tile_rows, tiles_k, tile_cols)
    weights = tile_mask.astype(amplitudes.dtype)[:, None, :, None]
    return (blocks * weights).reshape(amplitudes.shape)


def general(amplitudes, integrals, tile_mask):
    masked = apply_mask(amplitudes, tile_mask)
    partial_sums = jnp.dot(
        masked,
        lax.all_gather(integrals, "row", axis=1, tiled=True),
        preferred_element_type=jnp.float32,
    )
    summed = lax.psum_scatter(partial_sums, "col", scatter_dimension=1, tiled=True)
    return summed.astype(jnp.bfloat16)


def decode(ref, step, rows, block_rows, weight):
    groups = block_rows // TILE
    start = pl.multiple_of(step * block_rows, block_rows)
    levels = ref[pl.ds(start, block_rows), :].astype(jnp.int32).astype(jnp.float32)
    codes = ref[pl.ds(rows, CODE_ROWS), :].astype(jnp.int32).astype(jnp.float32)
    pieces = []
    which = lax.broadcasted_iota(jnp.int32, codes.shape, 0)
    for g in range(groups):
        code = jnp.sum(jnp.where(which == step * groups + g, codes, 0.0), axis=0, keepdims=True)
        unit = jnp.exp2(code / STEPS_PER_OCTAVE) * (weight / LEVELS)
        pieces.append(levels[g * TILE : (g + 1) * TILE] * unit)
    return jnp.concatenate(pieces, axis=0)


def encode(acc, step, out_ref, code_ref, rows):
    block_rows = acc.shape[0]
    groups = block_rows // TILE
    pieces = []
    for g in range(groups):
        part = acc[g * TILE : (g + 1) * TILE]
        largest = jnp.max(jnp.abs(part), axis=0, keepdims=True)
        code = jnp.ceil(jnp.log(jnp.maximum(largest, 1e-30)) * (STEPS_PER_OCTAVE / 0.6931471805599453))
        scaled = jnp.round(part * (jnp.exp2(-code / STEPS_PER_OCTAVE) * LEVELS))
        pieces.append(jnp.clip(scaled, -LEVELS, LEVELS).astype(jnp.int32))
        code_ref[pl.ds(step * groups + g, 1), :] = code
    start = pl.multiple_of(step * block_rows, block_rows)
    out_ref[pl.ds(start, block_rows), :] = jnp.concatenate(pieces, axis=0).astype(jnp.int16)

    @pl.when(step == pl.num_programs(0) - 1)
    def _():
        out_ref[pl.ds(rows, CODE_ROWS), :] = code_ref[...].astype(jnp.int32).astype(jnp.int16)


def fetch(chosen, core, whole, mine, other, b, columns, sems):
    half = b.shape[0] // 2

    @pl.when(chosen == 0)
    def _():
        copy = pltpu.make_async_copy(whole, b.at[:, columns], sems.at[0])
        copy.start()
        copy.wait()

    for j in range(3):

        @pl.when(chosen == j + 1)
        def _():
            copies = []
            for parts, side in ((mine[j], core), (other[j], 1 - core)):
                start = side * half
                for part in parts:
                    rows = pl.ds(pl.multiple_of(start, part.shape[0]), part.shape[0])
                    copies.append(pltpu.make_async_copy(part, b.at[rows, columns], sems.at[len(copies)]))
                    start = start + part.shape[0]
            for copy in copies:
                copy.start()
            for copy in copies:
                copy.wait()


def multiply_kernel(slots, kinds, rows, width, facts, a_ref, *refs):
    whole, mine, other, refs = refs[0], (refs[1:2], refs[2:3], refs[3:5]), (refs[5:6], refs[6:7], refs[7:9]), refs[9:]
    count = sum(len(kind) for kind in kinds)
    outs, refs = list(refs[:count]), refs[count:]
    b, sems, codes = refs[0], refs[1], list(refs[2:])
    step = pl.program_id(0)

    @pl.when(step == 0)
    def _():
        for j, slot in enumerate(slots):
            fetch(facts[slot] ^ facts[CHIP], facts[CORE], whole, mine, other, b, pl.ds(j * width, width), sems)

    acc = jnp.dot(a_ref[...], b[...], preferred_element_type=jnp.float32)
    for j, kind in enumerate(kinds):
        part = acc[:, j * width : (j + 1) * width]
        for form in kind:
            out_ref = outs.pop(0)
            if form == "coded":
                encode(part, step, out_ref, codes.pop(0), rows)
            else:
                out_ref[...] = part


def multiply(facts, masked, columns, slots, kinds):
    rows, depth = masked.shape
    width = columns[0].shape[1]
    packed = (rows + CODE_ROWS, width)
    forms = [form for kind in kinds for form in kind]
    coded = (pl.BlockSpec(packed, lambda i, c: (0, 0)), jax.ShapeDtypeStruct(packed, jnp.int16))
    plain = (pl.BlockSpec((BLOCK_ROWS, width), lambda i, c: (i, 0)), jax.ShapeDtypeStruct((rows, width), jnp.float32))
    outs = [coded if form == "coded" else plain for form in forms]
    return pl.pallas_call(
        functools.partial(multiply_kernel, slots, kinds, rows, width),
        out_shape=[shape for _, shape in outs],
        grid_spec=pltpu.PrefetchScalarGridSpec(
            num_scalar_prefetch=1,
            grid=(rows // BLOCK_ROWS,),
            in_specs=[pl.BlockSpec((BLOCK_ROWS, depth), lambda i, c: (i, 0))]
            + [pl.BlockSpec(memory_space=pl.ANY)] * len(columns),
            out_specs=[spec for spec, _ in outs],
            scratch_shapes=[pltpu.VMEM((depth, width * len(slots)), masked.dtype), pltpu.SemaphoreType.DMA((4,))]
            + [pltpu.VMEM((CODE_ROWS, width), jnp.float32)] * forms.count("coded"),
        ),
        compiler_params=pltpu.CompilerParams(vmem_limit_bytes=24 * 1024 * 1024),
        cost_estimate=pl.CostEstimate(flops=0, bytes_accessed=0, transcendentals=0),
    )(facts, masked, *columns)


def add_kernel(terms, beside, rows, facts, *refs):
    step = pl.program_id(0)
    blocks, refs = refs[: len(terms)], refs[len(terms) :]
    acc = None
    for block, weight in zip(blocks, terms):
        share = facts[weight].astype(jnp.float32)
        if block.dtype == jnp.int16:
            value = decode(block, step, rows, ADD_ROWS, share)
        else:
            value = block[...] if weight == ALWAYS else block[...] * share
        acc = value if acc is None else acc + value
    out_ref = refs[beside]
    if out_ref.dtype == jnp.int16:
        encode(acc, step, out_ref, refs[beside + 1], rows)
    else:
        acc = acc.astype(out_ref.dtype)
        out_ref[...] = jnp.concatenate([refs[0][...], acc], axis=1) if beside else acc


def add(facts, terms, dtype=jnp.int16, left=None):
    rows, width = next(x.shape for x, _ in terms if x.dtype == jnp.float32)
    packed = (rows + CODE_ROWS, width)
    beside = () if left is None else (left,)
    plain = pl.BlockSpec((ADD_ROWS, width), lambda i, c: (i, 0))
    coded = pl.BlockSpec(packed, lambda i, c: (0, 0))
    if dtype == jnp.int16:
        out_spec, out_shape = coded, jax.ShapeDtypeStruct(packed, dtype)
        scratch = [pltpu.VMEM((CODE_ROWS, width), jnp.float32)]
    else:
        total = width * (1 + len(beside))
        out_spec = pl.BlockSpec((ADD_ROWS, total), lambda i, c: (i, 0))
        out_shape = jax.ShapeDtypeStruct((rows, total), dtype)
        scratch = []
    return pl.pallas_call(
        functools.partial(add_kernel, tuple(weight for _, weight in terms), len(beside), rows),
        out_shape=out_shape,
        grid_spec=pltpu.PrefetchScalarGridSpec(
            num_scalar_prefetch=1,
            grid=(rows // ADD_ROWS,),
            in_specs=[coded if x.dtype == jnp.int16 else plain for x, _ in terms] + [plain] * len(beside),
            out_specs=out_spec,
            scratch_shapes=scratch,
        ),
        compiler_params=pltpu.CompilerParams(vmem_limit_bytes=16 * 1024 * 1024),
        cost_estimate=pl.CostEstimate(flops=0, bytes_accessed=0, transcendentals=0),
    )(facts, *[x for x, _ in terms], *beside)


PLAN = (
    (3, 2, 1, 0, 1, 1, 0),
    (0, 2, 3, 1, 1, 0, 1),
    (3, 1, 0, 2, 1, 0, 1),
    (0, 1, 2, 3, 1, 1, 0),
)
FIRST, SECOND, THIRD, HERE, ALWAYS, OUTER, INNER, CORE, CHIP = range(9)


def line_of_four(amplitudes, integrals, tile_mask):
    row = lax.axis_index("row")
    core, chip = row % 2, row // 2
    half = integrals.shape[0] // 2

    def after(value, *others):
        return lax.optimization_barrier((value, *others))[0]

    def across(block, bit):
        return lax.ppermute(block, "row", [(i, i ^ bit) for i in range(8)])

    def choose(low, high):
        return jnp.where(core == 0, low, high)

    def along(block, pairs):
        return lax.ppermute(block, "col", pairs)

    twin = across(integrals, 1)
    mine_a = choose(integrals[:half], twin[half:])
    own, pair, tile_mask, plan = lax.optimization_barrier(
        (integrals, twin, tile_mask, jnp.asarray(PLAN, jnp.int32), mine_a)
    )[:4]
    masked = apply_mask(amplitudes, tile_mask)
    planned = lax.dynamic_slice_in_dim(plan, lax.axis_index("col"), 1)[0]
    facts = jnp.concatenate([planned, jnp.stack([core, chip]).astype(jnp.int32)])
    mine_b = choose(pair[:half], own[half:])
    own, pair = lax.optimization_barrier((own, pair, mine_b))[:2]
    whole_a, whole_b = choose(own, pair), choose(pair, own)

    def relay(by_x, by_y):
        quarter = half // 2
        return across(by_y[:quarter], 2), across(by_x[quarter:], 4)

    got_a = [across(mine_a, 2), across(mine_a, 4)]
    ready = (masked, facts, whole_a, whole_b)
    got_a = [after(x, *ready) for x in got_a]
    got_a += relay(*got_a)
    columns_a = (whole_a, *got_a, *[across(x, 1) for x in got_a])
    ready_b = after(mine_b, *got_a[2:])
    got_b = [across(ready_b, 2), across(ready_b, 4)]

    pairs = [(0, 1), (1, 0), (2, 3), (3, 2)]
    inward = [(0, 1), (3, 2)]
    jump = [(0, 1), (1, 3), (2, 0), (3, 2)]
    middle = [(1, 2), (2, 1)]
    coded, plain = ("coded",), ("plain",)
    (out_one,) = multiply(facts, masked, columns_a, (FIRST,), (coded,))
    one = along(out_one, pairs)
    out_two, second_a, third_a, here_a = multiply(
        after(facts, out_one), masked, columns_a, (SECOND, THIRD, HERE), (coded + plain, plain, plain)
    )
    two = along(out_two, inward)
    got_b += relay(*[after(x, out_one) for x in got_b])
    columns_b = (whole_b, *got_b, *[across(after(x, out_two), 1) for x in got_b])
    out_three, second_b, out_six, third_b, here_b = multiply(
        after(facts, out_two, one), masked, columns_b,
        (FIRST, SECOND, THIRD, HERE), (coded, plain, coded + plain, plain),
    )
    three = along(out_three, pairs)
    out_near_a = add(after(facts, out_three), [(second_a, ALWAYS), (two, INNER)])
    near_a = along(out_near_a, middle)
    out_four = add(after(facts, out_near_a), [(second_b, OUTER), (third_a, INNER), (one, INNER)])
    four = along(out_four, jump)
    out_five = add(after(facts, out_four), [(third_a, OUTER), (third_b, INNER), (three, INNER)])
    five = along(out_five, jump)
    out_near_b = add(after(facts, out_five), [(second_b, ALWAYS), (four, INNER)])
    near_b = along(out_near_b, middle)
    six = along(after(out_six, out_near_b), inward)
    left = add(
        after(facts, out_near_b),
        [(here_a, ALWAYS), (one, OUTER), (four, OUTER), (five, INNER), (near_a, INNER)],
        jnp.bfloat16,
    )
    most_b = add(
        after(facts, left),
        [(here_b, ALWAYS), (three, OUTER), (five, OUTER), (near_b, INNER)],
        jnp.float32,
    )
    return add(facts, [(most_b, ALWAYS), (six, INNER)], jnp.bfloat16, left)


def solution(mesh):
    body = line_of_four if mesh.shape["col"] == 4 and mesh.shape["row"] == 8 else general
    placed = (P("row", "col"), P("col", "row"), P("row", "col"))
    return jax.shard_map(
        body, mesh=mesh, in_specs=placed, out_specs=P("row", "col"), check_vma=False
    )
```

```python
import functools

import jax
import jax.numpy as jnp
from jax import lax
from jax.experimental import pallas as pl
from jax.experimental.pallas import tpu as pltpu
from jax.sharding import PartitionSpec as P

TILE = 128
CODE_ROWS = 16
LEVELS = 32767.0
STEPS_PER_OCTAVE = 64.0
BLOCK_ROWS = 256
ADD_ROWS = 512


def apply_mask(amplitudes, tile_mask):
    tiles_m, tiles_k = tile_mask.shape
    tile_rows = amplitudes.shape[0] // tiles_m
    tile_cols = amplitudes.shape[1] // tiles_k
    blocks = amplitudes.reshape(tiles_m, tile_rows, tiles_k, tile_cols)
    weights = tile_mask.astype(amplitudes.dtype)[:, None, :, None]
    return (blocks * weights).reshape(amplitudes.shape)


def general(amplitudes, integrals, tile_mask):
    masked = apply_mask(amplitudes, tile_mask)
    partial_sums = jnp.dot(
        masked,
        lax.all_gather(integrals, "row", axis=1, tiled=True),
        preferred_element_type=jnp.float32,
    )
    summed = lax.psum_scatter(partial_sums, "col", scatter_dimension=1, tiled=True)
    return summed.astype(jnp.bfloat16)


def decode(ref, step, rows, block_rows, weight):
    groups = block_rows // TILE
    start = pl.multiple_of(step * block_rows, block_rows)
    levels = ref[pl.ds(start, block_rows), :].astype(jnp.int32).astype(jnp.float32)
    codes = ref[pl.ds(rows, CODE_ROWS), :].astype(jnp.int32).astype(jnp.float32)
    pieces = []
    which = lax.broadcasted_iota(jnp.int32, codes.shape, 0)
    for g in range(groups):
        code = jnp.sum(jnp.where(which == step * groups + g, codes, 0.0), axis=0, keepdims=True)
        unit = jnp.exp2(code / STEPS_PER_OCTAVE) * (weight / LEVELS)
        pieces.append(levels[g * TILE : (g + 1) * TILE] * unit)
    return jnp.concatenate(pieces, axis=0)


def encode(acc, step, out_ref, code_ref, rows):
    block_rows = acc.shape[0]
    groups = block_rows // TILE
    pieces = []
    for g in range(groups):
        part = acc[g * TILE : (g + 1) * TILE]
        largest = jnp.max(jnp.abs(part), axis=0, keepdims=True)
        code = jnp.ceil(jnp.log(jnp.maximum(largest, 1e-30)) * (STEPS_PER_OCTAVE / 0.6931471805599453))
        scaled = jnp.round(part * (jnp.exp2(-code / STEPS_PER_OCTAVE) * LEVELS))
        pieces.append(jnp.clip(scaled, -LEVELS, LEVELS).astype(jnp.int32))
        code_ref[pl.ds(step * groups + g, 1), :] = code
    start = pl.multiple_of(step * block_rows, block_rows)
    out_ref[pl.ds(start, block_rows), :] = jnp.concatenate(pieces, axis=0).astype(jnp.int16)

    @pl.when(step == pl.num_programs(0) - 1)
    def _():
        out_ref[pl.ds(rows, CODE_ROWS), :] = code_ref[...].astype(jnp.int32).astype(jnp.int16)


def pack_kernel(own, left, right):
    half, side = own.shape[0] // 2, own.shape[1] // 2
    top, bottom = own[:half], own[half:]
    left[...] = jnp.concatenate([top[:, :side], bottom[:, :side]], axis=1)
    right[...] = jnp.concatenate([top[:, side:], bottom[:, side:]], axis=1)


def pack(own):
    depth, width = own.shape
    shape = jax.ShapeDtypeStruct((depth // 2, width), own.dtype)
    return pl.pallas_call(pack_kernel, out_shape=(shape, shape))(own)


def multiply_kernel(slots, kinds, rows, width, facts, a_ref, *refs):
    mine, other, refs = refs[:4], refs[4:8], refs[8:]
    count = sum(len(kind) for kind in kinds)
    outs, refs = list(refs[:count]), refs[count:]
    b, packs, sems, codes = refs[0], refs[1], refs[2], list(refs[3:])
    step = pl.program_id(0)
    half, side = b.shape[0] // 2, width // 2

    @pl.when(step == 0)
    def _():
        core = facts[CORE]

        def copies(j, s):
            return (
                pltpu.make_async_copy(mine[s], packs.at[j, core], sems.at[j, 0]),
                pltpu.make_async_copy(other[s], packs.at[j, 1 - core], sems.at[j, 1]),
            )

        for j, slot in enumerate(slots):
            for s in range(4):

                @pl.when((facts[slot] ^ facts[CHIP]) == s)
                def _():
                    for copy in copies(j, s):
                        copy.start()

        for j in range(len(slots)):
            for copy in copies(j, 0):
                copy.wait()
            columns = slice(j * width, (j + 1) * width)
            one, two = packs[j, 0], packs[j, 1]
            b[:half, columns] = jnp.concatenate([one[:, :side], two[:, :side]], axis=1)
            b[half:, columns] = jnp.concatenate([one[:, side:], two[:, side:]], axis=1)

    block = pl.ds(pl.multiple_of(step * BLOCK_ROWS, BLOCK_ROWS), BLOCK_ROWS)
    acc = jnp.dot(a_ref[block, :], b[...], preferred_element_type=jnp.float32)
    for j, kind in enumerate(kinds):
        part = acc[:, j * width : (j + 1) * width]
        for form in kind:
            out_ref = outs.pop(0)
            if form == "coded":
                encode(part, step, out_ref, codes.pop(0), rows)
            else:
                out_ref[...] = part


def multiply(facts, masked, columns, slots, kinds):
    rows, depth = masked.shape
    width = columns[0].shape[1]
    packed = (rows + CODE_ROWS, width)
    forms = [form for kind in kinds for form in kind]
    coded = (pl.BlockSpec(packed, lambda i, c: (0, 0)), jax.ShapeDtypeStruct(packed, jnp.int16))
    plain = (pl.BlockSpec((BLOCK_ROWS, width), lambda i, c: (i, 0)), jax.ShapeDtypeStruct((rows, width), jnp.float32))
    outs = [coded if form == "coded" else plain for form in forms]
    return pl.pallas_call(
        functools.partial(multiply_kernel, slots, kinds, rows, width),
        out_shape=[shape for _, shape in outs],
        grid_spec=pltpu.PrefetchScalarGridSpec(
            num_scalar_prefetch=1,
            grid=(rows // BLOCK_ROWS,),
            in_specs=[pl.BlockSpec(memory_space=pltpu.VMEM)]
            + [pl.BlockSpec(memory_space=pl.ANY)] * len(columns),
            out_specs=[spec for spec, _ in outs],
            scratch_shapes=[
                pltpu.VMEM((depth, width * len(slots)), masked.dtype),
                pltpu.VMEM((len(slots), 2, depth // 2, width), masked.dtype),
                pltpu.SemaphoreType.DMA((len(slots), 2)),
            ]
            + [pltpu.VMEM((CODE_ROWS, width), jnp.float32)] * forms.count("coded"),
        ),
        compiler_params=pltpu.CompilerParams(vmem_limit_bytes=24 * 1024 * 1024),
        cost_estimate=pl.CostEstimate(flops=1000, bytes_accessed=1000, transcendentals=0),
    )(facts, masked, *columns)


def add_kernel(terms, beside, rows, facts, *refs):
    step = pl.program_id(0)
    blocks, refs = refs[: len(terms)], refs[len(terms) :]
    acc = None
    for block, weight in zip(blocks, terms):
        share = facts[weight].astype(jnp.float32)
        if block.dtype == jnp.int16:
            value = decode(block, step, rows, ADD_ROWS, share)
        else:
            value = block[...] if weight == ALWAYS else block[...] * share
        acc = value if acc is None else acc + value
    out_ref = refs[beside]
    if out_ref.dtype == jnp.int16:
        encode(acc, step, out_ref, refs[beside + 1], rows)
    else:
        if beside:
            first, side = refs[0][...], acc.shape[1] // 2
            acc = jnp.concatenate([first[:, :side], acc[:, :side], first[:, side:], acc[:, side:]], axis=1)
        out_ref[...] = acc.astype(out_ref.dtype)


def add(facts, terms, dtype=jnp.int16, left=None):
    rows, width = next(x.shape for x, _ in terms if x.dtype == jnp.float32)
    packed = (rows + CODE_ROWS, width)
    beside = () if left is None else (left,)
    plain = pl.BlockSpec((ADD_ROWS, width), lambda i, c: (i, 0))
    coded = pl.BlockSpec(packed, lambda i, c: (0, 0))
    if dtype == jnp.int16:
        out_spec, out_shape = coded, jax.ShapeDtypeStruct(packed, dtype)
        scratch = [pltpu.VMEM((CODE_ROWS, width), jnp.float32)]
    else:
        total = width * (1 + len(beside))
        out_spec = pl.BlockSpec((ADD_ROWS, total), lambda i, c: (i, 0))
        out_shape = jax.ShapeDtypeStruct((rows, total), dtype)
        scratch = []
    return pl.pallas_call(
        functools.partial(add_kernel, tuple(weight for _, weight in terms), len(beside), rows),
        out_shape=out_shape,
        grid_spec=pltpu.PrefetchScalarGridSpec(
            num_scalar_prefetch=1,
            grid=(rows // ADD_ROWS,),
            in_specs=[coded if x.dtype == jnp.int16 else plain for x, _ in terms] + [plain] * len(beside),
            out_specs=out_spec,
            scratch_shapes=scratch,
        ),
        compiler_params=pltpu.CompilerParams(vmem_limit_bytes=16 * 1024 * 1024),
        cost_estimate=pl.CostEstimate(flops=1000, bytes_accessed=1000, transcendentals=0),
    )(facts, *[x for x, _ in terms], *beside)


PLAN = (
    (3, 2, 1, 0, 1, 1, 0),
    (0, 2, 3, 1, 1, 0, 1),
    (3, 1, 0, 2, 1, 0, 1),
    (0, 1, 2, 3, 1, 1, 0),
)
FIRST, SECOND, THIRD, HERE, ALWAYS, OUTER, INNER, CORE, CHIP = range(9)


def line_of_four(amplitudes, integrals, tile_mask):
    row = lax.axis_index("row")
    core, chip = row % 2, row // 2

    def after(value, *others):
        return lax.optimization_barrier((value, *others))[0]

    def across(block, bit):
        return lax.ppermute(block, "row", [(i, i ^ bit) for i in range(8)])

    def along(block, pairs):
        return lax.ppermute(block, "col", pairs)

    pack_a, pack_b = pack(integrals)
    tile_mask, plan = lax.optimization_barrier((tile_mask, jnp.asarray(PLAN, jnp.int32), pack_a))[:2]
    masked = apply_mask(amplitudes, tile_mask)
    planned = lax.dynamic_slice_in_dim(plan, lax.axis_index("col"), 1)[0]
    facts = jnp.concatenate([planned, jnp.stack([core, chip]).astype(jnp.int32)])

    got_a = [across(pack_a, bit) for bit in (2, 4, 6)]
    got_a = [after(x, masked, facts) for x in got_a]
    columns_a = (pack_a, *got_a, *[across(x, 1) for x in (pack_a, *got_a)])
    later = after(pack_b, *got_a)
    got_b = [across(later, bit) for bit in (2, 4, 6)]

    pairs = [(0, 1), (1, 0), (2, 3), (3, 2)]
    inward = [(0, 1), (3, 2)]
    jump = [(0, 1), (1, 3), (2, 0), (3, 2)]
    middle = [(1, 2), (2, 1)]
    coded, plain = ("coded",), ("plain",)
    (out_one,) = multiply(facts, masked, columns_a, (FIRST,), (coded,))
    one = along(out_one, pairs)
    out_two, second_a, third_a, here_a = multiply(
        after(facts, out_one), masked, columns_a, (SECOND, THIRD, HERE), (coded + plain, plain, plain)
    )
    two = along(out_two, inward)
    columns_b = (pack_b, *got_b, *[across(after(x, out_two), 1) for x in (pack_b, *got_b)])
    (out_three,) = multiply(after(facts, out_two, one), masked, columns_b, (FIRST,), (coded,))
    three = along(out_three, pairs)
    out_four, second_b, third_b, here_b = multiply(
        after(facts, out_three, two), masked, columns_b, (SECOND, THIRD, HERE), (coded + plain, plain, plain)
    )
    four = along(out_four, inward)
    out_near_a = add(after(facts, out_four), [(second_a, ALWAYS), (two, INNER)])
    near_a = along(out_near_a, middle)
    out_five = add(after(facts, out_near_a), [(third_a, ALWAYS), (one, INNER)])
    five = along(out_five, jump)
    out_six = add(after(facts, out_five), [(third_b, ALWAYS), (three, INNER)])
    six = along(out_six, jump)
    out_near_b = add(after(facts, out_six), [(second_b, ALWAYS), (four, INNER)])
    near_b = along(out_near_b, middle)
    left = add(
        after(facts, out_near_b),
        [(here_a, ALWAYS), (one, OUTER), (five, ALWAYS), (near_a, INNER)],
        jnp.float32,
    )
    most_b = add(after(facts, left), [(here_b, ALWAYS), (three, OUTER), (near_b, INNER)], jnp.float32)
    return add(facts, [(most_b, ALWAYS), (six, ALWAYS)], jnp.bfloat16, left)


def solution(mesh):
    body = line_of_four if mesh.shape["col"] == 4 and mesh.shape["row"] == 8 else general
    placed = (P("row", "col"), P("col", "row"), P("row", "col"))
    return jax.shard_map(
        body, mesh=mesh, in_specs=placed, out_specs=P("row", "col"), check_vma=False
    )
```

```python
import functools

import jax
import jax.numpy as jnp
from jax import lax
from jax.experimental import pallas as pl
from jax.experimental.pallas import tpu as pltpu
from jax.sharding import PartitionSpec as P

TILE = 128
CODE_ROWS = 16
LEVELS = 32767.0
STEPS_PER_OCTAVE = 64.0
BLOCK_ROWS = 256
ADD_ROWS = 512


def apply_mask(amplitudes, tile_mask):
    tiles_m, tiles_k = tile_mask.shape
    tile_rows = amplitudes.shape[0] // tiles_m
    tile_cols = amplitudes.shape[1] // tiles_k
    blocks = amplitudes.reshape(tiles_m, tile_rows, tiles_k, tile_cols)
    weights = tile_mask.astype(amplitudes.dtype)[:, None, :, None]
    return (blocks * weights).reshape(amplitudes.shape)


def general(amplitudes, integrals, tile_mask):
    masked = apply_mask(amplitudes, tile_mask)
    partial_sums = jnp.dot(
        masked,
        lax.all_gather(integrals, "row", axis=1, tiled=True),
        preferred_element_type=jnp.float32,
    )
    summed = lax.psum_scatter(partial_sums, "col", scatter_dimension=1, tiled=True)
    return summed.astype(jnp.bfloat16)


def decode(ref, step, rows, block_rows, weight):
    groups = block_rows // TILE
    start = pl.multiple_of(step * block_rows, block_rows)
    levels = ref[pl.ds(start, block_rows), :].astype(jnp.int32).astype(jnp.float32)
    codes = ref[pl.ds(rows, CODE_ROWS), :].astype(jnp.int32).astype(jnp.float32)
    pieces = []
    which = lax.broadcasted_iota(jnp.int32, codes.shape, 0)
    for g in range(groups):
        code = jnp.sum(jnp.where(which == step * groups + g, codes, 0.0), axis=0, keepdims=True)
        unit = jnp.exp2(code / STEPS_PER_OCTAVE) * (weight / LEVELS)
        pieces.append(levels[g * TILE : (g + 1) * TILE] * unit)
    return jnp.concatenate(pieces, axis=0)


def encode(acc, step, out_ref, code_ref, rows):
    block_rows = acc.shape[0]
    groups = block_rows // TILE
    pieces = []
    for g in range(groups):
        part = acc[g * TILE : (g + 1) * TILE]
        largest = jnp.max(jnp.abs(part), axis=0, keepdims=True)
        code = jnp.ceil(jnp.log(jnp.maximum(largest, 1e-30)) * (STEPS_PER_OCTAVE / 0.6931471805599453))
        scaled = jnp.round(part * (jnp.exp2(-code / STEPS_PER_OCTAVE) * LEVELS))
        pieces.append(jnp.clip(scaled, -LEVELS, LEVELS).astype(jnp.int32))
        code_ref[pl.ds(step * groups + g, 1), :] = code
    start = pl.multiple_of(step * block_rows, block_rows)
    out_ref[pl.ds(start, block_rows), :] = jnp.concatenate(pieces, axis=0).astype(jnp.int16)

    @pl.when(step == pl.num_programs(0) - 1)
    def _():
        out_ref[pl.ds(rows, CODE_ROWS), :] = code_ref[...].astype(jnp.int32).astype(jnp.int16)


def fetch(chosen, core, whole, mine, other, b, columns, sem):
    half = b.shape[0] // 2

    @pl.when(chosen == 0)
    def _():
        pltpu.make_async_copy(whole, b.at[:, columns], sem).start()

    for j in range(3):

        @pl.when(chosen == j + 1)
        def _():
            here = pl.ds(pl.multiple_of(core * half, half), half)
            there = pl.ds(pl.multiple_of((1 - core) * half, half), half)
            pltpu.make_async_copy(mine[j], b.at[here, columns], sem).start()
            pltpu.make_async_copy(other[j], b.at[there, columns], sem).start()


def multiply_kernel(slots, kinds, rows, width, facts, a_ref, *refs):
    whole, mine, other, refs = refs[0], refs[1:4], refs[4:7], refs[7:]
    count = sum(len(kind) for kind in kinds)
    outs, refs = list(refs[:count]), refs[count:]
    b, sems, codes = refs[0], refs[1], list(refs[2:])
    step = pl.program_id(0)

    @pl.when(step == 0)
    def _():
        spans = [pl.ds(j * width, width) for j in range(len(slots))]
        for j, slot in enumerate(slots):
            fetch(facts[slot] ^ facts[CHIP], facts[CORE], whole, mine, other, b, spans[j], sems.at[j])
        for j, span in enumerate(spans):
            pltpu.make_async_copy(whole, b.at[:, span], sems.at[j]).wait()

    acc = jnp.dot(a_ref[...], b[...], preferred_element_type=jnp.float32)
    for j, kind in enumerate(kinds):
        part = acc[:, j * width : (j + 1) * width]
        for form in kind:
            out_ref = outs.pop(0)
            if form == "coded":
                encode(part, step, out_ref, codes.pop(0), rows)
            else:
                out_ref[...] = part


def multiply(facts, masked, columns, slots, kinds):
    rows, depth = masked.shape
    width = columns[0].shape[1]
    packed = (rows + CODE_ROWS, width)
    forms = [form for kind in kinds for form in kind]
    coded = (pl.BlockSpec(packed, lambda i, c: (0, 0)), jax.ShapeDtypeStruct(packed, jnp.int16))
    plain = (pl.BlockSpec((BLOCK_ROWS, width), lambda i, c: (i, 0)), jax.ShapeDtypeStruct((rows, width), jnp.float32))
    outs = [coded if form == "coded" else plain for form in forms]
    return pl.pallas_call(
        functools.partial(multiply_kernel, slots, kinds, rows, width),
        out_shape=[shape for _, shape in outs],
        grid_spec=pltpu.PrefetchScalarGridSpec(
            num_scalar_prefetch=1,
            grid=(rows // BLOCK_ROWS,),
            in_specs=[pl.BlockSpec((BLOCK_ROWS, depth), lambda i, c: (i, 0))]
            + [pl.BlockSpec(memory_space=pl.ANY)] * len(columns),
            out_specs=[spec for spec, _ in outs],
            scratch_shapes=[pltpu.VMEM((depth, width * len(slots)), masked.dtype), pltpu.SemaphoreType.DMA((4,))]
            + [pltpu.VMEM((CODE_ROWS, width), jnp.float32)] * forms.count("coded"),
        ),
        compiler_params=pltpu.CompilerParams(vmem_limit_bytes=24 * 1024 * 1024),
        cost_estimate=pl.CostEstimate(flops=3000000000, bytes_accessed=9000000, transcendentals=0),
    )(facts, masked, *columns)


def add_kernel(terms, beside, rows, facts, *refs):
    step = pl.program_id(0)
    blocks, refs = refs[: len(terms)], refs[len(terms) :]
    acc = None
    for block, weight in zip(blocks, terms):
        share = facts[weight].astype(jnp.float32)
        if block.dtype == jnp.int16:
            value = decode(block, step, rows, ADD_ROWS, share)
        else:
            value = block[...] if weight == ALWAYS else block[...] * share
        acc = value if acc is None else acc + value
    out_ref = refs[beside]
    if out_ref.dtype == jnp.int16:
        encode(acc, step, out_ref, refs[beside + 1], rows)
    else:
        acc = acc.astype(out_ref.dtype)
        out_ref[...] = jnp.concatenate([refs[0][...], acc], axis=1) if beside else acc


def add(facts, terms, dtype=jnp.int16, left=None):
    rows, width = next(x.shape for x, _ in terms if x.dtype == jnp.float32)
    packed = (rows + CODE_ROWS, width)
    beside = () if left is None else (left,)
    plain = pl.BlockSpec((ADD_ROWS, width), lambda i, c: (i, 0))
    coded = pl.BlockSpec(packed, lambda i, c: (0, 0))
    if dtype == jnp.int16:
        out_spec, out_shape = coded, jax.ShapeDtypeStruct(packed, dtype)
        scratch = [pltpu.VMEM((CODE_ROWS, width), jnp.float32)]
    else:
        total = width * (1 + len(beside))
        out_spec = pl.BlockSpec((ADD_ROWS, total), lambda i, c: (i, 0))
        out_shape = jax.ShapeDtypeStruct((rows, total), dtype)
        scratch = []
    return pl.pallas_call(
        functools.partial(add_kernel, tuple(weight for _, weight in terms), len(beside), rows),
        out_shape=out_shape,
        grid_spec=pltpu.PrefetchScalarGridSpec(
            num_scalar_prefetch=1,
            grid=(rows // ADD_ROWS,),
            in_specs=[coded if x.dtype == jnp.int16 else plain for x, _ in terms] + [plain] * len(beside),
            out_specs=out_spec,
            scratch_shapes=scratch,
        ),
        compiler_params=pltpu.CompilerParams(vmem_limit_bytes=16 * 1024 * 1024),
        cost_estimate=pl.CostEstimate(flops=3000000000, bytes_accessed=9000000, transcendentals=0),
    )(facts, *[x for x, _ in terms], *beside)


PLAN = (
    (3, 2, 1, 0, 1, 1, 0),
    (0, 2, 3, 1, 1, 0, 1),
    (3, 1, 0, 2, 1, 0, 1),
    (0, 1, 2, 3, 1, 1, 0),
)
FIRST, SECOND, THIRD, HERE, ALWAYS, OUTER, INNER, CORE, CHIP = range(9)


def line_of_four(amplitudes, integrals, tile_mask):
    row = lax.axis_index("row")
    core, chip = row % 2, row // 2
    half = integrals.shape[0] // 2

    def after(value, *others):
        return lax.optimization_barrier((value, *others))[0]

    def across(block, bit):
        return lax.ppermute(block, "row", [(i, i ^ bit) for i in range(8)])

    def choose(low, high):
        return jnp.where(core == 0, low, high)

    def along(block, pairs):
        return lax.ppermute(block, "col", pairs)

    twin = across(integrals, 1)
    mine_a = choose(integrals[:half], twin[half:])
    own, pair, tile_mask, plan = lax.optimization_barrier(
        (integrals, twin, tile_mask, jnp.asarray(PLAN, jnp.int32), mine_a)
    )[:4]
    masked = apply_mask(amplitudes, tile_mask)
    planned = lax.dynamic_slice_in_dim(plan, lax.axis_index("col"), 1)[0]
    facts = jnp.concatenate([planned, jnp.stack([core, chip]).astype(jnp.int32)])
    mine_b = choose(pair[:half], own[half:])
    own, pair = lax.optimization_barrier((own, pair, mine_b))[:2]
    whole_a, whole_b = choose(own, pair), choose(pair, own)

    got_a = [across(mine_a, bit) for bit in (2, 4, 6)]
    swapped_a = [across(after(x, masked, facts, whole_a, whole_b), 1) for x in got_a]
    columns_a = (whole_a, *got_a, *swapped_a)
    got_b = [across(after(mine_b, got_a[0]), bit) for bit in (2, 4, 6)]

    pairs = [(0, 1), (1, 0), (2, 3), (3, 2)]
    inward = [(0, 1), (3, 2)]
    jump = [(0, 1), (1, 3), (2, 0), (3, 2)]
    middle = [(1, 2), (2, 1)]
    coded, plain = ("coded",), ("plain",)
    (out_one,) = multiply(facts, masked, columns_a, (FIRST,), (coded,))
    one = along(out_one, pairs)
    out_two, second_a, third_a, here_a = multiply(
        after(facts, out_one), masked, columns_a, (SECOND, THIRD, HERE), (coded + plain, plain, plain)
    )
    two = along(out_two, inward)
    out_three = add(after(facts, out_two), [(third_a, ALWAYS), (one, INNER)])
    three = along(out_three, jump)
    out_near_a = add(after(facts, out_three), [(second_a, ALWAYS), (two, INNER)])
    near_a = along(out_near_a, middle)
    swapped_b = [across(after(x, out_two), 1) for x in got_b]
    columns_b = (whole_b, *got_b, *swapped_b)
    out_four, out_five, second_b = multiply(
        after(facts, out_near_a), masked, columns_b, (FIRST, SECOND), (coded, coded + plain)
    )
    four = along(out_four, pairs)
    five = along(out_five, inward)
    third_b, here_b = multiply(after(facts, out_five, three), masked, columns_b, (THIRD, HERE), (plain, plain))
    out_six = add(facts, [(third_b, ALWAYS), (four, INNER)])
    six = along(out_six, jump)
    out_near_b = add(after(facts, out_six, near_a), [(second_b, ALWAYS), (five, INNER)])
    near_b = along(out_near_b, middle)
    left = add(
        after(facts, out_near_b),
        [(here_a, ALWAYS), (one, OUTER), (three, ALWAYS), (near_a, INNER)],
        jnp.bfloat16,
    )
    most_b = add(after(facts, left), [(here_b, ALWAYS), (four, OUTER), (six, ALWAYS)], jnp.float32)
    return add(facts, [(most_b, ALWAYS), (near_b, INNER)], jnp.bfloat16, left)


def solution(mesh):
    body = line_of_four if mesh.shape["col"] == 4 and mesh.shape["row"] == 8 else general
    placed = (P("row", "col"), P("col", "row"), P("row", "col"))
    return jax.shard_map(
        body, mesh=mesh, in_specs=placed, out_specs=P("row", "col"), check_vma=False
    )
```

```python
import functools

import jax
import jax.numpy as jnp
from jax import lax
from jax.experimental import pallas as pl
from jax.experimental.pallas import tpu as pltpu
from jax.sharding import PartitionSpec as P

TILE = 128
CODE_ROWS = 16
LEVELS = 32767.0
STEPS_PER_OCTAVE = 64.0
BLOCK_ROWS = 512
ADD_ROWS = 512


def apply_mask(amplitudes, tile_mask):
    tiles_m, tiles_k = tile_mask.shape
    tile_rows = amplitudes.shape[0] // tiles_m
    tile_cols = amplitudes.shape[1] // tiles_k
    blocks = amplitudes.reshape(tiles_m, tile_rows, tiles_k, tile_cols)
    weights = tile_mask.astype(amplitudes.dtype)[:, None, :, None]
    return (blocks * weights).reshape(amplitudes.shape)


def general(amplitudes, integrals, tile_mask):
    masked = apply_mask(amplitudes, tile_mask)
    partial_sums = jnp.dot(
        masked,
        lax.all_gather(integrals, "row", axis=1, tiled=True),
        preferred_element_type=jnp.float32,
    )
    summed = lax.psum_scatter(partial_sums, "col", scatter_dimension=1, tiled=True)
    return summed.astype(jnp.bfloat16)


def decode(ref, step, rows, block_rows, weight):
    groups = block_rows // TILE
    start = pl.multiple_of(step * block_rows, block_rows)
    levels = ref[pl.ds(start, block_rows), :].astype(jnp.int32).astype(jnp.float32)
    codes = ref[pl.ds(rows, CODE_ROWS), :].astype(jnp.int32).astype(jnp.float32)
    pieces = []
    which = lax.broadcasted_iota(jnp.int32, codes.shape, 0)
    for g in range(groups):
        code = jnp.sum(jnp.where(which == step * groups + g, codes, 0.0), axis=0, keepdims=True)
        unit = jnp.exp2(code / STEPS_PER_OCTAVE) * (weight / LEVELS)
        pieces.append(levels[g * TILE : (g + 1) * TILE] * unit)
    return jnp.concatenate(pieces, axis=0)


def encode(acc, step, out_ref, code_ref, rows):
    block_rows = acc.shape[0]
    groups = block_rows // TILE
    pieces = []
    for g in range(groups):
        part = acc[g * TILE : (g + 1) * TILE]
        largest = jnp.max(jnp.abs(part), axis=0, keepdims=True)
        code = jnp.ceil(jnp.log(jnp.maximum(largest, 1e-30)) * (STEPS_PER_OCTAVE / 0.6931471805599453))
        scaled = jnp.round(part * (jnp.exp2(-code / STEPS_PER_OCTAVE) * LEVELS))
        pieces.append(jnp.clip(scaled, -LEVELS, LEVELS).astype(jnp.int32))
        code_ref[pl.ds(step * groups + g, 1), :] = code
    start = pl.multiple_of(step * block_rows, block_rows)
    out_ref[pl.ds(start, block_rows), :] = jnp.concatenate(pieces, axis=0).astype(jnp.int16)

    @pl.when(step == pl.num_programs(0) - 1)
    def _():
        out_ref[pl.ds(rows, CODE_ROWS), :] = code_ref[...].astype(jnp.int32).astype(jnp.int16)


def fetch(chosen, core, whole, mine, other, b, columns, sem):
    half = b.shape[0] // 2

    @pl.when(chosen == 0)
    def _():
        pltpu.make_async_copy(whole, b.at[:, columns], sem).start()

    for j in range(3):

        @pl.when(chosen == j + 1)
        def _():
            here = pl.ds(pl.multiple_of(core * half, half), half)
            there = pl.ds(pl.multiple_of((1 - core) * half, half), half)
            pltpu.make_async_copy(mine[j], b.at[here, columns], sem).start()
            pltpu.make_async_copy(other[j], b.at[there, columns], sem).start()


def multiply_kernel(slots, kinds, rows, width, facts, a_ref, *refs):
    whole, mine, other, refs = refs[0], refs[1:4], refs[4:7], refs[7:]
    count = sum(len(kind) for kind in kinds)
    outs, refs = list(refs[:count]), refs[count:]
    b, sems, codes = refs[0], refs[1], list(refs[2:])
    step = pl.program_id(0)

    @pl.when(step == 0)
    def _():
        spans = [pl.ds(j * width, width) for j in range(len(slots))]
        for j, slot in enumerate(slots):
            fetch(facts[slot] ^ facts[CHIP], facts[CORE], whole, mine, other, b, spans[j], sems.at[j])
        for j, span in enumerate(spans):
            pltpu.make_async_copy(whole, b.at[:, span], sems.at[j]).wait()

    acc = jnp.dot(a_ref[...], b[...], preferred_element_type=jnp.float32)
    for j, kind in enumerate(kinds):
        part = acc[:, j * width : (j + 1) * width]
        for form in kind:
            out_ref = outs.pop(0)
            if form == "coded":
                encode(part, step, out_ref, codes.pop(0), rows)
            else:
                out_ref[...] = part


def multiply(facts, masked, columns, slots, kinds):
    rows, depth = masked.shape
    width = columns[0].shape[1]
    packed = (rows + CODE_ROWS, width)
    forms = [form for kind in kinds for form in kind]
    coded = (pl.BlockSpec(packed, lambda i, c: (0, 0)), jax.ShapeDtypeStruct(packed, jnp.int16))
    plain = (pl.BlockSpec((BLOCK_ROWS, width), lambda i, c: (i, 0)), jax.ShapeDtypeStruct((rows, width), jnp.float32))
    outs = [coded if form == "coded" else plain for form in forms]
    return pl.pallas_call(
        functools.partial(multiply_kernel, slots, kinds, rows, width),
        out_shape=[shape for _, shape in outs],
        grid_spec=pltpu.PrefetchScalarGridSpec(
            num_scalar_prefetch=1,
            grid=(rows // BLOCK_ROWS,),
            in_specs=[pl.BlockSpec((BLOCK_ROWS, depth), lambda i, c: (i, 0))]
            + [pl.BlockSpec(memory_space=pl.ANY)] * len(columns),
            out_specs=[spec for spec, _ in outs],
            scratch_shapes=[pltpu.VMEM((depth, width * len(slots)), masked.dtype), pltpu.SemaphoreType.DMA((4,))]
            + [pltpu.VMEM((CODE_ROWS, width), jnp.float32)] * forms.count("coded"),
        ),
        compiler_params=pltpu.CompilerParams(vmem_limit_bytes=24 * 1024 * 1024),
        cost_estimate=pl.CostEstimate(flops=3000000000, bytes_accessed=9000000, transcendentals=0),
    )(facts, masked, *columns)


def add_kernel(terms, beside, rows, facts, *refs):
    step = pl.program_id(0)
    blocks, refs = refs[: len(terms)], refs[len(terms) :]
    acc = None
    for block, weight in zip(blocks, terms):
        share = facts[weight].astype(jnp.float32)
        if block.dtype == jnp.int16:
            value = decode(block, step, rows, ADD_ROWS, share)
        else:
            value = block[...] if weight == ALWAYS else block[...] * share
        acc = value if acc is None else acc + value
    out_ref = refs[beside]
    if out_ref.dtype == jnp.int16:
        encode(acc, step, out_ref, refs[beside + 1], rows)
    else:
        acc = acc.astype(out_ref.dtype)
        out_ref[...] = jnp.concatenate([refs[0][...], acc], axis=1) if beside else acc


def add(facts, terms, dtype=jnp.int16, left=None):
    rows, width = next(x.shape for x, _ in terms if x.dtype == jnp.float32)
    packed = (rows + CODE_ROWS, width)
    beside = () if left is None else (left,)
    plain = pl.BlockSpec((ADD_ROWS, width), lambda i, c: (i, 0))
    coded = pl.BlockSpec(packed, lambda i, c: (0, 0))
    if dtype == jnp.int16:
        out_spec, out_shape = coded, jax.ShapeDtypeStruct(packed, dtype)
        scratch = [pltpu.VMEM((CODE_ROWS, width), jnp.float32)]
    else:
        total = width * (1 + len(beside))
        out_spec = pl.BlockSpec((ADD_ROWS, total), lambda i, c: (i, 0))
        out_shape = jax.ShapeDtypeStruct((rows, total), dtype)
        scratch = []
    return pl.pallas_call(
        functools.partial(add_kernel, tuple(weight for _, weight in terms), len(beside), rows),
        out_shape=out_shape,
        grid_spec=pltpu.PrefetchScalarGridSpec(
            num_scalar_prefetch=1,
            grid=(rows // ADD_ROWS,),
            in_specs=[coded if x.dtype == jnp.int16 else plain for x, _ in terms] + [plain] * len(beside),
            out_specs=out_spec,
            scratch_shapes=scratch,
        ),
        compiler_params=pltpu.CompilerParams(vmem_limit_bytes=16 * 1024 * 1024),
        cost_estimate=pl.CostEstimate(flops=3000000000, bytes_accessed=9000000, transcendentals=0),
    )(facts, *[x for x, _ in terms], *beside)


PLAN = (
    (3, 2, 1, 0, 1, 1, 0),
    (0, 2, 3, 1, 1, 0, 1),
    (3, 1, 0, 2, 1, 0, 1),
    (0, 1, 2, 3, 1, 1, 0),
)
FIRST, SECOND, THIRD, HERE, ALWAYS, OUTER, INNER, CORE, CHIP = range(9)


def line_of_four(amplitudes, integrals, tile_mask):
    row = lax.axis_index("row")
    core, chip = row % 2, row // 2
    half = integrals.shape[0] // 2

    def after(value, *others):
        return lax.optimization_barrier((value, *others))[0]

    def across(block, bit):
        return lax.ppermute(block, "row", [(i, i ^ bit) for i in range(8)])

    def choose(low, high):
        return jnp.where(core == 0, low, high)

    def along(block, pairs):
        return lax.ppermute(block, "col", pairs)

    twin = across(integrals, 1)
    mine_a = choose(integrals[:half], twin[half:])
    own, pair, tile_mask, plan = lax.optimization_barrier(
        (integrals, twin, tile_mask, jnp.asarray(PLAN, jnp.int32), mine_a)
    )[:4]
    masked = apply_mask(amplitudes, tile_mask)
    planned = lax.dynamic_slice_in_dim(plan, lax.axis_index("col"), 1)[0]
    facts = jnp.concatenate([planned, jnp.stack([core, chip]).astype(jnp.int32)])
    mine_b = choose(pair[:half], own[half:])
    own, pair = lax.optimization_barrier((own, pair, mine_b))[:2]
    whole_a, whole_b = choose(own, pair), choose(pair, own)

    got_a = [across(mine_a, bit) for bit in (2, 4, 6)]
    swapped_a = [across(after(x, masked, facts, whole_a, whole_b), 1) for x in got_a]
    columns_a = (whole_a, *got_a, *swapped_a)
    got_b = [across(after(mine_b, got_a[0]), bit) for bit in (2, 4, 6)]

    pairs = [(0, 1), (1, 0), (2, 3), (3, 2)]
    inward = [(0, 1), (3, 2)]
    jump = [(0, 1), (1, 3), (2, 0), (3, 2)]
    middle = [(1, 2), (2, 1)]
    coded, plain = ("coded",), ("plain",)
    (out_one,) = multiply(facts, masked, columns_a, (FIRST,), (coded,))
    one = along(out_one, pairs)
    out_two, second_a = multiply(after(facts, out_one), masked, columns_a, (SECOND,), (coded + plain,))
    two = along(out_two, pairs)
    third_a, here_a = multiply(after(facts, out_two), masked, columns_a, (THIRD, HERE), (plain, plain))
    out_three = add(facts, [(third_a, ALWAYS), (one, INNER)])
    three = along(out_three, jump)
    swapped_b = [across(after(x, third_a), 1) for x in got_b]
    columns_b = (whole_b, *got_b, *swapped_b)
    (out_four,) = multiply(after(facts, out_three), masked, columns_b, (FIRST,), (coded,))
    four = along(out_four, pairs)
    out_five, second_b = multiply(after(facts, out_four), masked, columns_b, (SECOND,), (coded + plain,))
    five = along(out_five, inward)
    out_near_a = add(after(facts, out_five), [(second_a, ALWAYS), (two, INNER)])
    near_a = along(out_near_a, middle)
    third_b, here_b = multiply(after(facts, out_near_a, three), masked, columns_b, (THIRD, HERE), (plain, plain))
    out_six = add(facts, [(third_b, ALWAYS), (four, INNER)])
    six = along(out_six, jump)
    out_near_b = add(after(facts, out_six, near_a), [(second_b, ALWAYS), (five, INNER)])
    near_b = along(out_near_b, middle)
    left = add(
        after(facts, out_near_b),
        [(here_a, ALWAYS), (one, OUTER), (three, ALWAYS), (near_a, INNER)],
        jnp.bfloat16,
    )
    most_b = add(after(facts, left), [(here_b, ALWAYS), (four, OUTER), (six, ALWAYS)], jnp.float32)
    return add(facts, [(most_b, ALWAYS), (near_b, INNER)], jnp.bfloat16, left)


def solution(mesh):
    body = line_of_four if mesh.shape["col"] == 4 and mesh.shape["row"] == 8 else general
    placed = (P("row", "col"), P("col", "row"), P("row", "col"))
    return jax.shard_map(
        body, mesh=mesh, in_specs=placed, out_specs=P("row", "col"), check_vma=False
    )
```

```python
import functools

import jax
import jax.numpy as jnp
from jax import lax
from jax.experimental import pallas as pl
from jax.experimental.pallas import tpu as pltpu
from jax.sharding import PartitionSpec as P

TILE = 128
CODE_ROWS = 16
LEVELS = 32767.0
STEPS_PER_OCTAVE = 64.0
BLOCK_ROWS = 512
ADD_ROWS = 512


def apply_mask(amplitudes, tile_mask):
    tiles_m, tiles_k = tile_mask.shape
    tile_rows = amplitudes.shape[0] // tiles_m
    tile_cols = amplitudes.shape[1] // tiles_k
    blocks = amplitudes.reshape(tiles_m, tile_rows, tiles_k, tile_cols)
    weights = tile_mask.astype(amplitudes.dtype)[:, None, :, None]
    return (blocks * weights).reshape(amplitudes.shape)


def general(amplitudes, integrals, tile_mask):
    masked = apply_mask(amplitudes, tile_mask)
    partial_sums = jnp.dot(
        masked,
        lax.all_gather(integrals, "row", axis=1, tiled=True),
        preferred_element_type=jnp.float32,
    )
    summed = lax.psum_scatter(partial_sums, "col", scatter_dimension=1, tiled=True)
    return summed.astype(jnp.bfloat16)


def decode(ref, step, rows, block_rows, weight):
    groups = block_rows // TILE
    start = pl.multiple_of(step * block_rows, block_rows)
    levels = ref[pl.ds(start, block_rows), :].astype(jnp.int32).astype(jnp.float32)
    codes = ref[pl.ds(rows, CODE_ROWS), :].astype(jnp.int32).astype(jnp.float32)
    pieces = []
    which = lax.broadcasted_iota(jnp.int32, codes.shape, 0)
    for g in range(groups):
        code = jnp.sum(jnp.where(which == step * groups + g, codes, 0.0), axis=0, keepdims=True)
        unit = jnp.exp2(code / STEPS_PER_OCTAVE) * (weight / LEVELS)
        pieces.append(levels[g * TILE : (g + 1) * TILE] * unit)
    return jnp.concatenate(pieces, axis=0)


def encode(acc, step, out_ref, code_ref, rows):
    block_rows = acc.shape[0]
    groups = block_rows // TILE
    pieces = []
    for g in range(groups):
        part = acc[g * TILE : (g + 1) * TILE]
        largest = jnp.max(jnp.abs(part), axis=0, keepdims=True)
        code = jnp.ceil(jnp.log(jnp.maximum(largest, 1e-30)) * (STEPS_PER_OCTAVE / 0.6931471805599453))
        scaled = jnp.round(part * (jnp.exp2(-code / STEPS_PER_OCTAVE) * LEVELS))
        pieces.append(jnp.clip(scaled, -LEVELS, LEVELS).astype(jnp.int32))
        code_ref[pl.ds(step * groups + g, 1), :] = code
    start = pl.multiple_of(step * block_rows, block_rows)
    out_ref[pl.ds(start, block_rows), :] = jnp.concatenate(pieces, axis=0).astype(jnp.int16)

    @pl.when(step == pl.num_programs(0) - 1)
    def _():
        out_ref[pl.ds(rows, CODE_ROWS), :] = code_ref[...].astype(jnp.int32).astype(jnp.int16)


def fetch(chosen, core, mine, other, b, first, sem):
    width = mine[0].shape[1]
    here = pl.ds(pl.multiple_of(first + core * width, width), width)
    there = pl.ds(pl.multiple_of(first + (1 - core) * width, width), width)
    for j in range(len(mine)):

        @pl.when(chosen == j)
        def _():
            pltpu.make_async_copy(mine[j], b.at[:, here], sem).start()
            pltpu.make_async_copy(other[j], b.at[:, there], sem).start()


def multiply_kernel(slots, kinds, rows, width, sources, facts, a_ref, *refs):
    mine, other, refs = refs[:sources], refs[sources : 2 * sources], refs[2 * sources :]
    count = sum(len(kind) for kind in kinds)
    outs, refs = list(refs[:count]), refs[count:]
    b, sems, codes = refs[0], refs[1], list(refs[2:])
    step = pl.program_id(0)

    @pl.when(step == 0)
    def _():
        for j, slot in enumerate(slots):
            fetch(facts[slot] ^ facts[CHIP], facts[CORE], mine, other, b, j * width, sems.at[j])
        for j in range(len(slots)):
            span = b.at[:, pl.ds(j * width, width)]
            pltpu.make_async_copy(span, span, sems.at[j]).wait()

    acc = jnp.dot(a_ref[...], b[...], preferred_element_type=jnp.float32)
    for j, kind in enumerate(kinds):
        part = acc[:, j * width : (j + 1) * width]
        for form in kind:
            out_ref = outs.pop(0)
            if form == "coded":
                encode(part, step, out_ref, codes.pop(0), rows)
            else:
                out_ref[...] = part


def multiply(facts, masked, columns, slots, kinds):
    rows, depth = masked.shape
    sources = len(columns) // 2
    width = columns[0].shape[1] * 2
    packed = (rows + CODE_ROWS, width)
    forms = [form for kind in kinds for form in kind]
    coded = (pl.BlockSpec(packed, lambda i, c: (0, 0)), jax.ShapeDtypeStruct(packed, jnp.int16))
    plain = (pl.BlockSpec((BLOCK_ROWS, width), lambda i, c: (i, 0)), jax.ShapeDtypeStruct((rows, width), jnp.float32))
    outs = [coded if form == "coded" else plain for form in forms]
    return pl.pallas_call(
        functools.partial(multiply_kernel, slots, kinds, rows, width, sources),
        out_shape=[shape for _, shape in outs],
        grid_spec=pltpu.PrefetchScalarGridSpec(
            num_scalar_prefetch=1,
            grid=(rows // BLOCK_ROWS,),
            in_specs=[pl.BlockSpec((BLOCK_ROWS, depth), lambda i, c: (i, 0))]
            + [pl.BlockSpec(memory_space=pl.ANY)] * len(columns),
            out_specs=[spec for spec, _ in outs],
            scratch_shapes=[pltpu.VMEM((depth, width * len(slots)), masked.dtype), pltpu.SemaphoreType.DMA((len(slots),))]
            + [pltpu.VMEM((CODE_ROWS, width), jnp.float32)] * forms.count("coded"),
        ),
        compiler_params=pltpu.CompilerParams(vmem_limit_bytes=24 * 1024 * 1024),
        cost_estimate=pl.CostEstimate(flops=3000000000, bytes_accessed=9000000, transcendentals=0),
    )(facts, masked, *columns)


def add_kernel(terms, rows, facts, *refs):
    step = pl.program_id(0)
    blocks, refs = refs[: len(terms)], refs[len(terms) :]
    acc = None
    for block, weight in zip(blocks, terms):
        share = facts[weight].astype(jnp.float32)
        if block.dtype == jnp.int16:
            value = decode(block, step, rows, ADD_ROWS, share)
        else:
            value = block[...] if weight == ALWAYS else block[...] * share
        acc = value if acc is None else acc + value
    if refs[0].dtype == jnp.int16:
        encode(acc, step, refs[0], refs[1], rows)
    else:
        refs[0][...] = acc.astype(refs[0].dtype)


def add(facts, terms, dtype=jnp.int16):
    rows, width = next(x.shape for x, _ in terms if x.dtype == jnp.float32)
    packed = (rows + CODE_ROWS, width)
    plain = pl.BlockSpec((ADD_ROWS, width), lambda i, c: (i, 0))
    coded = pl.BlockSpec(packed, lambda i, c: (0, 0))
    if dtype == jnp.int16:
        out_spec, out_shape = coded, jax.ShapeDtypeStruct(packed, dtype)
        scratch = [pltpu.VMEM((CODE_ROWS, width), jnp.float32)]
    else:
        out_spec, out_shape = plain, jax.ShapeDtypeStruct((rows, width), dtype)
        scratch = []
    return pl.pallas_call(
        functools.partial(add_kernel, tuple(weight for _, weight in terms), rows),
        out_shape=out_shape,
        grid_spec=pltpu.PrefetchScalarGridSpec(
            num_scalar_prefetch=1,
            grid=(rows // ADD_ROWS,),
            in_specs=[coded if x.dtype == jnp.int16 else plain for x, _ in terms],
            out_specs=out_spec,
            scratch_shapes=scratch,
        ),
        compiler_params=pltpu.CompilerParams(vmem_limit_bytes=16 * 1024 * 1024),
        cost_estimate=pl.CostEstimate(flops=3000000000, bytes_accessed=9000000, transcendentals=0),
    )(facts, *[x for x, _ in terms])


def plan_of(chip, at):
    end = at in (0, 3)
    far, near = (3, 2) if at < 2 else (0, 1)
    late = chip == (0 if at < 2 else 3)
    passed = (near, far) if late else (far, near)
    home = 0 if at < 2 else 3
    if end:
        first, second, third, relayed = passed[0], passed[1], 3 - near, (chip, chip)
    else:
        straight = chip ^ home != 3
        first, second = (home, chip) if straight else (chip, home)
        third, relayed = chip, passed
    return (first, second, third, *relayed, at, 1, int(end), int(not end))


FIRST, SECOND, THIRD, RELAY_ONE, RELAY_TWO, HERE, ALWAYS, OUTER, INNER, CORE, CHIP = range(11)


def line_pairs(choose):
    return [(row * 4 + a, row * 4 + b) for row in range(8) for a, b in choose(row // 2)]


def line_of_four(amplitudes, integrals, tile_mask):
    row = lax.axis_index("row")
    at = lax.axis_index("col")
    core, chip = row % 2, row // 2

    def after(value, *others):
        return lax.optimization_barrier((value, *others))[0]

    def across(block, bit):
        return lax.ppermute(block, "row", [(i, i ^ bit) for i in range(8)])

    def along(block, choose):
        return lax.ppermute(block, ("row", "col"), line_pairs(choose))

    inward = [(0, 1), (3, 2)]

    def first_pairs(p):
        return inward + [(1, 0)] * (p != 3) + [(2, 3)] * (p != 0)

    def second_pairs(p):
        return inward + [(1, 0)] * (p == 3) + [(2, 3)] * (p == 0)

    def relay_one(p):
        return [(1, 2 if p == 0 else 3), (2, 1 if p == 3 else 0)]

    def relay_two(p):
        return [(1, 3 if p == 0 else 2), (2, 0 if p == 3 else 1)]

    by_x, by_y, twin = across(integrals, 2), across(integrals, 4), across(integrals, 1)
    plans = jnp.asarray([plan_of(p, z) for p in range(4) for z in range(4)], jnp.int32)
    planned = lax.dynamic_slice_in_dim(plans, chip * 4 + at, 1)[0]
    facts = jnp.concatenate([planned, jnp.stack([core, chip]).astype(jnp.int32)])
    masked = apply_mask(amplitudes, tile_mask)
    by_x, by_y = after(by_x, masked, facts), after(by_y, masked, facts)
    by_both = across(after(integrals, by_x, by_y), 6)
    straight = (integrals, by_x, by_y, twin, across(by_x, 1), across(by_y, 1))
    coded, plain = ("coded",), ("plain",)
    (out_one,) = multiply(facts, masked, straight, (FIRST,), (coded,))
    one = along(out_one, first_pairs)
    (share_one,) = multiply(after(facts, out_one), masked, straight, (RELAY_ONE,), (plain,))
    columns = (*straight[:3], by_both, *straight[3:], across(after(by_both, share_one), 1))
    out_two, share_two = multiply(
        after(facts, share_one, one), masked, columns, (SECOND, RELAY_TWO), (coded, plain)
    )
    two = along(out_two, second_pairs)
    out_relay_one = add(after(facts, out_two), [(share_one, ALWAYS), (one, ALWAYS)])
    relayed_one = along(out_relay_one, relay_one)
    out_three, own = multiply(
        after(facts, out_relay_one), masked, columns, (THIRD, HERE), (coded, plain)
    )
    out_relay_two = add(after(facts, own), [(share_two, ALWAYS), (two, ALWAYS)])
    relayed_two = along(out_relay_two, relay_two)
    three = along(after(out_three, out_relay_two), lambda p: inward)
    most = add(
        after(facts, out_relay_two),
        [(own, ALWAYS), (one, OUTER), (two, OUTER), (relayed_one, ALWAYS)],
        jnp.float32,
    )
    return add(facts, [(most, ALWAYS), (three, INNER), (relayed_two, ALWAYS)], jnp.bfloat16)


def solution(mesh):
    body = line_of_four if mesh.shape["col"] == 4 and mesh.shape["row"] == 8 else general
    placed = (P("row", "col"), P("col", "row"), P("row", "col"))
    return jax.shard_map(
        body, mesh=mesh, in_specs=placed, out_specs=P("row", "col"), check_vma=False
    )
```

```python
import functools

import jax
import jax.numpy as jnp
from jax import lax
from jax.experimental import pallas as pl
from jax.experimental.pallas import tpu as pltpu
from jax.sharding import PartitionSpec as P

TILE = 128
CODE_ROWS = 16
LEVELS = 32767.0
STEPS_PER_OCTAVE = 64.0
BLOCK_ROWS = 512
ADD_ROWS = 512


def apply_mask(amplitudes, tile_mask):
    tiles_m, tiles_k = tile_mask.shape
    tile_rows = amplitudes.shape[0] // tiles_m
    tile_cols = amplitudes.shape[1] // tiles_k
    blocks = amplitudes.reshape(tiles_m, tile_rows, tiles_k, tile_cols)
    weights = tile_mask.astype(amplitudes.dtype)[:, None, :, None]
    return (blocks * weights).reshape(amplitudes.shape)


def general(amplitudes, integrals, tile_mask):
    masked = apply_mask(amplitudes, tile_mask)
    partial_sums = jnp.dot(
        masked,
        lax.all_gather(integrals, "row", axis=1, tiled=True),
        preferred_element_type=jnp.float32,
    )
    summed = lax.psum_scatter(partial_sums, "col", scatter_dimension=1, tiled=True)
    return summed.astype(jnp.bfloat16)


def decode(ref, step, rows, block_rows, weight):
    groups = block_rows // TILE
    start = pl.multiple_of(step * block_rows, block_rows)
    levels = ref[pl.ds(start, block_rows), :].astype(jnp.int32).astype(jnp.float32)
    codes = ref[pl.ds(rows, CODE_ROWS), :].astype(jnp.int32).astype(jnp.float32)
    pieces = []
    which = lax.broadcasted_iota(jnp.int32, codes.shape, 0)
    for g in range(groups):
        code = jnp.sum(jnp.where(which == step * groups + g, codes, 0.0), axis=0, keepdims=True)
        unit = jnp.exp2(code / STEPS_PER_OCTAVE) * (weight / LEVELS)
        pieces.append(levels[g * TILE : (g + 1) * TILE] * unit)
    return jnp.concatenate(pieces, axis=0)


def encode(acc, step, out_ref, code_ref, rows):
    block_rows = acc.shape[0]
    groups = block_rows // TILE
    pieces = []
    for g in range(groups):
        part = acc[g * TILE : (g + 1) * TILE]
        largest = jnp.max(jnp.abs(part), axis=0, keepdims=True)
        code = jnp.ceil(jnp.log(jnp.maximum(largest, 1e-30)) * (STEPS_PER_OCTAVE / 0.6931471805599453))
        scaled = jnp.round(part * (jnp.exp2(-code / STEPS_PER_OCTAVE) * LEVELS))
        pieces.append(jnp.clip(scaled, -LEVELS, LEVELS).astype(jnp.int32))
        code_ref[pl.ds(step * groups + g, 1), :] = code
    start = pl.multiple_of(step * block_rows, block_rows)
    out_ref[pl.ds(start, block_rows), :] = jnp.concatenate(pieces, axis=0).astype(jnp.int16)

    @pl.when(step == pl.num_programs(0) - 1)
    def _():
        out_ref[pl.ds(rows, CODE_ROWS), :] = code_ref[...].astype(jnp.int32).astype(jnp.int16)


def fetch(chosen, core, mine, other, b, first, sem):
    width = mine[0][0].shape[1]
    here = pl.ds(pl.multiple_of(first + core * width, width), width)
    there = pl.ds(pl.multiple_of(first + (1 - core) * width, width), width)
    for j in range(len(mine)):

        @pl.when(chosen == j)
        def _():
            for parts, lanes in ((mine[j], here), (other[j], there)):
                start = 0
                for part in parts:
                    pltpu.make_async_copy(part, b.at[pl.ds(start, part.shape[0]), lanes], sem).start()
                    start += part.shape[0]


def multiply_kernel(slots, kinds, rows, width, sources, facts, a_ref, *refs):
    held, refs = list(refs[: sum(sources)]), refs[sum(sources) :]
    held = [[held.pop(0) for _ in range(parts)] for parts in sources]
    mine, other = held[: len(held) // 2], held[len(held) // 2 :]
    count = sum(len(kind) for kind in kinds)
    outs, refs = list(refs[:count]), refs[count:]
    b, sems, codes = refs[0], refs[1], list(refs[2:])
    step = pl.program_id(0)

    @pl.when(step == 0)
    def _():
        for j, slot in enumerate(slots):
            fetch(facts[slot] ^ facts[CHIP], facts[CORE], mine, other, b, j * width, sems.at[j])
        for j in range(len(slots)):
            span = b.at[:, pl.ds(j * width, width)]
            pltpu.make_async_copy(span, span, sems.at[j]).wait()

    acc = jnp.dot(a_ref[...], b[...], preferred_element_type=jnp.float32)
    for j, kind in enumerate(kinds):
        part = acc[:, j * width : (j + 1) * width]
        for form in kind:
            out_ref = outs.pop(0)
            if form != "plain":
                lanes = {"coded": slice(None), "left": slice(width // 2), "right": slice(width // 2, None)}[form]
                encode(part[:, lanes], step, out_ref, codes.pop(0), rows)
            else:
                out_ref[...] = part


def multiply(facts, masked, columns, slots, kinds):
    rows, depth = masked.shape
    columns = [x if isinstance(x, tuple) else (x,) for x in columns]
    sources = tuple(len(parts) for parts in columns)
    columns = [part for parts in columns for part in parts]
    width = columns[0].shape[1] * 2
    packed = (rows + CODE_ROWS, width)
    forms = [form for kind in kinds for form in kind]
    part = (packed[0], width // 2)
    specs = {
        "coded": (pl.BlockSpec(packed, lambda i, c: (0, 0)), jax.ShapeDtypeStruct(packed, jnp.int16)),
        "plain": (pl.BlockSpec((BLOCK_ROWS, width), lambda i, c: (i, 0)), jax.ShapeDtypeStruct((rows, width), jnp.float32)),
    }
    specs["left"] = specs["right"] = (pl.BlockSpec(part, lambda i, c: (0, 0)), jax.ShapeDtypeStruct(part, jnp.int16))
    outs = [specs[form] for form in forms]
    return pl.pallas_call(
        functools.partial(multiply_kernel, slots, kinds, rows, width, sources),
        out_shape=[shape for _, shape in outs],
        grid_spec=pltpu.PrefetchScalarGridSpec(
            num_scalar_prefetch=1,
            grid=(rows // BLOCK_ROWS,),
            in_specs=[pl.BlockSpec((BLOCK_ROWS, depth), lambda i, c: (i, 0))]
            + [pl.BlockSpec(memory_space=pl.ANY)] * len(columns),
            out_specs=[spec for spec, _ in outs],
            scratch_shapes=[pltpu.VMEM((depth, width * len(slots)), masked.dtype), pltpu.SemaphoreType.DMA((len(slots),))]
            + [pltpu.VMEM((CODE_ROWS, specs[form][1].shape[1]), jnp.float32) for form in forms if form != "plain"],
        ),
        compiler_params=pltpu.CompilerParams(vmem_limit_bytes=24 * 1024 * 1024),
        cost_estimate=pl.CostEstimate(flops=3000000000, bytes_accessed=9000000, transcendentals=0),
    )(facts, masked, *columns)


def add_kernel(terms, rows, facts, *refs):
    step = pl.program_id(0)
    count = sum(parts for _, parts in terms)
    blocks, refs = list(refs[:count]), refs[count:]
    acc = None
    for weight, parts in terms:
        share = facts[weight].astype(jnp.float32)
        block, *more = [blocks.pop(0) for _ in range(parts)]
        if block.dtype == jnp.int16:
            value = jnp.concatenate([decode(x, step, rows, ADD_ROWS, share) for x in (block, *more)], axis=1)
        else:
            value = block[...] if weight == ALWAYS else block[...] * share
        acc = value if acc is None else acc + value
    if refs[0].dtype == jnp.int16:
        encode(acc, step, refs[0], refs[1], rows)
    else:
        refs[0][...] = acc.astype(refs[0].dtype)


def add(facts, terms, dtype=jnp.int16):
    rows, width = terms[0][0].shape
    terms = [(x if isinstance(x, tuple) else (x,), weight) for x, weight in terms]
    blocks = [part for x, _ in terms for part in x]
    packed = (rows + CODE_ROWS, width)
    plain = pl.BlockSpec((ADD_ROWS, width), lambda i, c: (i, 0))
    coded = pl.BlockSpec(packed, lambda i, c: (0, 0))
    if dtype == jnp.int16:
        out_spec, out_shape = coded, jax.ShapeDtypeStruct(packed, dtype)
        scratch = [pltpu.VMEM((CODE_ROWS, width), jnp.float32)]
    else:
        out_spec, out_shape = plain, jax.ShapeDtypeStruct((rows, width), dtype)
        scratch = []
    return pl.pallas_call(
        functools.partial(add_kernel, tuple((weight, len(x)) for x, weight in terms), rows),
        out_shape=out_shape,
        grid_spec=pltpu.PrefetchScalarGridSpec(
            num_scalar_prefetch=1,
            grid=(rows // ADD_ROWS,),
            in_specs=[pl.BlockSpec(x.shape, lambda i, c: (0, 0)) if x.dtype == jnp.int16 else plain for x in blocks],
            out_specs=out_spec,
            scratch_shapes=scratch,
        ),
        compiler_params=pltpu.CompilerParams(vmem_limit_bytes=16 * 1024 * 1024),
        cost_estimate=pl.CostEstimate(flops=3000000000, bytes_accessed=9000000, transcendentals=0),
    )(facts, *blocks)


def plan_of(chip, at):
    end = at in (0, 3)
    far, near = (3, 2) if at < 2 else (0, 1)
    late = chip == (0 if at < 2 else 3)
    passed = (near, far) if late else (far, near)
    home = 0 if at < 2 else 3
    if end:
        first, second, third, relayed = passed[0], passed[1], 3 - near, (chip, chip)
    else:
        straight = chip ^ home != 3
        first, second = (home, chip) if straight else (chip, home)
        third, relayed = chip, passed
    early = chip != (3 if at < 2 else 0)
    return (first, second, third, *relayed, at, 1, int(end and early), int(end and not early), int(not end))


FIRST, SECOND, THIRD, RELAY_ONE, RELAY_TWO, HERE, ALWAYS, EARLY, LATE, INNER, CORE, CHIP = range(12)


def line_pairs(choose):
    return [(row * 4 + a, row * 4 + b) for row in range(8) for a, b in choose(row // 2)]


def line_of_four(amplitudes, integrals, tile_mask):
    row = lax.axis_index("row")
    at = lax.axis_index("col")
    core, chip = row % 2, row // 2

    def after(value, *others):
        return lax.optimization_barrier((value, *others))[0]

    def across(block, bit):
        return lax.ppermute(block, "row", [(i, i ^ bit) for i in range(8)])

    def along(block, choose):
        return lax.ppermute(block, ("row", "col"), line_pairs(choose))

    def pairs(p):
        return [(0, 1), (1, 0), (2, 3), (3, 2)]

    def relay_one(p):
        return [(1, 2 if p == 0 else 3), (2, 1 if p == 3 else 0)]

    def relay_two(p):
        return [(1, 3 if p == 0 else 2), (2, 0 if p == 3 else 1)]

    by_x, by_y, twin = across(integrals, 2), across(integrals, 4), across(integrals, 1)
    plans = jnp.asarray([plan_of(p, z) for p in range(4) for z in range(4)], jnp.int32)
    planned = lax.dynamic_slice_in_dim(plans, chip * 4 + at, 1)[0]
    facts = jnp.concatenate([planned, jnp.stack([core, chip]).astype(jnp.int32)])
    masked = apply_mask(amplitudes, tile_mask)
    by_x, by_y = after(by_x, masked, facts), after(by_y, masked, facts)
    half = integrals.shape[0] // 2
    mine = after(integrals, by_x, by_y)
    by_both = across(mine[:half], 6), across(mine[half:], 6)
    straight = (integrals, by_x, by_y, twin, across(by_x, 1), across(by_y, 1))
    coded, plain = ("coded",), ("plain",)
    out_left, out_right = multiply(facts, masked, straight, (FIRST,), (("left", "right"),))
    one = along(out_left, pairs), along(out_right, pairs)
    (share_one,) = multiply(after(facts, out_right), masked, straight, (RELAY_ONE,), (plain,))
    columns = (*straight[:3], by_both, *straight[3:], tuple(across(after(x, share_one), 1) for x in by_both))
    (out_two,) = multiply(after(facts, share_one, one[0]), masked, columns, (SECOND,), (coded,))
    two = along(out_two, pairs)
    out_relay_one = add(after(facts, out_two), [(share_one, ALWAYS), (one, ALWAYS)])
    relayed_one = along(out_relay_one, relay_one)
    out_three, share_two = multiply(
        after(facts, out_relay_one), masked, columns, (THIRD, RELAY_TWO), (coded, plain)
    )
    three = along(out_three, pairs)
    out_relay_two = add(after(facts, out_three), [(share_two, ALWAYS), (two, ALWAYS)])
    relayed_two = along(out_relay_two, relay_two)
    (own,) = multiply(after(facts, out_relay_two), masked, columns, (HERE,), (plain,))
    most = add(
        facts,
        [(own, ALWAYS), (one, EARLY), (two, LATE), (relayed_one, ALWAYS)],
        jnp.float32,
    )
    return add(facts, [(most, ALWAYS), (three, INNER), (relayed_two, ALWAYS)], jnp.bfloat16)


def solution(mesh):
    body = line_of_four if mesh.shape["col"] == 4 and mesh.shape["row"] == 8 else general
    placed = (P("row", "col"), P("col", "row"), P("row", "col"))
    return jax.shard_map(
        body, mesh=mesh, in_specs=placed, out_specs=P("row", "col"), check_vma=False
    )
```

```python
import functools

import jax
import jax.numpy as jnp
from jax import lax
from jax.experimental import pallas as pl
from jax.experimental.pallas import tpu as pltpu
from jax.sharding import PartitionSpec as P

TILE = 128
CODE_ROWS = 16
LEVELS = 32767.0
STEPS_PER_OCTAVE = 64.0
BLOCK_ROWS = 512
ADD_ROWS = 512


def apply_mask(amplitudes, tile_mask):
    tiles_m, tiles_k = tile_mask.shape
    tile_rows = amplitudes.shape[0] // tiles_m
    tile_cols = amplitudes.shape[1] // tiles_k
    blocks = amplitudes.reshape(tiles_m, tile_rows, tiles_k, tile_cols)
    weights = tile_mask.astype(amplitudes.dtype)[:, None, :, None]
    return (blocks * weights).reshape(amplitudes.shape)


def general(amplitudes, integrals, tile_mask):
    masked = apply_mask(amplitudes, tile_mask)
    partial_sums = jnp.dot(
        masked,
        lax.all_gather(integrals, "row", axis=1, tiled=True),
        preferred_element_type=jnp.float32,
    )
    summed = lax.psum_scatter(partial_sums, "col", scatter_dimension=1, tiled=True)
    return summed.astype(jnp.bfloat16)


def decode(ref, step, rows, block_rows, weight):
    groups = block_rows // TILE
    start = pl.multiple_of(step * block_rows, block_rows)
    levels = ref[pl.ds(start, block_rows), :].astype(jnp.int32).astype(jnp.float32)
    codes = ref[pl.ds(rows, CODE_ROWS), :].astype(jnp.int32).astype(jnp.float32)
    pieces = []
    which = lax.broadcasted_iota(jnp.int32, codes.shape, 0)
    for g in range(groups):
        code = jnp.sum(jnp.where(which == step * groups + g, codes, 0.0), axis=0, keepdims=True)
        unit = jnp.exp2(code / STEPS_PER_OCTAVE) * (weight / LEVELS)
        pieces.append(levels[g * TILE : (g + 1) * TILE] * unit)
    return jnp.concatenate(pieces, axis=0)


def encode(acc, step, out_ref, code_ref, rows):
    block_rows = acc.shape[0]
    groups = block_rows // TILE
    pieces = []
    for g in range(groups):
        part = acc[g * TILE : (g + 1) * TILE]
        largest = jnp.max(jnp.abs(part), axis=0, keepdims=True)
        code = jnp.ceil(jnp.log(jnp.maximum(largest, 1e-30)) * (STEPS_PER_OCTAVE / 0.6931471805599453))
        scaled = jnp.round(part * (jnp.exp2(-code / STEPS_PER_OCTAVE) * LEVELS))
        pieces.append(jnp.clip(scaled, -LEVELS, LEVELS).astype(jnp.int32))
        code_ref[pl.ds(step * groups + g, 1), :] = code
    start = pl.multiple_of(step * block_rows, block_rows)
    out_ref[pl.ds(start, block_rows), :] = jnp.concatenate(pieces, axis=0).astype(jnp.int16)

    @pl.when(step == pl.num_programs(0) - 1)
    def _():
        out_ref[pl.ds(rows, CODE_ROWS), :] = code_ref[...].astype(jnp.int32).astype(jnp.int16)


def fetch(chosen, core, mine, other, b, first, sem):
    width = mine[0][0].shape[1]
    here = pl.ds(pl.multiple_of(first + core * width, width), width)
    there = pl.ds(pl.multiple_of(first + (1 - core) * width, width), width)
    for j in range(len(mine)):

        @pl.when(chosen == j)
        def _():
            for parts, lanes in ((mine[j], here), (other[j], there)):
                start = 0
                for part in parts:
                    pltpu.make_async_copy(part, b.at[pl.ds(start, part.shape[0]), lanes], sem).start()
                    start += part.shape[0]


def multiply_kernel(slots, kinds, rows, width, sources, facts, a_ref, *refs):
    held, refs = list(refs[: sum(sources)]), refs[sum(sources) :]
    held = [[held.pop(0) for _ in range(parts)] for parts in sources]
    mine, other = held[: len(held) // 2], held[len(held) // 2 :]
    count = sum(len(kind) for kind in kinds)
    outs, refs = list(refs[:count]), refs[count:]
    b, sems, codes = refs[0], refs[1], list(refs[2:])
    step = pl.program_id(0)

    @pl.when(step == 0)
    def _():
        for j, slot in enumerate(slots):
            fetch(facts[slot] ^ facts[CHIP], facts[CORE], mine, other, b, j * width, sems.at[j])
        for j in range(len(slots)):
            span = b.at[:, pl.ds(j * width, width)]
            pltpu.make_async_copy(span, span, sems.at[j]).wait()

    acc = jnp.dot(a_ref[...], b[...], preferred_element_type=jnp.float32)
    for j, kind in enumerate(kinds):
        part = acc[:, j * width : (j + 1) * width]
        for form in kind:
            out_ref = outs.pop(0)
            if form != "plain":
                lanes = {"coded": slice(None), "left": slice(width // 2), "right": slice(width // 2, None)}[form]
                encode(part[:, lanes], step, out_ref, codes.pop(0), rows)
            else:
                out_ref[...] = part


def multiply(facts, masked, columns, slots, kinds):
    rows, depth = masked.shape
    columns = [x if isinstance(x, tuple) else (x,) for x in columns]
    sources = tuple(len(parts) for parts in columns)
    columns = [part for parts in columns for part in parts]
    width = columns[0].shape[1] * 2
    packed = (rows + CODE_ROWS, width)
    forms = [form for kind in kinds for form in kind]
    part = (packed[0], width // 2)
    specs = {
        "coded": (pl.BlockSpec(packed, lambda i, c: (0, 0)), jax.ShapeDtypeStruct(packed, jnp.int16)),
        "plain": (pl.BlockSpec((BLOCK_ROWS, width), lambda i, c: (i, 0)), jax.ShapeDtypeStruct((rows, width), jnp.float32)),
    }
    specs["left"] = specs["right"] = (pl.BlockSpec(part, lambda i, c: (0, 0)), jax.ShapeDtypeStruct(part, jnp.int16))
    outs = [specs[form] for form in forms]
    return pl.pallas_call(
        functools.partial(multiply_kernel, slots, kinds, rows, width, sources),
        out_shape=[shape for _, shape in outs],
        grid_spec=pltpu.PrefetchScalarGridSpec(
            num_scalar_prefetch=1,
            grid=(rows // BLOCK_ROWS,),
            in_specs=[pl.BlockSpec((BLOCK_ROWS, depth), lambda i, c: (i, 0))]
            + [pl.BlockSpec(memory_space=pl.ANY)] * len(columns),
            out_specs=[spec for spec, _ in outs],
            scratch_shapes=[pltpu.VMEM((depth, width * len(slots)), masked.dtype), pltpu.SemaphoreType.DMA((len(slots),))]
            + [pltpu.VMEM((CODE_ROWS, specs[form][1].shape[1]), jnp.float32) for form in forms if form != "plain"],
        ),
        compiler_params=pltpu.CompilerParams(vmem_limit_bytes=24 * 1024 * 1024),
        cost_estimate=pl.CostEstimate(flops=3000000000, bytes_accessed=9000000, transcendentals=0),
    )(facts, masked, *columns)


def add_kernel(terms, rows, facts, *refs):
    step = pl.program_id(0)
    count = sum(parts for _, parts in terms)
    blocks, refs = list(refs[:count]), refs[count:]
    acc = None
    for weight, parts in terms:
        share = facts[weight].astype(jnp.float32)
        block, *more = [blocks.pop(0) for _ in range(parts)]
        if block.dtype == jnp.int16:
            value = jnp.concatenate([decode(x, step, rows, ADD_ROWS, share) for x in (block, *more)], axis=1)
        else:
            value = block[...] if weight == ALWAYS else block[...] * share
        acc = value if acc is None else acc + value
    if refs[0].dtype == jnp.int16:
        encode(acc, step, refs[0], refs[1], rows)
    else:
        refs[0][...] = acc.astype(refs[0].dtype)


def add(facts, terms, dtype=jnp.int16):
    rows, width = terms[0][0].shape
    terms = [(x if isinstance(x, tuple) else (x,), weight) for x, weight in terms]
    blocks = [part for x, _ in terms for part in x]
    packed = (rows + CODE_ROWS, width)
    plain = pl.BlockSpec((ADD_ROWS, width), lambda i, c: (i, 0))
    coded = pl.BlockSpec(packed, lambda i, c: (0, 0))
    if dtype == jnp.int16:
        out_spec, out_shape = coded, jax.ShapeDtypeStruct(packed, dtype)
        scratch = [pltpu.VMEM((CODE_ROWS, width), jnp.float32)]
    else:
        out_spec, out_shape = plain, jax.ShapeDtypeStruct((rows, width), dtype)
        scratch = []
    return pl.pallas_call(
        functools.partial(add_kernel, tuple((weight, len(x)) for x, weight in terms), rows),
        out_shape=out_shape,
        grid_spec=pltpu.PrefetchScalarGridSpec(
            num_scalar_prefetch=1,
            grid=(rows // ADD_ROWS,),
            in_specs=[pl.BlockSpec(x.shape, lambda i, c: (0, 0)) if x.dtype == jnp.int16 else plain for x in blocks],
            out_specs=out_spec,
            scratch_shapes=scratch,
        ),
        compiler_params=pltpu.CompilerParams(vmem_limit_bytes=16 * 1024 * 1024),
        cost_estimate=pl.CostEstimate(flops=3000000000, bytes_accessed=9000000, transcendentals=0),
    )(facts, *blocks)


def plan_of(chip, at):
    end = at in (0, 3)
    far, near = (3, 2) if at < 2 else (0, 1)
    late = chip == (0 if at < 2 else 3)
    passed = (near, far) if late else (far, near)
    home = 0 if at < 2 else 3
    if end:
        first, second, third, relayed = passed[0], passed[1], 3 - near, (chip, chip)
    else:
        straight = chip ^ home != 3
        first, second = (home, chip) if straight else (chip, home)
        third, relayed = chip, passed
    early = chip != (3 if at < 2 else 0)
    return (first, second, third, *relayed, at, 1, int(end and early), int(end and not early), int(not end))


FIRST, SECOND, THIRD, RELAY_ONE, RELAY_TWO, HERE, ALWAYS, EARLY, LATE, INNER, CORE, CHIP = range(12)


def line_pairs(choose):
    return [(row * 4 + a, row * 4 + b) for row in range(8) for a, b in choose(row // 2)]


def line_of_four(amplitudes, integrals, tile_mask):
    row = lax.axis_index("row")
    at = lax.axis_index("col")
    core, chip = row % 2, row // 2

    def after(value, *others):
        return lax.optimization_barrier((value, *others))[0]

    def across(block, bit):
        return lax.ppermute(block, "row", [(i, i ^ bit) for i in range(8)])

    def along(block, choose):
        return lax.ppermute(block, ("row", "col"), line_pairs(choose))

    def pairs(p):
        return [(0, 1), (1, 0), (2, 3), (3, 2)]

    inward = [(0, 1), (3, 2)]

    def second_pairs(p):
        return inward + [(1, 0)] * (p == 3) + [(2, 3)] * (p == 0)

    def relay_one(p):
        return [(1, 2 if p == 0 else 3), (2, 1 if p == 3 else 0)]

    def relay_two(p):
        return [(1, 3 if p == 0 else 2), (2, 0 if p == 3 else 1)]

    by_x, by_y, twin = across(integrals, 2), across(integrals, 4), across(integrals, 1)
    plans = jnp.asarray([plan_of(p, z) for p in range(4) for z in range(4)], jnp.int32)
    planned = lax.dynamic_slice_in_dim(plans, chip * 4 + at, 1)[0]
    facts = jnp.concatenate([planned, jnp.stack([core, chip]).astype(jnp.int32)])
    masked = apply_mask(amplitudes, tile_mask)
    by_x, by_y = after(by_x, masked, facts), after(by_y, masked, facts)
    half = integrals.shape[0] // 2
    by_both = across(by_y[:half], 2), across(by_x[half:], 4)
    straight = (integrals, by_x, by_y, twin, across(by_x, 1), across(by_y, 1))
    coded, plain = ("coded",), ("plain",)
    out_left, out_right = multiply(facts, masked, straight, (FIRST,), (("left", "right"),))
    one = along(out_left, pairs), along(out_right, pairs)
    (share_one,) = multiply(after(facts, out_right), masked, straight, (RELAY_ONE,), (plain,))
    columns = (*straight[:3], by_both, *straight[3:], tuple(across(after(x, share_one), 1) for x in by_both))
    (out_two,) = multiply(after(facts, share_one, one[0]), masked, columns, (SECOND,), (coded,))
    two = along(out_two, second_pairs)
    out_relay_one = add(after(facts, out_two), [(share_one, ALWAYS), (one, ALWAYS)])
    relayed_one = along(out_relay_one, relay_one)
    out_three, share_two = multiply(
        after(facts, out_relay_one), masked, columns, (THIRD, RELAY_TWO), (coded, plain)
    )
    three = along(out_three, lambda p: inward)
    out_relay_two = add(after(facts, out_three), [(share_two, ALWAYS), (two, ALWAYS)])
    relayed_two = along(out_relay_two, relay_two)
    (own,) = multiply(after(facts, out_relay_two), masked, columns, (HERE,), (plain,))
    most = add(
        facts,
        [(own, ALWAYS), (one, EARLY), (two, LATE), (relayed_one, ALWAYS)],
        jnp.float32,
    )
    return add(facts, [(most, ALWAYS), (three, INNER), (relayed_two, ALWAYS)], jnp.bfloat16)


def solution(mesh):
    body = line_of_four if mesh.shape["col"] == 4 and mesh.shape["row"] == 8 else general
    placed = (P("row", "col"), P("col", "row"), P("row", "col"))
    return jax.shard_map(
        body, mesh=mesh, in_specs=placed, out_specs=P("row", "col"), check_vma=False
    )
```

```python
import functools

import jax
import jax.numpy as jnp
from jax import lax
from jax.experimental import pallas as pl
from jax.experimental.pallas import tpu as pltpu
from jax.sharding import PartitionSpec as P

TILE = 128
CODE_ROWS = 16
LEVELS = 32767.0
STEPS_PER_OCTAVE = 64.0
BLOCK_ROWS = 512
ADD_ROWS = 512


def apply_mask(amplitudes, tile_mask):
    tiles_m, tiles_k = tile_mask.shape
    tile_rows = amplitudes.shape[0] // tiles_m
    tile_cols = amplitudes.shape[1] // tiles_k
    blocks = amplitudes.reshape(tiles_m, tile_rows, tiles_k, tile_cols)
    weights = tile_mask.astype(amplitudes.dtype)[:, None, :, None]
    return (blocks * weights).reshape(amplitudes.shape)


def general(amplitudes, integrals, tile_mask):
    masked = apply_mask(amplitudes, tile_mask)
    partial_sums = jnp.dot(
        masked,
        lax.all_gather(integrals, "row", axis=1, tiled=True),
        preferred_element_type=jnp.float32,
    )
    summed = lax.psum_scatter(partial_sums, "col", scatter_dimension=1, tiled=True)
    return summed.astype(jnp.bfloat16)


def decode(ref, step, rows, block_rows, weight):
    groups = block_rows // TILE
    start = pl.multiple_of(step * block_rows, block_rows)
    levels = ref[pl.ds(start, block_rows), :].astype(jnp.int32).astype(jnp.float32)
    codes = ref[pl.ds(rows, CODE_ROWS), :].astype(jnp.int32).astype(jnp.float32)
    pieces = []
    which = lax.broadcasted_iota(jnp.int32, codes.shape, 0)
    for g in range(groups):
        code = jnp.sum(jnp.where(which == step * groups + g, codes, 0.0), axis=0, keepdims=True)
        unit = jnp.exp2(code / STEPS_PER_OCTAVE) * (weight / LEVELS)
        pieces.append(levels[g * TILE : (g + 1) * TILE] * unit)
    return jnp.concatenate(pieces, axis=0)


def encode(acc, step, out_ref, code_ref, rows):
    block_rows = acc.shape[0]
    groups = block_rows // TILE
    pieces = []
    for g in range(groups):
        part = acc[g * TILE : (g + 1) * TILE]
        largest = jnp.max(jnp.abs(part), axis=0, keepdims=True)
        code = jnp.ceil(jnp.log(jnp.maximum(largest, 1e-30)) * (STEPS_PER_OCTAVE / 0.6931471805599453))
        scaled = jnp.round(part * (jnp.exp2(-code / STEPS_PER_OCTAVE) * LEVELS))
        pieces.append(jnp.clip(scaled, -LEVELS, LEVELS).astype(jnp.int32))
        code_ref[pl.ds(step * groups + g, 1), :] = code
    start = pl.multiple_of(step * block_rows, block_rows)
    out_ref[pl.ds(start, block_rows), :] = jnp.concatenate(pieces, axis=0).astype(jnp.int16)

    @pl.when(step == pl.num_programs(0) - 1)
    def _():
        out_ref[pl.ds(rows, CODE_ROWS), :] = code_ref[...].astype(jnp.int32).astype(jnp.int16)


def fetch(chosen, core, mine, other, b, first, sem):
    width = mine[0][0].shape[1]
    here = pl.ds(pl.multiple_of(first + core * width, width), width)
    there = pl.ds(pl.multiple_of(first + (1 - core) * width, width), width)
    for j in range(len(mine)):

        @pl.when(chosen == j)
        def _():
            for parts, lanes in ((mine[j], here), (other[j], there)):
                start = 0
                for part in parts:
                    pltpu.make_async_copy(part, b.at[pl.ds(start, part.shape[0]), lanes], sem).start()
                    start += part.shape[0]


def multiply_kernel(slots, kinds, rows, width, sources, facts, a_ref, *refs):
    held, refs = list(refs[: sum(sources)]), refs[sum(sources) :]
    held = [[held.pop(0) for _ in range(parts)] for parts in sources]
    mine, other = held[: len(held) // 2], held[len(held) // 2 :]
    count = sum(len(kind) for kind in kinds)
    outs, refs = list(refs[:count]), refs[count:]
    b, sems, codes = refs[0], refs[1], list(refs[2:])
    step = pl.program_id(0)

    @pl.when(step == 0)
    def _():
        for j, slot in enumerate(slots):
            fetch(facts[slot] ^ facts[CHIP], facts[CORE], mine, other, b, j * width, sems.at[j])
        for j in range(len(slots)):
            span = b.at[:, pl.ds(j * width, width)]
            pltpu.make_async_copy(span, span, sems.at[j]).wait()

    acc = jnp.dot(a_ref[...], b[...], preferred_element_type=jnp.float32)
    for j, kind in enumerate(kinds):
        part = acc[:, j * width : (j + 1) * width]
        for form in kind:
            out_ref = outs.pop(0)
            if form != "plain":
                lanes = {"coded": slice(None), "left": slice(width // 2), "right": slice(width // 2, None)}[form]
                encode(part[:, lanes], step, out_ref, codes.pop(0), rows)
            else:
                out_ref[...] = part


def multiply(facts, masked, columns, slots, kinds):
    rows, depth = masked.shape
    columns = [x if isinstance(x, tuple) else (x,) for x in columns]
    sources = tuple(len(parts) for parts in columns)
    columns = [part for parts in columns for part in parts]
    width = columns[0].shape[1] * 2
    packed = (rows + CODE_ROWS, width)
    forms = [form for kind in kinds for form in kind]
    part = (packed[0], width // 2)
    specs = {
        "coded": (pl.BlockSpec(packed, lambda i, c: (0, 0)), jax.ShapeDtypeStruct(packed, jnp.int16)),
        "plain": (pl.BlockSpec((BLOCK_ROWS, width), lambda i, c: (i, 0)), jax.ShapeDtypeStruct((rows, width), jnp.float32)),
    }
    specs["left"] = specs["right"] = (pl.BlockSpec(part, lambda i, c: (0, 0)), jax.ShapeDtypeStruct(part, jnp.int16))
    outs = [specs[form] for form in forms]
    return pl.pallas_call(
        functools.partial(multiply_kernel, slots, kinds, rows, width, sources),
        out_shape=[shape for _, shape in outs],
        grid_spec=pltpu.PrefetchScalarGridSpec(
            num_scalar_prefetch=1,
            grid=(rows // BLOCK_ROWS,),
            in_specs=[pl.BlockSpec((BLOCK_ROWS, depth), lambda i, c: (i, 0))]
            + [pl.BlockSpec(memory_space=pl.ANY)] * len(columns),
            out_specs=[spec for spec, _ in outs],
            scratch_shapes=[pltpu.VMEM((depth, width * len(slots)), masked.dtype), pltpu.SemaphoreType.DMA((len(slots),))]
            + [pltpu.VMEM((CODE_ROWS, specs[form][1].shape[1]), jnp.float32) for form in forms if form != "plain"],
        ),
        compiler_params=pltpu.CompilerParams(vmem_limit_bytes=24 * 1024 * 1024),
        cost_estimate=pl.CostEstimate(flops=3000000000, bytes_accessed=9000000, transcendentals=0),
    )(facts, masked, *columns)


def add_kernel(terms, rows, facts, *refs):
    step = pl.program_id(0)
    count = sum(parts for _, parts in terms)
    blocks, refs = list(refs[:count]), refs[count:]
    acc = None
    for weight, parts in terms:
        share = facts[weight].astype(jnp.float32)
        block, *more = [blocks.pop(0) for _ in range(parts)]
        if block.dtype == jnp.int16:
            value = jnp.concatenate([decode(x, step, rows, ADD_ROWS, share) for x in (block, *more)], axis=1)
        else:
            value = block[...] if weight == ALWAYS else block[...] * share
        acc = value if acc is None else acc + value
    if refs[0].dtype == jnp.int16:
        encode(acc, step, refs[0], refs[1], rows)
    else:
        refs[0][...] = acc.astype(refs[0].dtype)


def add(facts, terms, dtype=jnp.int16, side=None):
    rows, width = terms[0][0].shape
    if side is not None:
        width //= 2
    terms = [(x if isinstance(x, tuple) else (x,), weight) for x, weight in terms]
    blocks = [part for x, _ in terms for part in x]
    packed = (rows + CODE_ROWS, width)
    plain = pl.BlockSpec((ADD_ROWS, width), lambda i, c: (i, side or 0))
    coded = pl.BlockSpec(packed, lambda i, c: (0, 0))
    if dtype == jnp.int16:
        out_spec, out_shape = coded, jax.ShapeDtypeStruct(packed, dtype)
        scratch = [pltpu.VMEM((CODE_ROWS, width), jnp.float32)]
    else:
        out_spec, out_shape = plain, jax.ShapeDtypeStruct((rows, width), dtype)
        scratch = []
    return pl.pallas_call(
        functools.partial(add_kernel, tuple((weight, len(x)) for x, weight in terms), rows),
        out_shape=out_shape,
        grid_spec=pltpu.PrefetchScalarGridSpec(
            num_scalar_prefetch=1,
            grid=(rows // ADD_ROWS,),
            in_specs=[pl.BlockSpec(x.shape, lambda i, c: (0, 0)) if x.dtype == jnp.int16 else plain for x in blocks],
            out_specs=out_spec,
            scratch_shapes=scratch,
        ),
        compiler_params=pltpu.CompilerParams(vmem_limit_bytes=16 * 1024 * 1024),
        cost_estimate=pl.CostEstimate(flops=3000000000, bytes_accessed=9000000, transcendentals=0),
    )(facts, *blocks)


def plan_of(chip, at):
    end = at in (0, 3)
    far, near = (3, 2) if at < 2 else (0, 1)
    late = chip == (0 if at < 2 else 3)
    passed = (near, far) if late else (far, near)
    home = 0 if at < 2 else 3
    if end:
        first, second, third, relayed = passed[0], passed[1], 3 - near, (chip, chip)
    else:
        straight = chip ^ home != 3
        first, second = (home, chip) if straight else (chip, home)
        third, relayed = chip, passed
    early = chip != (3 if at < 2 else 0)
    return (first, second, third, *relayed, at, 1, int(end and early), int(end and not early), int(not end))


FIRST, SECOND, THIRD, RELAY_ONE, RELAY_TWO, HERE, ALWAYS, EARLY, LATE, INNER, CORE, CHIP = range(12)


def line_pairs(choose):
    return [(row * 4 + a, row * 4 + b) for row in range(8) for a, b in choose(row // 2)]


def line_of_four(amplitudes, integrals, tile_mask):
    row = lax.axis_index("row")
    at = lax.axis_index("col")
    core, chip = row % 2, row // 2

    def after(value, *others):
        return lax.optimization_barrier((value, *others))[0]

    def across(block, bit):
        return lax.ppermute(block, "row", [(i, i ^ bit) for i in range(8)])

    def along(block, choose):
        return lax.ppermute(block, ("row", "col"), line_pairs(choose))

    def pairs(p):
        return [(0, 1), (1, 0), (2, 3), (3, 2)]

    inward = [(0, 1), (3, 2)]

    def second_pairs(p):
        return inward + [(1, 0)] * (p == 3) + [(2, 3)] * (p == 0)

    def relay_one(p):
        return [(1, 2 if p == 0 else 3), (2, 1 if p == 3 else 0)]

    def relay_two(p):
        return [(1, 3 if p == 0 else 2), (2, 0 if p == 3 else 1)]

    by_x, by_y, twin = across(integrals, 2), across(integrals, 4), across(integrals, 1)
    plans = jnp.asarray([plan_of(p, z) for p in range(4) for z in range(4)], jnp.int32)
    planned = lax.dynamic_slice_in_dim(plans, chip * 4 + at, 1)[0]
    facts = jnp.concatenate([planned, jnp.stack([core, chip]).astype(jnp.int32)])
    masked = apply_mask(amplitudes, tile_mask)
    by_x, by_y = after(by_x, masked, facts), after(by_y, masked, facts)
    half = integrals.shape[0] // 2
    by_both = across(by_y[:half], 2), across(by_x[half:], 4)
    straight = (integrals, by_x, by_y, twin, across(by_x, 1), across(by_y, 1))
    coded, plain = ("coded",), ("plain",)
    out_left, out_right = multiply(facts, masked, straight, (FIRST,), (("left", "right"),))
    one = along(out_left, pairs), along(out_right, pairs)
    (share_one,) = multiply(after(facts, out_right), masked, straight, (RELAY_ONE,), (plain,))
    columns = (*straight[:3], by_both, *straight[3:], tuple(across(after(x, share_one), 1) for x in by_both))
    *out_two, own = multiply(
        after(facts, share_one, one[0]), masked, columns, (SECOND, HERE), (("left", "right"), plain)
    )
    two = along(out_two[0], second_pairs), along(out_two[1], second_pairs)
    out_relay_one = add(after(facts, *out_two), [(share_one, ALWAYS), (one, ALWAYS)])
    relayed_one = along(out_relay_one, relay_one)
    out_three, share_two = multiply(
        after(facts, out_relay_one), masked, columns, (THIRD, RELAY_TWO), (coded, plain)
    )
    relay_left = add(after(facts, out_three), [(share_two, ALWAYS), (two[0], ALWAYS)], side=0)
    three = along(after(out_three, relay_left), lambda p: inward)
    relay_right = add(after(facts, relay_left), [(share_two, ALWAYS), (two[1], ALWAYS)], side=1)
    relayed_two = along(relay_left, relay_two), along(relay_right, relay_two)
    most = add(
        after(facts, relay_right),
        [(own, ALWAYS), (one, EARLY), (two, LATE), (relayed_one, ALWAYS)],
        jnp.float32,
    )
    return add(facts, [(most, ALWAYS), (three, INNER), (relayed_two, ALWAYS)], jnp.bfloat16)


def solution(mesh):
    body = line_of_four if mesh.shape["col"] == 4 and mesh.shape["row"] == 8 else general
    placed = (P("row", "col"), P("col", "row"), P("row", "col"))
    return jax.shard_map(
        body, mesh=mesh, in_specs=placed, out_specs=P("row", "col"), check_vma=False
    )
```

```python
import functools

import jax
import jax.numpy as jnp
from jax import lax
from jax.experimental import pallas as pl
from jax.experimental.pallas import tpu as pltpu
from jax.sharding import PartitionSpec as P

TILE = 128
CODE_ROWS = 16
LEVELS = 32767.0
STEPS_PER_OCTAVE = 64.0
BLOCK_ROWS = 512
ADD_ROWS = 512


def apply_mask(amplitudes, tile_mask):
    tiles_m, tiles_k = tile_mask.shape
    tile_rows = amplitudes.shape[0] // tiles_m
    tile_cols = amplitudes.shape[1] // tiles_k
    blocks = amplitudes.reshape(tiles_m, tile_rows, tiles_k, tile_cols)
    weights = tile_mask.astype(amplitudes.dtype)[:, None, :, None]
    return (blocks * weights).reshape(amplitudes.shape)


def general(amplitudes, integrals, tile_mask):
    masked = apply_mask(amplitudes, tile_mask)
    partial_sums = jnp.dot(
        masked,
        lax.all_gather(integrals, "row", axis=1, tiled=True),
        preferred_element_type=jnp.float32,
    )
    summed = lax.psum_scatter(partial_sums, "col", scatter_dimension=1, tiled=True)
    return summed.astype(jnp.bfloat16)


def decode(ref, step, rows, block_rows, weight):
    groups = block_rows // TILE
    start = pl.multiple_of(step * block_rows, block_rows)
    levels = ref[pl.ds(start, block_rows), :].astype(jnp.int32).astype(jnp.float32)
    codes = ref[pl.ds(rows, CODE_ROWS), :].astype(jnp.int32).astype(jnp.float32)
    pieces = []
    which = lax.broadcasted_iota(jnp.int32, codes.shape, 0)
    for g in range(groups):
        code = jnp.sum(jnp.where(which == step * groups + g, codes, 0.0), axis=0, keepdims=True)
        unit = jnp.exp2(code / STEPS_PER_OCTAVE) * (weight / LEVELS)
        pieces.append(levels[g * TILE : (g + 1) * TILE] * unit)
    return jnp.concatenate(pieces, axis=0)


def encode(acc, step, out_ref, code_ref, rows):
    block_rows = acc.shape[0]
    groups = block_rows // TILE
    pieces = []
    for g in range(groups):
        part = acc[g * TILE : (g + 1) * TILE]
        largest = jnp.max(jnp.abs(part), axis=0, keepdims=True)
        code = jnp.ceil(jnp.log(jnp.maximum(largest, 1e-30)) * (STEPS_PER_OCTAVE / 0.6931471805599453))
        scaled = jnp.round(part * (jnp.exp2(-code / STEPS_PER_OCTAVE) * LEVELS))
        pieces.append(jnp.clip(scaled, -LEVELS, LEVELS).astype(jnp.int32))
        code_ref[pl.ds(step * groups + g, 1), :] = code
    start = pl.multiple_of(step * block_rows, block_rows)
    out_ref[pl.ds(start, block_rows), :] = jnp.concatenate(pieces, axis=0).astype(jnp.int16)

    @pl.when(step == pl.num_programs(0) - 1)
    def _():
        out_ref[pl.ds(rows, CODE_ROWS), :] = code_ref[...].astype(jnp.int32).astype(jnp.int16)


def fetch(chosen, core, mine, other, b, first, sem):
    width = mine[0][0].shape[1]
    here = pl.ds(pl.multiple_of(first + core * width, width), width)
    there = pl.ds(pl.multiple_of(first + (1 - core) * width, width), width)
    for j in range(len(mine)):

        @pl.when(chosen == j)
        def _():
            for parts, lanes in ((mine[j], here), (other[j], there)):
                start = 0
                for part in parts:
                    pltpu.make_async_copy(part, b.at[pl.ds(start, part.shape[0]), lanes], sem).start()
                    start += part.shape[0]


def multiply_kernel(slots, kinds, rows, width, sources, facts, a_ref, *refs):
    held, refs = list(refs[: sum(sources)]), refs[sum(sources) :]
    held = [[held.pop(0) for _ in range(parts)] for parts in sources]
    mine, other = held[: len(held) // 2], held[len(held) // 2 :]
    count = sum(len(kind) for kind in kinds)
    outs, refs = list(refs[:count]), refs[count:]
    b, sems, codes = refs[0], refs[1], list(refs[2:])
    step = pl.program_id(0)

    @pl.when(step == 0)
    def _():
        for j, slot in enumerate(slots):
            fetch(facts[slot] ^ facts[CHIP], facts[CORE], mine, other, b, j * width, sems.at[j])
        for j in range(len(slots)):
            span = b.at[:, pl.ds(j * width, width)]
            pltpu.make_async_copy(span, span, sems.at[j]).wait()

    acc = jnp.dot(a_ref[...], b[...], preferred_element_type=jnp.float32)
    for j, kind in enumerate(kinds):
        part = acc[:, j * width : (j + 1) * width]
        for form in kind:
            out_ref = outs.pop(0)
            if form != "plain":
                lanes = {"coded": slice(None), "left": slice(width // 2), "right": slice(width // 2, None)}[form]
                encode(part[:, lanes], step, out_ref, codes.pop(0), rows)
            else:
                out_ref[...] = part


def multiply(facts, masked, columns, slots, kinds):
    rows, depth = masked.shape
    columns = [x if isinstance(x, tuple) else (x,) for x in columns]
    sources = tuple(len(parts) for parts in columns)
    columns = [part for parts in columns for part in parts]
    width = columns[0].shape[1] * 2
    packed = (rows + CODE_ROWS, width)
    forms = [form for kind in kinds for form in kind]
    part = (packed[0], width // 2)
    specs = {
        "coded": (pl.BlockSpec(packed, lambda i, c: (0, 0)), jax.ShapeDtypeStruct(packed, jnp.int16)),
        "plain": (pl.BlockSpec((BLOCK_ROWS, width), lambda i, c: (i, 0)), jax.ShapeDtypeStruct((rows, width), jnp.float32)),
    }
    specs["left"] = specs["right"] = (pl.BlockSpec(part, lambda i, c: (0, 0)), jax.ShapeDtypeStruct(part, jnp.int16))
    outs = [specs[form] for form in forms]
    return pl.pallas_call(
        functools.partial(multiply_kernel, slots, kinds, rows, width, sources),
        out_shape=[shape for _, shape in outs],
        grid_spec=pltpu.PrefetchScalarGridSpec(
            num_scalar_prefetch=1,
            grid=(rows // BLOCK_ROWS,),
            in_specs=[pl.BlockSpec((BLOCK_ROWS, depth), lambda i, c: (i, 0))]
            + [pl.BlockSpec(memory_space=pl.ANY)] * len(columns),
            out_specs=[spec for spec, _ in outs],
            scratch_shapes=[pltpu.VMEM((depth, width * len(slots)), masked.dtype), pltpu.SemaphoreType.DMA((len(slots),))]
            + [pltpu.VMEM((CODE_ROWS, specs[form][1].shape[1]), jnp.float32) for form in forms if form != "plain"],
        ),
        compiler_params=pltpu.CompilerParams(vmem_limit_bytes=24 * 1024 * 1024),
        cost_estimate=pl.CostEstimate(flops=3000000000, bytes_accessed=9000000, transcendentals=0),
    )(facts, masked, *columns)


def add_kernel(terms, rows, facts, *refs):
    step = pl.program_id(0)
    count = sum(parts for _, parts in terms)
    blocks, refs = list(refs[:count]), refs[count:]
    acc = None
    for weight, parts in terms:
        share = facts[weight].astype(jnp.float32)
        block, *more = [blocks.pop(0) for _ in range(parts)]
        if block.dtype == jnp.int16:
            value = jnp.concatenate([decode(x, step, rows, ADD_ROWS, share) for x in (block, *more)], axis=1)
        else:
            value = block[...] if weight == ALWAYS else block[...] * share
        acc = value if acc is None else acc + value
    if refs[0].dtype == jnp.int16:
        encode(acc, step, refs[0], refs[1], rows)
    else:
        refs[0][...] = acc.astype(refs[0].dtype)


def add(facts, terms, dtype=jnp.int16):
    rows, width = terms[0][0].shape
    terms = [(x if isinstance(x, tuple) else (x,), weight) for x, weight in terms]
    blocks = [part for x, _ in terms for part in x]
    packed = (rows + CODE_ROWS, width)
    plain = pl.BlockSpec((ADD_ROWS, width), lambda i, c: (i, 0))
    coded = pl.BlockSpec(packed, lambda i, c: (0, 0))
    if dtype == jnp.int16:
        out_spec, out_shape = coded, jax.ShapeDtypeStruct(packed, dtype)
        scratch = [pltpu.VMEM((CODE_ROWS, width), jnp.float32)]
    else:
        out_spec, out_shape = plain, jax.ShapeDtypeStruct((rows, width), dtype)
        scratch = []
    return pl.pallas_call(
        functools.partial(add_kernel, tuple((weight, len(x)) for x, weight in terms), rows),
        out_shape=out_shape,
        grid_spec=pltpu.PrefetchScalarGridSpec(
            num_scalar_prefetch=1,
            grid=(rows // ADD_ROWS,),
            in_specs=[pl.BlockSpec(x.shape, lambda i, c: (0, 0)) if x.dtype == jnp.int16 else plain for x in blocks],
            out_specs=out_spec,
            scratch_shapes=scratch,
        ),
        compiler_params=pltpu.CompilerParams(vmem_limit_bytes=16 * 1024 * 1024),
        cost_estimate=pl.CostEstimate(flops=3000000000, bytes_accessed=9000000, transcendentals=0),
    )(facts, *blocks)


def plan_of(chip, at):
    end = at in (0, 3)
    far, near = (3, 2) if at < 2 else (0, 1)
    late = chip == (0 if at < 2 else 3)
    passed = (near, far) if late else (far, near)
    home = 0 if at < 2 else 3
    early = chip != (3 if at < 2 else 0)
    if end:
        first, second, third, relayed = passed[0], passed[1], 3 - near, chip
    else:
        first, second = home if early else chip, passed[1]
        third, relayed = chip if early else home, passed[0]
    return (first, second, third, relayed, at, 1, int(end and early), int(not (end and early)))


FIRST, SECOND, THIRD, RELAY, HERE, ALWAYS, EARLY, OTHERS, CORE, CHIP = range(10)


def line_pairs(choose):
    return [(row * 4 + a, row * 4 + b) for row in range(8) for a, b in choose(row // 2)]


def line_of_four(amplitudes, integrals, tile_mask):
    row = lax.axis_index("row")
    at = lax.axis_index("col")
    core, chip = row % 2, row // 2

    def after(value, *others):
        return lax.optimization_barrier((value, *others))[0]

    def across(block, bit):
        return lax.ppermute(block, "row", [(i, i ^ bit) for i in range(8)])

    def along(block, choose):
        return lax.ppermute(block, ("row", "col"), line_pairs(choose))

    def pairs(p):
        return [(0, 1), (1, 0), (2, 3), (3, 2)]

    inward = [(0, 1), (3, 2)]

    def straight_pairs(p):
        return [(0, 3 if p == 0 else 2), (3, 0 if p == 3 else 1)]

    def share_pairs(p):
        return [(1, 3 if p == 0 else 2), (2, 0 if p == 3 else 1)]

    def relay_pairs(p):
        return [(1, 2 if p == 0 else 3), (2, 1 if p == 3 else 0)]

    def third_pairs(p):
        return inward + [(1, 0)] * (p == 3) + [(2, 3)] * (p == 0)

    by_x, by_y, twin = across(integrals, 2), across(integrals, 4), across(integrals, 1)
    plans = jnp.asarray([plan_of(p, z) for p in range(4) for z in range(4)], jnp.int32)
    planned = lax.dynamic_slice_in_dim(plans, chip * 4 + at, 1)[0]
    facts = jnp.concatenate([planned, jnp.stack([core, chip]).astype(jnp.int32)])
    masked = apply_mask(amplitudes, tile_mask)
    by_x, by_y = after(by_x, masked, facts), after(by_y, masked, facts)
    half = integrals.shape[0] // 2
    by_both = across(by_y[:half], 2), across(by_x[half:], 4)
    straight = (integrals, by_x, by_y, twin, across(by_x, 1), across(by_y, 1))
    coded, plain = ("coded",), ("plain",)
    out_left, out_right = multiply(facts, masked, straight, (FIRST,), (("left", "right"),))
    one = along(out_left, pairs), along(out_right, pairs)
    (share_one,) = multiply(after(facts, out_right), masked, straight, (RELAY,), (plain,))
    columns = (*straight[:3], by_both, *straight[3:], tuple(across(after(x, share_one), 1) for x in by_both))
    (out_two,) = multiply(after(facts, share_one, one[0]), masked, columns, (SECOND,), (coded,))
    two = along(out_two, straight_pairs)
    shared = along(out_two, share_pairs)
    out_relay = add(after(facts, out_two), [(share_one, ALWAYS), (one, ALWAYS)])
    relayed = along(out_relay, relay_pairs)
    (out_three,) = multiply(after(facts, out_relay), masked, columns, (THIRD,), (coded,))
    three = along(out_three, third_pairs)
    (own,) = multiply(after(facts, out_three, two, shared), masked, columns, (HERE,), (plain,))
    most = add(
        facts,
        [(own, ALWAYS), (one, EARLY), (two, ALWAYS), (shared, ALWAYS), (relayed, ALWAYS)],
        jnp.float32,
    )
    return add(facts, [(most, ALWAYS), (three, OTHERS)], jnp.bfloat16)


def solution(mesh):
    body = line_of_four if mesh.shape["col"] == 4 and mesh.shape["row"] == 8 else general
    placed = (P("row", "col"), P("col", "row"), P("row", "col"))
    return jax.shard_map(
        body, mesh=mesh, in_specs=placed, out_specs=P("row", "col"), check_vma=False
    )
```

```python
import functools

import jax
import jax.numpy as jnp
from jax import lax
from jax.experimental import pallas as pl
from jax.experimental.pallas import tpu as pltpu
from jax.sharding import PartitionSpec as P

TILE = 128
CODE_ROWS = 16
LEVELS = 32767.0
STEPS_PER_OCTAVE = 64.0
BLOCK_ROWS = 512
ADD_ROWS = 512


def apply_mask(amplitudes, tile_mask):
    tiles_m, tiles_k = tile_mask.shape
    tile_rows = amplitudes.shape[0] // tiles_m
    tile_cols = amplitudes.shape[1] // tiles_k
    blocks = amplitudes.reshape(tiles_m, tile_rows, tiles_k, tile_cols)
    weights = tile_mask.astype(amplitudes.dtype)[:, None, :, None]
    return (blocks * weights).reshape(amplitudes.shape)


def general(amplitudes, integrals, tile_mask):
    masked = apply_mask(amplitudes, tile_mask)
    partial_sums = jnp.dot(
        masked,
        lax.all_gather(integrals, "row", axis=1, tiled=True),
        preferred_element_type=jnp.float32,
    )
    summed = lax.psum_scatter(partial_sums, "col", scatter_dimension=1, tiled=True)
    return summed.astype(jnp.bfloat16)


def decode(ref, step, rows, block_rows, weight):
    groups = block_rows // TILE
    start = pl.multiple_of(step * block_rows, block_rows)
    levels = ref[pl.ds(start, block_rows), :].astype(jnp.int32).astype(jnp.float32)
    codes = ref[pl.ds(rows, CODE_ROWS), :].astype(jnp.int32).astype(jnp.float32)
    pieces = []
    which = lax.broadcasted_iota(jnp.int32, codes.shape, 0)
    for g in range(groups):
        code = jnp.sum(jnp.where(which == step * groups + g, codes, 0.0), axis=0, keepdims=True)
        unit = jnp.exp2(code / STEPS_PER_OCTAVE) * (weight / LEVELS)
        pieces.append(levels[g * TILE : (g + 1) * TILE] * unit)
    return jnp.concatenate(pieces, axis=0)


def encode(acc, step, out_ref, code_ref, rows):
    block_rows = acc.shape[0]
    groups = block_rows // TILE
    pieces = []
    for g in range(groups):
        part = acc[g * TILE : (g + 1) * TILE]
        largest = jnp.max(jnp.abs(part), axis=0, keepdims=True)
        code = jnp.ceil(jnp.log(jnp.maximum(largest, 1e-30)) * (STEPS_PER_OCTAVE / 0.6931471805599453))
        scaled = jnp.round(part * (jnp.exp2(-code / STEPS_PER_OCTAVE) * LEVELS))
        pieces.append(jnp.clip(scaled, -LEVELS, LEVELS).astype(jnp.int32))
        code_ref[pl.ds(step * groups + g, 1), :] = code
    start = pl.multiple_of(step * block_rows, block_rows)
    out_ref[pl.ds(start, block_rows), :] = jnp.concatenate(pieces, axis=0).astype(jnp.int16)

    @pl.when(step == pl.num_programs(0) - 1)
    def _():
        out_ref[pl.ds(rows, CODE_ROWS), :] = code_ref[...].astype(jnp.int32).astype(jnp.int16)


def fetch(chosen, core, mine, other, b, first, sem):
    width = mine[0][0].shape[1]
    here = pl.ds(pl.multiple_of(first + core * width, width), width)
    there = pl.ds(pl.multiple_of(first + (1 - core) * width, width), width)
    for j in range(len(mine)):

        @pl.when(chosen == j)
        def _():
            for parts, lanes in ((mine[j], here), (other[j], there)):
                start = 0
                for part in parts:
                    pltpu.make_async_copy(part, b.at[pl.ds(start, part.shape[0]), lanes], sem).start()
                    start += part.shape[0]


def multiply_kernel(slots, kinds, rows, width, sources, facts, a_ref, *refs):
    held, refs = list(refs[: sum(sources)]), refs[sum(sources) :]
    held = [[held.pop(0) for _ in range(parts)] for parts in sources]
    mine, other = held[: len(held) // 2], held[len(held) // 2 :]
    count = sum(len(kind) for kind in kinds)
    outs, refs = list(refs[:count]), refs[count:]
    b, sems, codes = refs[0], refs[1], list(refs[2:])
    step = pl.program_id(0)

    @pl.when(step == 0)
    def _():
        for j, slot in enumerate(slots):
            fetch(facts[slot] ^ facts[CHIP], facts[CORE], mine, other, b, j * width, sems.at[j])
        for j in range(len(slots)):
            span = b.at[:, pl.ds(j * width, width)]
            pltpu.make_async_copy(span, span, sems.at[j]).wait()

    acc = jnp.dot(a_ref[...], b[...], preferred_element_type=jnp.float32)
    for j, kind in enumerate(kinds):
        part = acc[:, j * width : (j + 1) * width]
        for form in kind:
            out_ref = outs.pop(0)
            if form != "plain":
                lanes = {"coded": slice(None), "left": slice(width // 2), "right": slice(width // 2, None)}[form]
                encode(part[:, lanes], step, out_ref, codes.pop(0), rows)
            else:
                out_ref[...] = part


def multiply(facts, masked, columns, slots, kinds):
    rows, depth = masked.shape
    columns = [x if isinstance(x, tuple) else (x,) for x in columns]
    sources = tuple(len(parts) for parts in columns)
    columns = [part for parts in columns for part in parts]
    width = columns[0].shape[1] * 2
    packed = (rows + CODE_ROWS, width)
    forms = [form for kind in kinds for form in kind]
    part = (packed[0], width // 2)
    specs = {
        "coded": (pl.BlockSpec(packed, lambda i, c: (0, 0)), jax.ShapeDtypeStruct(packed, jnp.int16)),
        "plain": (pl.BlockSpec((BLOCK_ROWS, width), lambda i, c: (i, 0)), jax.ShapeDtypeStruct((rows, width), jnp.float32)),
    }
    specs["left"] = specs["right"] = (pl.BlockSpec(part, lambda i, c: (0, 0)), jax.ShapeDtypeStruct(part, jnp.int16))
    outs = [specs[form] for form in forms]
    return pl.pallas_call(
        functools.partial(multiply_kernel, slots, kinds, rows, width, sources),
        out_shape=[shape for _, shape in outs],
        grid_spec=pltpu.PrefetchScalarGridSpec(
            num_scalar_prefetch=1,
            grid=(rows // BLOCK_ROWS,),
            in_specs=[pl.BlockSpec((BLOCK_ROWS, depth), lambda i, c: (i, 0))]
            + [pl.BlockSpec(memory_space=pl.ANY)] * len(columns),
            out_specs=[spec for spec, _ in outs],
            scratch_shapes=[pltpu.VMEM((depth, width * len(slots)), masked.dtype), pltpu.SemaphoreType.DMA((len(slots),))]
            + [pltpu.VMEM((CODE_ROWS, specs[form][1].shape[1]), jnp.float32) for form in forms if form != "plain"],
        ),
        compiler_params=pltpu.CompilerParams(vmem_limit_bytes=24 * 1024 * 1024),
        cost_estimate=pl.CostEstimate(flops=3000000000, bytes_accessed=9000000, transcendentals=0),
    )(facts, masked, *columns)


def add_kernel(terms, rows, facts, *refs):
    step = pl.program_id(0)
    count = sum(parts for _, parts in terms)
    blocks, refs = list(refs[:count]), refs[count:]
    acc = None
    for weight, parts in terms:
        share = facts[weight].astype(jnp.float32)
        block, *more = [blocks.pop(0) for _ in range(parts)]
        if block.dtype == jnp.int16:
            value = jnp.concatenate([decode(x, step, rows, ADD_ROWS, share) for x in (block, *more)], axis=1)
        else:
            value = block[...] if weight == ALWAYS else block[...] * share
        acc = value if acc is None else acc + value
    if refs[0].dtype == jnp.int16:
        encode(acc, step, refs[0], refs[1], rows)
    else:
        refs[0][...] = acc.astype(refs[0].dtype)


def add(facts, terms, dtype=jnp.int16):
    rows, width = terms[0][0].shape
    terms = [(x if isinstance(x, tuple) else (x,), weight) for x, weight in terms]
    blocks = [part for x, _ in terms for part in x]
    packed = (rows + CODE_ROWS, width)
    plain = pl.BlockSpec((ADD_ROWS, width), lambda i, c: (i, 0))
    coded = pl.BlockSpec(packed, lambda i, c: (0, 0))
    if dtype == jnp.int16:
        out_spec, out_shape = coded, jax.ShapeDtypeStruct(packed, dtype)
        scratch = [pltpu.VMEM((CODE_ROWS, width), jnp.float32)]
    else:
        out_spec, out_shape = plain, jax.ShapeDtypeStruct((rows, width), dtype)
        scratch = []
    return pl.pallas_call(
        functools.partial(add_kernel, tuple((weight, len(x)) for x, weight in terms), rows),
        out_shape=out_shape,
        grid_spec=pltpu.PrefetchScalarGridSpec(
            num_scalar_prefetch=1,
            grid=(rows // ADD_ROWS,),
            in_specs=[pl.BlockSpec(x.shape, lambda i, c: (0, 0)) if x.dtype == jnp.int16 else plain for x in blocks],
            out_specs=out_spec,
            scratch_shapes=scratch,
        ),
        compiler_params=pltpu.CompilerParams(vmem_limit_bytes=16 * 1024 * 1024),
        cost_estimate=pl.CostEstimate(flops=3000000000, bytes_accessed=9000000, transcendentals=0),
    )(facts, *blocks)


def plan_of(chip, at):
    end = at in (0, 3)
    far, near = (3, 2) if at < 2 else (0, 1)
    late = chip == (0 if at < 2 else 3)
    passed = (near, far) if late else (far, near)
    home = 0 if at < 2 else 3
    if end:
        first, second, third, relayed = passed[0], passed[1], 3 - near, (chip, chip)
    else:
        straight = chip ^ home != 3
        first, second = (home, chip) if straight else (chip, home)
        third, relayed = chip, passed
    early = chip != (3 if at < 2 else 0)
    return (first, second, third, *relayed, at, 1, int(end and early), int(end and not early), int(not end))


FIRST, SECOND, THIRD, RELAY_ONE, RELAY_TWO, HERE, ALWAYS, EARLY, LATE, INNER, CORE, CHIP = range(12)


def line_pairs(choose):
    return [(row * 4 + a, row * 4 + b) for row in range(8) for a, b in choose(row // 2)]


def line_of_four(amplitudes, integrals, tile_mask):
    row = lax.axis_index("row")
    at = lax.axis_index("col")
    core, chip = row % 2, row // 2

    def after(value, *others):
        return lax.optimization_barrier((value, *others))[0]

    def across(block, bit):
        return lax.ppermute(block, "row", [(i, i ^ bit) for i in range(8)])

    def along(block, choose):
        return lax.ppermute(block, ("row", "col"), line_pairs(choose))

    def pairs(p):
        return [(0, 1), (1, 0), (2, 3), (3, 2)]

    inward = [(0, 1), (3, 2)]

    def second_pairs(p):
        return inward + [(1, 0)] * (p == 3) + [(2, 3)] * (p == 0)

    def relay_one(p):
        return [(1, 2 if p == 0 else 3), (2, 1 if p == 3 else 0)]

    def relay_two(p):
        return [(1, 3 if p == 0 else 2), (2, 0 if p == 3 else 1)]

    by_x, by_y = across(integrals, 2), across(integrals, 4)
    plans = jnp.asarray([plan_of(p, z) for p in range(4) for z in range(4)], jnp.int32)
    planned = lax.dynamic_slice_in_dim(plans, chip * 4 + at, 1)[0]
    facts = jnp.concatenate([planned, jnp.stack([core, chip]).astype(jnp.int32)])
    twin = across(after(integrals, facts), 1)
    masked = apply_mask(amplitudes, tile_mask)
    by_x, by_y = after(by_x, masked, facts), after(by_y, masked, facts)
    half = integrals.shape[0] // 2
    by_both = across(by_y[:half], 2), across(by_x[half:], 4)
    straight = (integrals, by_x, by_y, twin, across(by_x, 1), across(by_y, 1))
    coded, plain = ("coded",), ("plain",)
    out_left, out_right = multiply(facts, masked, straight, (FIRST,), (("left", "right"),))
    one = along(out_left, pairs), along(out_right, pairs)
    (share_one,) = multiply(after(facts, out_right), masked, straight, (RELAY_ONE,), (plain,))
    columns = (*straight[:3], by_both, *straight[3:], tuple(across(after(x, share_one), 1) for x in by_both))
    (out_two,) = multiply(after(facts, share_one, one[0]), masked, columns, (SECOND,), (coded,))
    two = along(out_two, second_pairs)
    out_three, share_two = multiply(
        after(facts, out_two), masked, columns, (THIRD, RELAY_TWO), (coded, plain)
    )
    out_relay_one = add(after(facts, out_three), [(share_one, ALWAYS), (one, ALWAYS)])
    relayed_one = along(out_relay_one, relay_one)
    three = along(after(out_three, out_relay_one), lambda p: inward)
    out_relay_two = add(after(facts, out_three), [(share_two, ALWAYS), (two, ALWAYS)])
    relayed_two = along(out_relay_two, relay_two)
    (own,) = multiply(after(facts, out_relay_two), masked, columns, (HERE,), (plain,))
    most = add(
        facts,
        [(own, ALWAYS), (one, EARLY), (two, LATE), (relayed_one, ALWAYS)],
        jnp.float32,
    )
    return add(facts, [(most, ALWAYS), (three, INNER), (relayed_two, ALWAYS)], jnp.bfloat16)


def solution(mesh):
    body = line_of_four if mesh.shape["col"] == 4 and mesh.shape["row"] == 8 else general
    placed = (P("row", "col"), P("col", "row"), P("row", "col"))
    return jax.shard_map(
        body, mesh=mesh, in_specs=placed, out_specs=P("row", "col"), check_vma=False
    )
```

```python
import functools

import jax
import jax.numpy as jnp
from jax import lax
from jax.experimental import pallas as pl
from jax.experimental.pallas import tpu as pltpu
from jax.sharding import PartitionSpec as P

TILE = 128
CODE_ROWS = 16
LEVELS = 32767.0
STEPS_PER_OCTAVE = 64.0
BLOCK_ROWS = 512
ADD_ROWS = 512


def apply_mask(amplitudes, tile_mask):
    tiles_m, tiles_k = tile_mask.shape
    tile_rows = amplitudes.shape[0] // tiles_m
    tile_cols = amplitudes.shape[1] // tiles_k
    blocks = amplitudes.reshape(tiles_m, tile_rows, tiles_k, tile_cols)
    weights = tile_mask.astype(amplitudes.dtype)[:, None, :, None]
    return (blocks * weights).reshape(amplitudes.shape)


def general(amplitudes, integrals, tile_mask):
    masked = apply_mask(amplitudes, tile_mask)
    partial_sums = jnp.dot(
        masked,
        lax.all_gather(integrals, "row", axis=1, tiled=True),
        preferred_element_type=jnp.float32,
    )
    summed = lax.psum_scatter(partial_sums, "col", scatter_dimension=1, tiled=True)
    return summed.astype(jnp.bfloat16)


def decode(ref, step, rows, block_rows, weight):
    groups = block_rows // TILE
    start = pl.multiple_of(step * block_rows, block_rows)
    levels = ref[pl.ds(start, block_rows), :].astype(jnp.int32).astype(jnp.float32)
    codes = ref[pl.ds(rows, CODE_ROWS), :].astype(jnp.int32).astype(jnp.float32)
    pieces = []
    which = lax.broadcasted_iota(jnp.int32, codes.shape, 0)
    for g in range(groups):
        code = jnp.sum(jnp.where(which == step * groups + g, codes, 0.0), axis=0, keepdims=True)
        unit = jnp.exp2(code / STEPS_PER_OCTAVE) * (weight / LEVELS)
        pieces.append(levels[g * TILE : (g + 1) * TILE] * unit)
    return jnp.concatenate(pieces, axis=0)


def encode(acc, step, out_ref, code_ref, rows):
    block_rows = acc.shape[0]
    groups = block_rows // TILE
    pieces = []
    for g in range(groups):
        part = acc[g * TILE : (g + 1) * TILE]
        largest = jnp.max(jnp.abs(part), axis=0, keepdims=True)
        code = jnp.ceil(jnp.log(jnp.maximum(largest, 1e-30)) * (STEPS_PER_OCTAVE / 0.6931471805599453))
        scaled = jnp.round(part * (jnp.exp2(-code / STEPS_PER_OCTAVE) * LEVELS))
        pieces.append(jnp.clip(scaled, -LEVELS, LEVELS).astype(jnp.int32))
        code_ref[pl.ds(step * groups + g, 1), :] = code
    start = pl.multiple_of(step * block_rows, block_rows)
    out_ref[pl.ds(start, block_rows), :] = jnp.concatenate(pieces, axis=0).astype(jnp.int16)

    @pl.when(step == pl.num_programs(0) - 1)
    def _():
        out_ref[pl.ds(rows, CODE_ROWS), :] = code_ref[...].astype(jnp.int32).astype(jnp.int16)


def fetch(chosen, core, mine, other, b, first, sem):
    width = mine[0][0].shape[1]
    here = pl.ds(pl.multiple_of(first + core * width, width), width)
    there = pl.ds(pl.multiple_of(first + (1 - core) * width, width), width)
    for j in range(len(mine)):

        @pl.when(chosen == j)
        def _():
            for parts, lanes in ((mine[j], here), (other[j], there)):
                start = 0
                for part in parts:
                    pltpu.make_async_copy(part, b.at[pl.ds(start, part.shape[0]), lanes], sem).start()
                    start += part.shape[0]


def multiply_kernel(slots, kinds, rows, width, sources, facts, a_ref, *refs):
    held, refs = list(refs[: sum(sources)]), refs[sum(sources) :]
    held = [[held.pop(0) for _ in range(parts)] for parts in sources]
    mine, other = held[: len(held) // 2], held[len(held) // 2 :]
    count = sum(len(kind) for kind in kinds)
    outs, refs = list(refs[:count]), refs[count:]
    b, sems, codes = refs[0], refs[1], list(refs[2:])
    step = pl.program_id(0)

    @pl.when(step == 0)
    def _():
        for j, slot in enumerate(slots):
            fetch(facts[slot] ^ facts[CHIP], facts[CORE], mine, other, b, j * width, sems.at[j])
        for j in range(len(slots)):
            span = b.at[:, pl.ds(j * width, width)]
            pltpu.make_async_copy(span, span, sems.at[j]).wait()

    acc = jnp.dot(a_ref[...], b[...], preferred_element_type=jnp.float32)
    for j, kind in enumerate(kinds):
        part = acc[:, j * width : (j + 1) * width]
        for form in kind:
            out_ref = outs.pop(0)
            if form != "plain":
                lanes = {"coded": slice(None), "left": slice(width // 2), "right": slice(width // 2, None)}[form]
                encode(part[:, lanes], step, out_ref, codes.pop(0), rows)
            else:
                out_ref[...] = part


def multiply(facts, masked, columns, slots, kinds):
    rows, depth = masked.shape
    columns = [x if isinstance(x, tuple) else (x,) for x in columns]
    sources = tuple(len(parts) for parts in columns)
    columns = [part for parts in columns for part in parts]
    width = columns[0].shape[1] * 2
    packed = (rows + CODE_ROWS, width)
    forms = [form for kind in kinds for form in kind]
    part = (packed[0], width // 2)
    specs = {
        "coded": (pl.BlockSpec(packed, lambda i, c: (0, 0)), jax.ShapeDtypeStruct(packed, jnp.int16)),
        "plain": (pl.BlockSpec((BLOCK_ROWS, width), lambda i, c: (i, 0)), jax.ShapeDtypeStruct((rows, width), jnp.float32)),
    }
    specs["left"] = specs["right"] = (pl.BlockSpec(part, lambda i, c: (0, 0)), jax.ShapeDtypeStruct(part, jnp.int16))
    outs = [specs[form] for form in forms]
    return pl.pallas_call(
        functools.partial(multiply_kernel, slots, kinds, rows, width, sources),
        out_shape=[shape for _, shape in outs],
        grid_spec=pltpu.PrefetchScalarGridSpec(
            num_scalar_prefetch=1,
            grid=(rows // BLOCK_ROWS,),
            in_specs=[pl.BlockSpec((BLOCK_ROWS, depth), lambda i, c: (i, 0))]
            + [pl.BlockSpec(memory_space=pl.ANY)] * len(columns),
            out_specs=[spec for spec, _ in outs],
            scratch_shapes=[pltpu.VMEM((depth, width * len(slots)), masked.dtype), pltpu.SemaphoreType.DMA((len(slots),))]
            + [pltpu.VMEM((CODE_ROWS, specs[form][1].shape[1]), jnp.float32) for form in forms if form != "plain"],
        ),
        compiler_params=pltpu.CompilerParams(vmem_limit_bytes=24 * 1024 * 1024),
        cost_estimate=pl.CostEstimate(flops=3000000000, bytes_accessed=9000000, transcendentals=0),
    )(facts, masked, *columns)


def add_kernel(terms, rows, facts, *refs):
    step = pl.program_id(0)
    count = sum(parts for _, parts in terms)
    blocks, refs = list(refs[:count]), refs[count:]
    acc = None
    for weight, parts in terms:
        share = facts[weight].astype(jnp.float32)
        block, *more = [blocks.pop(0) for _ in range(parts)]
        if block.dtype == jnp.int16:
            value = jnp.concatenate([decode(x, step, rows, ADD_ROWS, share) for x in (block, *more)], axis=1)
        else:
            value = block[...] if weight == ALWAYS else block[...] * share
        acc = value if acc is None else acc + value
    if refs[0].dtype == jnp.int16:
        encode(acc, step, refs[0], refs[1], rows)
    else:
        refs[0][...] = acc.astype(refs[0].dtype)


def add(facts, terms, dtype=jnp.int16):
    rows, width = terms[0][0].shape
    terms = [(x if isinstance(x, tuple) else (x,), weight) for x, weight in terms]
    blocks = [part for x, _ in terms for part in x]
    packed = (rows + CODE_ROWS, width)
    plain = pl.BlockSpec((ADD_ROWS, width), lambda i, c: (i, 0))
    coded = pl.BlockSpec(packed, lambda i, c: (0, 0))
    if dtype == jnp.int16:
        out_spec, out_shape = coded, jax.ShapeDtypeStruct(packed, dtype)
        scratch = [pltpu.VMEM((CODE_ROWS, width), jnp.float32)]
    else:
        out_spec, out_shape = plain, jax.ShapeDtypeStruct((rows, width), dtype)
        scratch = []
    return pl.pallas_call(
        functools.partial(add_kernel, tuple((weight, len(x)) for x, weight in terms), rows),
        out_shape=out_shape,
        grid_spec=pltpu.PrefetchScalarGridSpec(
            num_scalar_prefetch=1,
            grid=(rows // ADD_ROWS,),
            in_specs=[pl.BlockSpec(x.shape, lambda i, c: (0, 0)) if x.dtype == jnp.int16 else plain for x in blocks],
            out_specs=out_spec,
            scratch_shapes=scratch,
        ),
        compiler_params=pltpu.CompilerParams(vmem_limit_bytes=16 * 1024 * 1024),
        cost_estimate=pl.CostEstimate(flops=3000000000, bytes_accessed=9000000, transcendentals=0),
    )(facts, *blocks)


def plan_of(chip, at):
    end = at in (0, 3)
    far, near = (3, 2) if at < 2 else (0, 1)
    late = chip == (0 if at < 2 else 3)
    passed = (near, far) if late else (far, near)
    home = 0 if at < 2 else 3
    if end:
        first, second, third, relayed = passed[0], passed[1], 3 - near, (chip, chip)
    else:
        straight = chip ^ home != 3
        first, second = (home, chip) if straight else (chip, home)
        third, relayed = chip, passed
    early = chip != (3 if at < 2 else 0)
    return (first, second, third, *relayed, at, 1, int(end and early), int(end and not early), int(not end))


FIRST, SECOND, THIRD, RELAY_ONE, RELAY_TWO, HERE, ALWAYS, EARLY, LATE, INNER, CORE, CHIP = range(12)


def line_pairs(choose):
    return [(row * 4 + a, row * 4 + b) for row in range(8) for a, b in choose(row // 2)]


def line_of_four(amplitudes, integrals, tile_mask):
    row = lax.axis_index("row")
    at = lax.axis_index("col")
    core, chip = row % 2, row // 2

    def after(value, *others):
        return lax.optimization_barrier((value, *others))[0]

    def across(block, bit):
        return lax.ppermute(block, "row", [(i, i ^ bit) for i in range(8)])

    def along(block, choose):
        return lax.ppermute(block, ("row", "col"), line_pairs(choose))

    def pairs(p):
        return [(0, 1), (1, 0), (2, 3), (3, 2)]

    inward = [(0, 1), (3, 2)]

    def second_pairs(p):
        return inward + [(1, 0)] * (p == 3) + [(2, 3)] * (p == 0)

    def relay_one(p):
        return [(1, 2 if p == 0 else 3), (2, 1 if p == 3 else 0)]

    def relay_two(p):
        return [(1, 3 if p == 0 else 2), (2, 0 if p == 3 else 1)]

    by_x, by_y = across(integrals, 2), across(integrals, 4)
    plans = jnp.asarray([plan_of(p, z) for p in range(4) for z in range(4)], jnp.int32)
    planned = lax.dynamic_slice_in_dim(plans, chip * 4 + at, 1)[0]
    facts = jnp.concatenate([planned, jnp.stack([core, chip]).astype(jnp.int32)])
    twin = across(after(integrals, facts), 1)
    masked = apply_mask(amplitudes, tile_mask)
    by_x, by_y = after(by_x, masked, facts), after(by_y, masked, facts)
    half = integrals.shape[0] // 2
    by_both = across(by_y[:half], 2), across(by_x[half:], 4)
    straight = (integrals, by_x, by_y, twin, across(by_x, 1), across(by_y, 1))
    coded, plain = ("coded",), ("plain",)
    out_left, out_right = multiply(facts, masked, straight, (FIRST,), (("left", "right"),))
    one = along(out_left, pairs), along(out_right, pairs)
    (share_one,) = multiply(after(facts, out_right), masked, straight, (RELAY_ONE,), (plain,))
    columns = (*straight[:3], by_both, *straight[3:], tuple(across(after(x, share_one), 1) for x in by_both))
    (out_two,) = multiply(after(facts, share_one, one[0]), masked, columns, (SECOND,), (coded,))
    two = along(out_two, second_pairs)
    out_relay_one = add(after(facts, out_two), [(share_one, ALWAYS), (one, ALWAYS)])
    relayed_one = along(out_relay_one, relay_one)
    out_three, share_two = multiply(
        after(facts, out_relay_one), masked, columns, (THIRD, RELAY_TWO), (coded, plain)
    )
    three = along(out_three, lambda p: inward)
    out_relay_two = add(after(facts, out_three), [(share_two, ALWAYS), (two, ALWAYS)])
    relayed_two = along(out_relay_two, relay_two)
    (own,) = multiply(after(facts, out_relay_two), masked, columns, (HERE,), (plain,))
    most = add(
        facts,
        [(own, ALWAYS), (one, EARLY), (two, LATE), (relayed_one, ALWAYS)],
        jnp.float32,
    )
    return add(facts, [(most, ALWAYS), (three, INNER), (relayed_two, ALWAYS)], jnp.bfloat16)


def solution(mesh):
    body = line_of_four if mesh.shape["col"] == 4 and mesh.shape["row"] == 8 else general
    placed = (P("row", "col"), P("col", "row"), P("row", "col"))
    return jax.shard_map(
        body, mesh=mesh, in_specs=placed, out_specs=P("row", "col"), check_vma=False
    )
```

```python
import functools

import jax
import jax.numpy as jnp
from jax import lax
from jax.experimental import pallas as pl
from jax.experimental.pallas import tpu as pltpu
from jax.sharding import PartitionSpec as P

TILE = 128
CODE_ROWS = 16
LEVELS = 32767.0
STEPS_PER_OCTAVE = 64.0
BLOCK_ROWS = 512
ADD_ROWS = 512


def apply_mask(amplitudes, tile_mask):
    tiles_m, tiles_k = tile_mask.shape
    tile_rows = amplitudes.shape[0] // tiles_m
    tile_cols = amplitudes.shape[1] // tiles_k
    blocks = amplitudes.reshape(tiles_m, tile_rows, tiles_k, tile_cols)
    weights = tile_mask.astype(amplitudes.dtype)[:, None, :, None]
    return (blocks * weights).reshape(amplitudes.shape)


def general(amplitudes, integrals, tile_mask):
    masked = apply_mask(amplitudes, tile_mask)
    partial_sums = jnp.dot(
        masked,
        lax.all_gather(integrals, "row", axis=1, tiled=True),
        preferred_element_type=jnp.float32,
    )
    summed = lax.psum_scatter(partial_sums, "col", scatter_dimension=1, tiled=True)
    return summed.astype(jnp.bfloat16)


def decode(ref, step, rows, block_rows, weight):
    groups = block_rows // TILE
    start = pl.multiple_of(step * block_rows, block_rows)
    levels = ref[pl.ds(start, block_rows), :].astype(jnp.int32).astype(jnp.float32)
    codes = ref[pl.ds(rows, CODE_ROWS), :].astype(jnp.int32).astype(jnp.float32)
    pieces = []
    which = lax.broadcasted_iota(jnp.int32, codes.shape, 0)
    for g in range(groups):
        code = jnp.sum(jnp.where(which == step * groups + g, codes, 0.0), axis=0, keepdims=True)
        unit = jnp.exp2(code / STEPS_PER_OCTAVE) * (weight / LEVELS)
        pieces.append(levels[g * TILE : (g + 1) * TILE] * unit)
    return jnp.concatenate(pieces, axis=0)


def encode(acc, step, out_ref, code_ref, rows):
    block_rows = acc.shape[0]
    groups = block_rows // TILE
    pieces = []
    for g in range(groups):
        part = acc[g * TILE : (g + 1) * TILE]
        largest = jnp.max(jnp.abs(part), axis=0, keepdims=True)
        code = jnp.ceil(jnp.log(jnp.maximum(largest, 1e-30)) * (STEPS_PER_OCTAVE / 0.6931471805599453))
        scaled = jnp.round(part * (jnp.exp2(-code / STEPS_PER_OCTAVE) * LEVELS))
        pieces.append(jnp.clip(scaled, -LEVELS, LEVELS).astype(jnp.int32))
        code_ref[pl.ds(step * groups + g, 1), :] = code
    start = pl.multiple_of(step * block_rows, block_rows)
    out_ref[pl.ds(start, block_rows), :] = jnp.concatenate(pieces, axis=0).astype(jnp.int16)

    @pl.when(step == pl.num_programs(0) - 1)
    def _():
        out_ref[pl.ds(rows, CODE_ROWS), :] = code_ref[...].astype(jnp.int32).astype(jnp.int16)


def fetch(chosen, core, mine, other, b, first, sem):
    width = mine[0][0].shape[1]
    here = pl.ds(pl.multiple_of(first + core * width, width), width)
    there = pl.ds(pl.multiple_of(first + (1 - core) * width, width), width)
    for j in range(len(mine)):

        @pl.when(chosen == j)
        def _():
            for parts, lanes in ((mine[j], here), (other[j], there)):
                start = 0
                for part in parts:
                    pltpu.make_async_copy(part, b.at[pl.ds(start, part.shape[0]), lanes], sem).start()
                    start += part.shape[0]


def multiply_kernel(slots, kinds, rows, width, sources, facts, a_ref, *refs):
    held, refs = list(refs[: sum(sources)]), refs[sum(sources) :]
    held = [[held.pop(0) for _ in range(parts)] for parts in sources]
    mine, other = held[: len(held) // 2], held[len(held) // 2 :]
    count = sum(len(kind) for kind in kinds)
    outs, refs = list(refs[:count]), refs[count:]
    b, sems, codes = refs[0], refs[1], list(refs[2:])
    step = pl.program_id(0)

    @pl.when(step == 0)
    def _():
        for j, slot in enumerate(slots):
            fetch(facts[slot] ^ facts[CHIP], facts[CORE], mine, other, b, j * width, sems.at[j])
        for j in range(len(slots)):
            span = b.at[:, pl.ds(j * width, width)]
            pltpu.make_async_copy(span, span, sems.at[j]).wait()

    acc = jnp.dot(a_ref[...], b[...], preferred_element_type=jnp.float32)
    for j, kind in enumerate(kinds):
        part = acc[:, j * width : (j + 1) * width]
        for form in kind:
            out_ref = outs.pop(0)
            if form != "plain":
                lanes = {"coded": slice(None), "left": slice(width // 2), "right": slice(width // 2, None)}[form]
                encode(part[:, lanes], step, out_ref, codes.pop(0), rows)
            else:
                out_ref[...] = part


def multiply(facts, masked, columns, slots, kinds):
    rows, depth = masked.shape
    columns = [x if isinstance(x, tuple) else (x,) for x in columns]
    sources = tuple(len(parts) for parts in columns)
    columns = [part for parts in columns for part in parts]
    width = columns[0].shape[1] * 2
    packed = (rows + CODE_ROWS, width)
    forms = [form for kind in kinds for form in kind]
    part = (packed[0], width // 2)
    specs = {
        "coded": (pl.BlockSpec(packed, lambda i, c: (0, 0)), jax.ShapeDtypeStruct(packed, jnp.int16)),
        "plain": (pl.BlockSpec((BLOCK_ROWS, width), lambda i, c: (i, 0)), jax.ShapeDtypeStruct((rows, width), jnp.float32)),
    }
    specs["left"] = specs["right"] = (pl.BlockSpec(part, lambda i, c: (0, 0)), jax.ShapeDtypeStruct(part, jnp.int16))
    outs = [specs[form] for form in forms]
    return pl.pallas_call(
        functools.partial(multiply_kernel, slots, kinds, rows, width, sources),
        out_shape=[shape for _, shape in outs],
        grid_spec=pltpu.PrefetchScalarGridSpec(
            num_scalar_prefetch=1,
            grid=(rows // BLOCK_ROWS,),
            in_specs=[pl.BlockSpec((BLOCK_ROWS, depth), lambda i, c: (i, 0))]
            + [pl.BlockSpec(memory_space=pl.ANY)] * len(columns),
            out_specs=[spec for spec, _ in outs],
            scratch_shapes=[pltpu.VMEM((depth, width * len(slots)), masked.dtype), pltpu.SemaphoreType.DMA((len(slots),))]
            + [pltpu.VMEM((CODE_ROWS, specs[form][1].shape[1]), jnp.float32) for form in forms if form != "plain"],
        ),
        compiler_params=pltpu.CompilerParams(vmem_limit_bytes=24 * 1024 * 1024),
        cost_estimate=pl.CostEstimate(flops=3000000000, bytes_accessed=9000000, transcendentals=0),
    )(facts, masked, *columns)


def add_kernel(terms, rows, facts, *refs):
    step = pl.program_id(0)
    count = sum(parts for _, parts in terms)
    blocks, refs = list(refs[:count]), refs[count:]
    acc = None
    for weight, parts in terms:
        share = facts[weight].astype(jnp.float32)
        block, *more = [blocks.pop(0) for _ in range(parts)]
        if block.dtype == jnp.int16:
            value = jnp.concatenate([decode(x, step, rows, ADD_ROWS, share) for x in (block, *more)], axis=1)
        else:
            value = block[...] if weight == ALWAYS else block[...] * share
        acc = value if acc is None else acc + value
    if refs[0].dtype == jnp.int16:
        encode(acc, step, refs[0], refs[1], rows)
    else:
        refs[0][...] = acc.astype(refs[0].dtype)


def add(facts, terms, dtype=jnp.int16):
    rows, width = terms[0][0].shape
    terms = [(x if isinstance(x, tuple) else (x,), weight) for x, weight in terms]
    blocks = [part for x, _ in terms for part in x]
    packed = (rows + CODE_ROWS, width)
    plain = pl.BlockSpec((ADD_ROWS, width), lambda i, c: (i, 0))
    coded = pl.BlockSpec(packed, lambda i, c: (0, 0))
    if dtype == jnp.int16:
        out_spec, out_shape = coded, jax.ShapeDtypeStruct(packed, dtype)
        scratch = [pltpu.VMEM((CODE_ROWS, width), jnp.float32)]
    else:
        out_spec, out_shape = plain, jax.ShapeDtypeStruct((rows, width), dtype)
        scratch = []
    return pl.pallas_call(
        functools.partial(add_kernel, tuple((weight, len(x)) for x, weight in terms), rows),
        out_shape=out_shape,
        grid_spec=pltpu.PrefetchScalarGridSpec(
            num_scalar_prefetch=1,
            grid=(rows // ADD_ROWS,),
            in_specs=[pl.BlockSpec(x.shape, lambda i, c: (0, 0)) if x.dtype == jnp.int16 else plain for x in blocks],
            out_specs=out_spec,
            scratch_shapes=scratch,
        ),
        compiler_params=pltpu.CompilerParams(vmem_limit_bytes=16 * 1024 * 1024),
        cost_estimate=pl.CostEstimate(flops=3000000000, bytes_accessed=9000000, transcendentals=0),
    )(facts, *blocks)


def plan_of(chip, at):
    end = at in (0, 3)
    far, near = (3, 2) if at < 2 else (0, 1)
    late = chip == (0 if at < 2 else 3)
    passed = (near, far) if late else (far, near)
    home = 0 if at < 2 else 3
    if end:
        first, second, third, relayed = passed[0], passed[1], 3 - near, (chip, chip)
    else:
        straight = chip ^ home != 3
        first, second = (home, chip) if straight else (chip, home)
        third, relayed = chip, passed
    early = chip != (3 if at < 2 else 0)
    return (first, second, third, *relayed, at, 1, int(end and early), int(end and not early), int(not end))


FIRST, SECOND, THIRD, RELAY_ONE, RELAY_TWO, HERE, ALWAYS, EARLY, LATE, INNER, CORE, CHIP = range(12)


def line_pairs(choose):
    return [(row * 4 + a, row * 4 + b) for row in range(8) for a, b in choose(row // 2)]


def line_of_four(amplitudes, integrals, tile_mask):
    row = lax.axis_index("row")
    at = lax.axis_index("col")
    core, chip = row % 2, row // 2

    def after(value, *others):
        return lax.optimization_barrier((value, *others))[0]

    def across(block, bit):
        return lax.ppermute(block, "row", [(i, i ^ bit) for i in range(8)])

    def along(block, choose):
        return lax.ppermute(block, ("row", "col"), line_pairs(choose))

    def pairs(p):
        return [(0, 1), (1, 0), (2, 3), (3, 2)]

    inward = [(0, 1), (3, 2)]

    def second_pairs(p):
        return inward + [(1, 0)] * (p == 3) + [(2, 3)] * (p == 0)

    def relay_one(p):
        return [(1, 2 if p == 0 else 3), (2, 1 if p == 3 else 0)]

    def relay_two(p):
        return [(1, 3 if p == 0 else 2), (2, 0 if p == 3 else 1)]

    by_x, by_y = across(integrals, 2), across(integrals, 4)
    plans = jnp.asarray([plan_of(p, z) for p in range(4) for z in range(4)], jnp.int32)
    planned = lax.dynamic_slice_in_dim(plans, chip * 4 + at, 1)[0]
    facts = jnp.concatenate([planned, jnp.stack([core, chip]).astype(jnp.int32)])
    twin = across(after(integrals, facts), 1)
    masked = apply_mask(amplitudes, tile_mask)
    by_x, by_y = after(by_x, masked, facts), after(by_y, masked, facts)
    half = integrals.shape[0] // 2
    by_both = across(by_y[:half], 2), across(by_x[half:], 4)
    straight = (integrals, by_x, by_y, twin, across(by_x, 1), across(by_y, 1))
    coded, plain = ("coded",), ("plain",)
    out_left, out_right = multiply(facts, masked, straight, (FIRST,), (("left", "right"),))
    one = along(out_left, pairs), along(out_right, pairs)
    (share_one,) = multiply(after(facts, out_right), masked, straight, (RELAY_ONE,), (plain,))
    columns = (*straight[:3], by_both, *straight[3:], tuple(across(after(x, share_one), 1) for x in by_both))
    (out_two,) = multiply(after(facts, share_one, one[0]), masked, columns, (SECOND,), (coded,))
    two = along(out_two, second_pairs)
    out_relay_one = add(after(facts, out_two), [(share_one, ALWAYS), (one, ALWAYS)])
    relayed_one = along(out_relay_one, relay_one)
    out_three, share_two = multiply(
        after(facts, out_relay_one), masked, columns, (THIRD, RELAY_TWO), (coded, plain)
    )
    three = along(out_three, lambda p: inward)
    out_relay_two = add(after(facts, out_three), [(share_two, ALWAYS), (two, ALWAYS)])
    relayed_two = along(out_relay_two, relay_two)
    (own,) = multiply(after(facts, out_relay_two), masked, columns, (HERE,), (plain,))
    most = add(
        facts,
        [(own, ALWAYS), (one, EARLY), (two, LATE), (relayed_one, ALWAYS), (three, INNER)],
        jnp.float32,
    )
    return add(facts, [(most, ALWAYS), (relayed_two, ALWAYS)], jnp.bfloat16)


def solution(mesh):
    body = line_of_four if mesh.shape["col"] == 4 and mesh.shape["row"] == 8 else general
    placed = (P("row", "col"), P("col", "row"), P("row", "col"))
    return jax.shard_map(
        body, mesh=mesh, in_specs=placed, out_specs=P("row", "col"), check_vma=False
    )
```

```python
import functools

import jax
import jax.numpy as jnp
from jax import lax
from jax.experimental import pallas as pl
from jax.experimental.pallas import tpu as pltpu
from jax.sharding import PartitionSpec as P

TILE = 128
CODE_ROWS = 16
LEVELS = 32767.0
STEPS_PER_OCTAVE = 64.0
BLOCK_ROWS = 512
ADD_ROWS = 256


def apply_mask(amplitudes, tile_mask):
    tiles_m, tiles_k = tile_mask.shape
    tile_rows = amplitudes.shape[0] // tiles_m
    tile_cols = amplitudes.shape[1] // tiles_k
    blocks = amplitudes.reshape(tiles_m, tile_rows, tiles_k, tile_cols)
    weights = tile_mask.astype(amplitudes.dtype)[:, None, :, None]
    return (blocks * weights).reshape(amplitudes.shape)


def general(amplitudes, integrals, tile_mask):
    masked = apply_mask(amplitudes, tile_mask)
    partial_sums = jnp.dot(
        masked,
        lax.all_gather(integrals, "row", axis=1, tiled=True),
        preferred_element_type=jnp.float32,
    )
    summed = lax.psum_scatter(partial_sums, "col", scatter_dimension=1, tiled=True)
    return summed.astype(jnp.bfloat16)


def decode(ref, step, rows, block_rows, weight):
    groups = block_rows // TILE
    start = pl.multiple_of(step * block_rows, block_rows)
    levels = ref[pl.ds(start, block_rows), :].astype(jnp.int32).astype(jnp.float32)
    codes = ref[pl.ds(rows, CODE_ROWS), :].astype(jnp.int32).astype(jnp.float32)
    pieces = []
    which = lax.broadcasted_iota(jnp.int32, codes.shape, 0)
    for g in range(groups):
        code = jnp.sum(jnp.where(which == step * groups + g, codes, 0.0), axis=0, keepdims=True)
        unit = jnp.exp2(code / STEPS_PER_OCTAVE) * (weight / LEVELS)
        pieces.append(levels[g * TILE : (g + 1) * TILE] * unit)
    return jnp.concatenate(pieces, axis=0)


def encode(acc, step, out_ref, code_ref, rows):
    block_rows = acc.shape[0]
    groups = block_rows // TILE
    pieces = []
    for g in range(groups):
        part = acc[g * TILE : (g + 1) * TILE]
        largest = jnp.max(jnp.abs(part), axis=0, keepdims=True)
        code = jnp.ceil(jnp.log(jnp.maximum(largest, 1e-30)) * (STEPS_PER_OCTAVE / 0.6931471805599453))
        scaled = jnp.round(part * (jnp.exp2(-code / STEPS_PER_OCTAVE) * LEVELS))
        pieces.append(jnp.clip(scaled, -LEVELS, LEVELS).astype(jnp.int32))
        code_ref[pl.ds(step * groups + g, 1), :] = code
    start = pl.multiple_of(step * block_rows, block_rows)
    out_ref[pl.ds(start, block_rows), :] = jnp.concatenate(pieces, axis=0).astype(jnp.int16)

    @pl.when(step == pl.num_programs(0) - 1)
    def _():
        out_ref[pl.ds(rows, CODE_ROWS), :] = code_ref[...].astype(jnp.int32).astype(jnp.int16)


def fetch(chosen, core, mine, other, b, first, sem):
    width = mine[0][0].shape[1]
    here = pl.ds(pl.multiple_of(first + core * width, width), width)
    there = pl.ds(pl.multiple_of(first + (1 - core) * width, width), width)
    for j in range(len(mine)):

        @pl.when(chosen == j)
        def _():
            for parts, lanes in ((mine[j], here), (other[j], there)):
                start = 0
                for part in parts:
                    pltpu.make_async_copy(part, b.at[pl.ds(start, part.shape[0]), lanes], sem).start()
                    start += part.shape[0]


def multiply_kernel(slots, kinds, rows, width, sources, facts, a_ref, *refs):
    held, refs = list(refs[: sum(sources)]), refs[sum(sources) :]
    held = [[held.pop(0) for _ in range(parts)] for parts in sources]
    mine, other = held[: len(held) // 2], held[len(held) // 2 :]
    count = sum(len(kind) for kind in kinds)
    outs, refs = list(refs[:count]), refs[count:]
    b, sems, codes = refs[0], refs[1], list(refs[2:])
    step = pl.program_id(0)

    @pl.when(step == 0)
    def _():
        for j, slot in enumerate(slots):
            fetch(facts[slot] ^ facts[CHIP], facts[CORE], mine, other, b, j * width, sems.at[j])
        for j in range(len(slots)):
            span = b.at[:, pl.ds(j * width, width)]
            pltpu.make_async_copy(span, span, sems.at[j]).wait()

    acc = jnp.dot(a_ref[...], b[...], preferred_element_type=jnp.float32)
    for j, kind in enumerate(kinds):
        part = acc[:, j * width : (j + 1) * width]
        for form in kind:
            out_ref = outs.pop(0)
            if form != "plain":
                lanes = {"coded": slice(None), "left": slice(width // 2), "right": slice(width // 2, None)}[form]
                encode(part[:, lanes], step, out_ref, codes.pop(0), rows)
            else:
                out_ref[...] = part


def multiply(facts, masked, columns, slots, kinds):
    rows, depth = masked.shape
    columns = [x if isinstance(x, tuple) else (x,) for x in columns]
    sources = tuple(len(parts) for parts in columns)
    columns = [part for parts in columns for part in parts]
    width = columns[0].shape[1] * 2
    packed = (rows + CODE_ROWS, width)
    forms = [form for kind in kinds for form in kind]
    part = (packed[0], width // 2)
    specs = {
        "coded": (pl.BlockSpec(packed, lambda i, c: (0, 0)), jax.ShapeDtypeStruct(packed, jnp.int16)),
        "plain": (pl.BlockSpec((BLOCK_ROWS, width), lambda i, c: (i, 0)), jax.ShapeDtypeStruct((rows, width), jnp.float32)),
    }
    specs["left"] = specs["right"] = (pl.BlockSpec(part, lambda i, c: (0, 0)), jax.ShapeDtypeStruct(part, jnp.int16))
    outs = [specs[form] for form in forms]
    return pl.pallas_call(
        functools.partial(multiply_kernel, slots, kinds, rows, width, sources),
        out_shape=[shape for _, shape in outs],
        grid_spec=pltpu.PrefetchScalarGridSpec(
            num_scalar_prefetch=1,
            grid=(rows // BLOCK_ROWS,),
            in_specs=[pl.BlockSpec((BLOCK_ROWS, depth), lambda i, c: (i, 0))]
            + [pl.BlockSpec(memory_space=pl.ANY)] * len(columns),
            out_specs=[spec for spec, _ in outs],
            scratch_shapes=[pltpu.VMEM((depth, width * len(slots)), masked.dtype), pltpu.SemaphoreType.DMA((len(slots),))]
            + [pltpu.VMEM((CODE_ROWS, specs[form][1].shape[1]), jnp.float32) for form in forms if form != "plain"],
        ),
        compiler_params=pltpu.CompilerParams(vmem_limit_bytes=24 * 1024 * 1024),
        cost_estimate=pl.CostEstimate(flops=3000000000, bytes_accessed=9000000, transcendentals=0),
    )(facts, masked, *columns)


def add_kernel(terms, rows, facts, *refs):
    step = pl.program_id(0)
    count = sum(parts for _, parts in terms)
    blocks, refs = list(refs[:count]), refs[count:]
    acc = None
    for weight, parts in terms:
        share = facts[weight].astype(jnp.float32)
        block, *more = [blocks.pop(0) for _ in range(parts)]
        if block.dtype == jnp.int16:
            value = jnp.concatenate([decode(x, step, rows, ADD_ROWS, share) for x in (block, *more)], axis=1)
        else:
            value = block[...] if weight == ALWAYS else block[...] * share
        acc = value if acc is None else acc + value
    if refs[0].dtype == jnp.int16:
        encode(acc, step, refs[0], refs[1], rows)
    else:
        refs[0][...] = acc.astype(refs[0].dtype)


def add(facts, terms, dtype=jnp.int16):
    rows, width = terms[0][0].shape
    terms = [(x if isinstance(x, tuple) else (x,), weight) for x, weight in terms]
    blocks = [part for x, _ in terms for part in x]
    packed = (rows + CODE_ROWS, width)
    plain = pl.BlockSpec((ADD_ROWS, width), lambda i, c: (i, 0))
    coded = pl.BlockSpec(packed, lambda i, c: (0, 0))
    if dtype == jnp.int16:
        out_spec, out_shape = coded, jax.ShapeDtypeStruct(packed, dtype)
        scratch = [pltpu.VMEM((CODE_ROWS, width), jnp.float32)]
    else:
        out_spec, out_shape = plain, jax.ShapeDtypeStruct((rows, width), dtype)
        scratch = []
    return pl.pallas_call(
        functools.partial(add_kernel, tuple((weight, len(x)) for x, weight in terms), rows),
        out_shape=out_shape,
        grid_spec=pltpu.PrefetchScalarGridSpec(
            num_scalar_prefetch=1,
            grid=(rows // ADD_ROWS,),
            in_specs=[pl.BlockSpec(x.shape, lambda i, c: (0, 0)) if x.dtype == jnp.int16 else plain for x in blocks],
            out_specs=out_spec,
            scratch_shapes=scratch,
        ),
        compiler_params=pltpu.CompilerParams(vmem_limit_bytes=16 * 1024 * 1024),
        cost_estimate=pl.CostEstimate(flops=3000000000, bytes_accessed=9000000, transcendentals=0),
    )(facts, *blocks)


def plan_of(chip, at):
    end = at in (0, 3)
    far, near = (3, 2) if at < 2 else (0, 1)
    late = chip == (0 if at < 2 else 3)
    passed = (near, far) if late else (far, near)
    home = 0 if at < 2 else 3
    if end:
        first, second, third, relayed = passed[0], passed[1], 3 - near, (chip, chip)
    else:
        straight = chip ^ home != 3
        first, second = (home, chip) if straight else (chip, home)
        third, relayed = chip, passed
    early = chip != (3 if at < 2 else 0)
    return (first, second, third, *relayed, at, 1, int(end and early), int(end and not early), int(not end))


FIRST, SECOND, THIRD, RELAY_ONE, RELAY_TWO, HERE, ALWAYS, EARLY, LATE, INNER, CORE, CHIP = range(12)


def line_pairs(choose):
    return [(row * 4 + a, row * 4 + b) for row in range(8) for a, b in choose(row // 2)]


def line_of_four(amplitudes, integrals, tile_mask):
    row = lax.axis_index("row")
    at = lax.axis_index("col")
    core, chip = row % 2, row // 2

    def after(value, *others):
        return lax.optimization_barrier((value, *others))[0]

    def across(block, bit):
        return lax.ppermute(block, "row", [(i, i ^ bit) for i in range(8)])

    def along(block, choose):
        return lax.ppermute(block, ("row", "col"), line_pairs(choose))

    def pairs(p):
        return [(0, 1), (1, 0), (2, 3), (3, 2)]

    inward = [(0, 1), (3, 2)]

    def second_pairs(p):
        return inward + [(1, 0)] * (p == 3) + [(2, 3)] * (p == 0)

    def relay_one(p):
        return [(1, 2 if p == 0 else 3), (2, 1 if p == 3 else 0)]

    def relay_two(p):
        return [(1, 3 if p == 0 else 2), (2, 0 if p == 3 else 1)]

    by_x, by_y = across(integrals, 2), across(integrals, 4)
    plans = jnp.asarray([plan_of(p, z) for p in range(4) for z in range(4)], jnp.int32)
    planned = lax.dynamic_slice_in_dim(plans, chip * 4 + at, 1)[0]
    facts = jnp.concatenate([planned, jnp.stack([core, chip]).astype(jnp.int32)])
    twin = across(after(integrals, facts), 1)
    masked = apply_mask(amplitudes, tile_mask)
    by_x, by_y = after(by_x, masked, facts), after(by_y, masked, facts)
    half = integrals.shape[0] // 2
    by_both = across(by_y[:half], 2), across(by_x[half:], 4)
    straight = (integrals, by_x, by_y, twin, across(by_x, 1), across(by_y, 1))
    coded, plain = ("coded",), ("plain",)
    out_left, out_right = multiply(facts, masked, straight, (FIRST,), (("left", "right"),))
    one = along(out_left, pairs), along(out_right, pairs)
    (share_one,) = multiply(after(facts, out_right), masked, straight, (RELAY_ONE,), (plain,))
    columns = (*straight[:3], by_both, *straight[3:], tuple(across(after(x, share_one), 1) for x in by_both))
    (out_two,) = multiply(after(facts, share_one, one[0]), masked, columns, (SECOND,), (coded,))
    two = along(out_two, second_pairs)
    out_relay_one = add(after(facts, out_two), [(share_one, ALWAYS), (one, ALWAYS)])
    relayed_one = along(out_relay_one, relay_one)
    out_three, share_two = multiply(
        after(facts, out_relay_one), masked, columns, (THIRD, RELAY_TWO), (coded, plain)
    )
    three = along(out_three, lambda p: inward)
    out_relay_two = add(after(facts, out_three), [(share_two, ALWAYS), (two, ALWAYS)])
    relayed_two = along(out_relay_two, relay_two)
    (own,) = multiply(after(facts, out_relay_two), masked, columns, (HERE,), (plain,))
    most = add(
        facts,
        [(own, ALWAYS), (one, EARLY), (two, LATE), (relayed_one, ALWAYS), (three, INNER)],
        jnp.float32,
    )
    return add(facts, [(most, ALWAYS), (relayed_two, ALWAYS)], jnp.bfloat16)


def solution(mesh):
    body = line_of_four if mesh.shape["col"] == 4 and mesh.shape["row"] == 8 else general
    placed = (P("row", "col"), P("col", "row"), P("row", "col"))
    return jax.shard_map(
        body, mesh=mesh, in_specs=placed, out_specs=P("row", "col"), check_vma=False
    )
```

```python
import functools

import jax
import jax.numpy as jnp
from jax import lax
from jax.experimental import pallas as pl
from jax.experimental.pallas import tpu as pltpu
from jax.sharding import PartitionSpec as P

TILE = 128
CODE_ROWS = 16
LEVELS = 32767.0
STEPS_PER_OCTAVE = 64.0
BLOCK_ROWS = 512
ADD_ROWS = 1024


def apply_mask(amplitudes, tile_mask):
    tiles_m, tiles_k = tile_mask.shape
    tile_rows = amplitudes.shape[0] // tiles_m
    tile_cols = amplitudes.shape[1] // tiles_k
    blocks = amplitudes.reshape(tiles_m, tile_rows, tiles_k, tile_cols)
    weights = tile_mask.astype(amplitudes.dtype)[:, None, :, None]
    return (blocks * weights).reshape(amplitudes.shape)


def general(amplitudes, integrals, tile_mask):
    masked = apply_mask(amplitudes, tile_mask)
    partial_sums = jnp.dot(
        masked,
        lax.all_gather(integrals, "row", axis=1, tiled=True),
        preferred_element_type=jnp.float32,
    )
    summed = lax.psum_scatter(partial_sums, "col", scatter_dimension=1, tiled=True)
    return summed.astype(jnp.bfloat16)


def decode(ref, step, rows, block_rows, weight):
    groups = block_rows // TILE
    start = pl.multiple_of(step * block_rows, block_rows)
    levels = ref[pl.ds(start, block_rows), :].astype(jnp.int32).astype(jnp.float32)
    codes = ref[pl.ds(rows, CODE_ROWS), :].astype(jnp.int32).astype(jnp.float32)
    pieces = []
    which = lax.broadcasted_iota(jnp.int32, codes.shape, 0)
    for g in range(groups):
        code = jnp.sum(jnp.where(which == step * groups + g, codes, 0.0), axis=0, keepdims=True)
        unit = jnp.exp2(code / STEPS_PER_OCTAVE) * (weight / LEVELS)
        pieces.append(levels[g * TILE : (g + 1) * TILE] * unit)
    return jnp.concatenate(pieces, axis=0)


def encode(acc, step, out_ref, code_ref, rows):
    block_rows = acc.shape[0]
    groups = block_rows // TILE
    pieces = []
    for g in range(groups):
        part = acc[g * TILE : (g + 1) * TILE]
        largest = jnp.max(jnp.abs(part), axis=0, keepdims=True)
        code = jnp.ceil(jnp.log(jnp.maximum(largest, 1e-30)) * (STEPS_PER_OCTAVE / 0.6931471805599453))
        scaled = jnp.round(part * (jnp.exp2(-code / STEPS_PER_OCTAVE) * LEVELS))
        pieces.append(jnp.clip(scaled, -LEVELS, LEVELS).astype(jnp.int32))
        code_ref[pl.ds(step * groups + g, 1), :] = code
    start = pl.multiple_of(step * block_rows, block_rows)
    out_ref[pl.ds(start, block_rows), :] = jnp.concatenate(pieces, axis=0).astype(jnp.int16)

    @pl.when(step == pl.num_programs(0) - 1)
    def _():
        out_ref[pl.ds(rows, CODE_ROWS), :] = code_ref[...].astype(jnp.int32).astype(jnp.int16)


def fetch(chosen, core, mine, other, b, first, sem):
    width = mine[0][0].shape[1]
    here = pl.ds(pl.multiple_of(first + core * width, width), width)
    there = pl.ds(pl.multiple_of(first + (1 - core) * width, width), width)
    for j in range(len(mine)):

        @pl.when(chosen == j)
        def _():
            for parts, lanes in ((mine[j], here), (other[j], there)):
                start = 0
                for part in parts:
                    pltpu.make_async_copy(part, b.at[pl.ds(start, part.shape[0]), lanes], sem).start()
                    start += part.shape[0]


def multiply_kernel(slots, kinds, rows, width, sources, facts, a_ref, *refs):
    held, refs = list(refs[: sum(sources)]), refs[sum(sources) :]
    held = [[held.pop(0) for _ in range(parts)] for parts in sources]
    mine, other = held[: len(held) // 2], held[len(held) // 2 :]
    count = sum(len(kind) for kind in kinds)
    outs, refs = list(refs[:count]), refs[count:]
    b, sems, codes = refs[0], refs[1], list(refs[2:])
    step = pl.program_id(0)

    @pl.when(step == 0)
    def _():
        for j, slot in enumerate(slots):
            fetch(facts[slot] ^ facts[CHIP], facts[CORE], mine, other, b, j * width, sems.at[j])
        for j in range(len(slots)):
            span = b.at[:, pl.ds(j * width, width)]
            pltpu.make_async_copy(span, span, sems.at[j]).wait()

    acc = jnp.dot(a_ref[...], b[...], preferred_element_type=jnp.float32)
    for j, kind in enumerate(kinds):
        part = acc[:, j * width : (j + 1) * width]
        for form in kind:
            out_ref = outs.pop(0)
            if form != "plain":
                lanes = {"coded": slice(None), "left": slice(width // 2), "right": slice(width // 2, None)}[form]
                encode(part[:, lanes], step, out_ref, codes.pop(0), rows)
            else:
                out_ref[...] = part


def multiply(facts, masked, columns, slots, kinds):
    rows, depth = masked.shape
    columns = [x if isinstance(x, tuple) else (x,) for x in columns]
    sources = tuple(len(parts) for parts in columns)
    columns = [part for parts in columns for part in parts]
    width = columns[0].shape[1] * 2
    packed = (rows + CODE_ROWS, width)
    forms = [form for kind in kinds for form in kind]
    part = (packed[0], width // 2)
    specs = {
        "coded": (pl.BlockSpec(packed, lambda i, c: (0, 0)), jax.ShapeDtypeStruct(packed, jnp.int16)),
        "plain": (pl.BlockSpec((BLOCK_ROWS, width), lambda i, c: (i, 0)), jax.ShapeDtypeStruct((rows, width), jnp.float32)),
    }
    specs["left"] = specs["right"] = (pl.BlockSpec(part, lambda i, c: (0, 0)), jax.ShapeDtypeStruct(part, jnp.int16))
    outs = [specs[form] for form in forms]
    return pl.pallas_call(
        functools.partial(multiply_kernel, slots, kinds, rows, width, sources),
        out_shape=[shape for _, shape in outs],
        grid_spec=pltpu.PrefetchScalarGridSpec(
            num_scalar_prefetch=1,
            grid=(rows // BLOCK_ROWS,),
            in_specs=[pl.BlockSpec((BLOCK_ROWS, depth), lambda i, c: (i, 0))]
            + [pl.BlockSpec(memory_space=pl.ANY)] * len(columns),
            out_specs=[spec for spec, _ in outs],
            scratch_shapes=[pltpu.VMEM((depth, width * len(slots)), masked.dtype), pltpu.SemaphoreType.DMA((len(slots),))]
            + [pltpu.VMEM((CODE_ROWS, specs[form][1].shape[1]), jnp.float32) for form in forms if form != "plain"],
        ),
        compiler_params=pltpu.CompilerParams(vmem_limit_bytes=24 * 1024 * 1024),
        cost_estimate=pl.CostEstimate(flops=3000000000, bytes_accessed=9000000, transcendentals=0),
    )(facts, masked, *columns)


def add_kernel(terms, rows, facts, *refs):
    step = pl.program_id(0)
    count = sum(parts for _, parts in terms)
    blocks, refs = list(refs[:count]), refs[count:]
    acc = None
    for weight, parts in terms:
        share = facts[weight].astype(jnp.float32)
        block, *more = [blocks.pop(0) for _ in range(parts)]
        if block.dtype == jnp.int16:
            value = jnp.concatenate([decode(x, step, rows, ADD_ROWS, share) for x in (block, *more)], axis=1)
        else:
            value = block[...] if weight == ALWAYS else block[...] * share
        acc = value if acc is None else acc + value
    if refs[0].dtype == jnp.int16:
        encode(acc, step, refs[0], refs[1], rows)
    else:
        refs[0][...] = acc.astype(refs[0].dtype)


def add(facts, terms, dtype=jnp.int16):
    rows, width = terms[0][0].shape
    terms = [(x if isinstance(x, tuple) else (x,), weight) for x, weight in terms]
    blocks = [part for x, _ in terms for part in x]
    packed = (rows + CODE_ROWS, width)
    plain = pl.BlockSpec((ADD_ROWS, width), lambda i, c: (i, 0))
    coded = pl.BlockSpec(packed, lambda i, c: (0, 0))
    if dtype == jnp.int16:
        out_spec, out_shape = coded, jax.ShapeDtypeStruct(packed, dtype)
        scratch = [pltpu.VMEM((CODE_ROWS, width), jnp.float32)]
    else:
        out_spec, out_shape = plain, jax.ShapeDtypeStruct((rows, width), dtype)
        scratch = []
    return pl.pallas_call(
        functools.partial(add_kernel, tuple((weight, len(x)) for x, weight in terms), rows),
        out_shape=out_shape,
        grid_spec=pltpu.PrefetchScalarGridSpec(
            num_scalar_prefetch=1,
            grid=(rows // ADD_ROWS,),
            in_specs=[pl.BlockSpec(x.shape, lambda i, c: (0, 0)) if x.dtype == jnp.int16 else plain for x in blocks],
            out_specs=out_spec,
            scratch_shapes=scratch,
        ),
        compiler_params=pltpu.CompilerParams(vmem_limit_bytes=16 * 1024 * 1024),
        cost_estimate=pl.CostEstimate(flops=3000000000, bytes_accessed=9000000, transcendentals=0),
    )(facts, *blocks)


def plan_of(chip, at):
    end = at in (0, 3)
    far, near = (3, 2) if at < 2 else (0, 1)
    late = chip == (0 if at < 2 else 3)
    passed = (near, far) if late else (far, near)
    home = 0 if at < 2 else 3
    if end:
        first, second, third, relayed = passed[0], passed[1], 3 - near, (chip, chip)
    else:
        straight = chip ^ home != 3
        first, second = (home, chip) if straight else (chip, home)
        third, relayed = chip, passed
    early = chip != (3 if at < 2 else 0)
    return (first, second, third, *relayed, at, 1, int(end and early), int(end and not early), int(not end))


FIRST, SECOND, THIRD, RELAY_ONE, RELAY_TWO, HERE, ALWAYS, EARLY, LATE, INNER, CORE, CHIP = range(12)


def line_pairs(choose):
    return [(row * 4 + a, row * 4 + b) for row in range(8) for a, b in choose(row // 2)]


def line_of_four(amplitudes, integrals, tile_mask):
    row = lax.axis_index("row")
    at = lax.axis_index("col")
    core, chip = row % 2, row // 2

    def after(value, *others):
        return lax.optimization_barrier((value, *others))[0]

    def across(block, bit):
        return lax.ppermute(block, "row", [(i, i ^ bit) for i in range(8)])

    def along(block, choose):
        return lax.ppermute(block, ("row", "col"), line_pairs(choose))

    def pairs(p):
        return [(0, 1), (1, 0), (2, 3), (3, 2)]

    inward = [(0, 1), (3, 2)]

    def second_pairs(p):
        return inward + [(1, 0)] * (p == 3) + [(2, 3)] * (p == 0)

    def relay_one(p):
        return [(1, 2 if p == 0 else 3), (2, 1 if p == 3 else 0)]

    def relay_two(p):
        return [(1, 3 if p == 0 else 2), (2, 0 if p == 3 else 1)]

    by_x, by_y = across(integrals, 2), across(integrals, 4)
    plans = jnp.asarray([plan_of(p, z) for p in range(4) for z in range(4)], jnp.int32)
    planned = lax.dynamic_slice_in_dim(plans, chip * 4 + at, 1)[0]
    facts = jnp.concatenate([planned, jnp.stack([core, chip]).astype(jnp.int32)])
    twin = across(after(integrals, facts), 1)
    masked = apply_mask(amplitudes, tile_mask)
    by_x, by_y = after(by_x, masked, facts), after(by_y, masked, facts)
    half = integrals.shape[0] // 2
    by_both = across(by_y[:half], 2), across(by_x[half:], 4)
    straight = (integrals, by_x, by_y, twin, across(by_x, 1), across(by_y, 1))
    coded, plain = ("coded",), ("plain",)
    out_left, out_right = multiply(facts, masked, straight, (FIRST,), (("left", "right"),))
    one = along(out_left, pairs), along(out_right, pairs)
    (share_one,) = multiply(after(facts, out_right), masked, straight, (RELAY_ONE,), (plain,))
    columns = (*straight[:3], by_both, *straight[3:], tuple(across(after(x, share_one), 1) for x in by_both))
    (out_two,) = multiply(after(facts, share_one, one[0]), masked, columns, (SECOND,), (coded,))
    two = along(out_two, second_pairs)
    out_relay_one = add(after(facts, out_two), [(share_one, ALWAYS), (one, ALWAYS)])
    relayed_one = along(out_relay_one, relay_one)
    out_three, share_two = multiply(
        after(facts, out_relay_one), masked, columns, (THIRD, RELAY_TWO), (coded, plain)
    )
    three = along(out_three, lambda p: inward)
    out_relay_two = add(after(facts, out_three), [(share_two, ALWAYS), (two, ALWAYS)])
    relayed_two = along(out_relay_two, relay_two)
    (own,) = multiply(after(facts, out_relay_two), masked, columns, (HERE,), (plain,))
    most = add(
        facts,
        [(own, ALWAYS), (one, EARLY), (two, LATE), (relayed_one, ALWAYS), (three, INNER)],
        jnp.float32,
    )
    return add(facts, [(most, ALWAYS), (relayed_two, ALWAYS)], jnp.bfloat16)


def solution(mesh):
    body = line_of_four if mesh.shape["col"] == 4 and mesh.shape["row"] == 8 else general
    placed = (P("row", "col"), P("col", "row"), P("row", "col"))
    return jax.shard_map(
        body, mesh=mesh, in_specs=placed, out_specs=P("row", "col"), check_vma=False
    )
```

```python
import functools

import jax
import jax.numpy as jnp
from jax import lax
from jax.experimental import pallas as pl
from jax.experimental.pallas import tpu as pltpu
from jax.sharding import PartitionSpec as P

TILE = 128
CODE_ROWS = 16
LEVELS = 32767.0
STEPS_PER_OCTAVE = 64.0
BLOCK_ROWS = 256
ADD_ROWS = 512


def apply_mask(amplitudes, tile_mask):
    tiles_m, tiles_k = tile_mask.shape
    tile_rows = amplitudes.shape[0] // tiles_m
    tile_cols = amplitudes.shape[1] // tiles_k
    blocks = amplitudes.reshape(tiles_m, tile_rows, tiles_k, tile_cols)
    weights = tile_mask.astype(amplitudes.dtype)[:, None, :, None]
    return (blocks * weights).reshape(amplitudes.shape)


def general(amplitudes, integrals, tile_mask):
    masked = apply_mask(amplitudes, tile_mask)
    partial_sums = jnp.dot(
        masked,
        lax.all_gather(integrals, "row", axis=1, tiled=True),
        preferred_element_type=jnp.float32,
    )
    summed = lax.psum_scatter(partial_sums, "col", scatter_dimension=1, tiled=True)
    return summed.astype(jnp.bfloat16)


def decode(ref, step, rows, block_rows, weight):
    groups = block_rows // TILE
    start = pl.multiple_of(step * block_rows, block_rows)
    levels = ref[pl.ds(start, block_rows), :].astype(jnp.int32).astype(jnp.float32)
    codes = ref[pl.ds(rows, CODE_ROWS), :].astype(jnp.int32).astype(jnp.float32)
    pieces = []
    which = lax.broadcasted_iota(jnp.int32, codes.shape, 0)
    for g in range(groups):
        code = jnp.sum(jnp.where(which == step * groups + g, codes, 0.0), axis=0, keepdims=True)
        unit = jnp.exp2(code / STEPS_PER_OCTAVE) * (weight / LEVELS)
        pieces.append(levels[g * TILE : (g + 1) * TILE] * unit)
    return jnp.concatenate(pieces, axis=0)


def encode(acc, step, out_ref, code_ref, rows):
    block_rows = acc.shape[0]
    groups = block_rows // TILE
    pieces = []
    for g in range(groups):
        part = acc[g * TILE : (g + 1) * TILE]
        largest = jnp.max(jnp.abs(part), axis=0, keepdims=True)
        code = jnp.ceil(jnp.log(jnp.maximum(largest, 1e-30)) * (STEPS_PER_OCTAVE / 0.6931471805599453))
        scaled = jnp.round(part * (jnp.exp2(-code / STEPS_PER_OCTAVE) * LEVELS))
        pieces.append(jnp.clip(scaled, -LEVELS, LEVELS).astype(jnp.int32))
        code_ref[pl.ds(step * groups + g, 1), :] = code
    start = pl.multiple_of(step * block_rows, block_rows)
    out_ref[pl.ds(start, block_rows), :] = jnp.concatenate(pieces, axis=0).astype(jnp.int16)

    @pl.when(step == pl.num_programs(0) - 1)
    def _():
        out_ref[pl.ds(rows, CODE_ROWS), :] = code_ref[...].astype(jnp.int32).astype(jnp.int16)


def fetch(chosen, core, mine, other, b, first, sem):
    width = mine[0][0].shape[1]
    here = pl.ds(pl.multiple_of(first + core * width, width), width)
    there = pl.ds(pl.multiple_of(first + (1 - core) * width, width), width)
    for j in range(len(mine)):

        @pl.when(chosen == j)
        def _():
            for parts, lanes in ((mine[j], here), (other[j], there)):
                start = 0
                for part in parts:
                    pltpu.make_async_copy(part, b.at[pl.ds(start, part.shape[0]), lanes], sem).start()
                    start += part.shape[0]


def multiply_kernel(slots, kinds, rows, width, sources, facts, a_ref, *refs):
    held, refs = list(refs[: sum(sources)]), refs[sum(sources) :]
    held = [[held.pop(0) for _ in range(parts)] for parts in sources]
    mine, other = held[: len(held) // 2], held[len(held) // 2 :]
    count = sum(len(kind) for kind in kinds)
    outs, refs = list(refs[:count]), refs[count:]
    b, sems, codes = refs[0], refs[1], list(refs[2:])
    step = pl.program_id(0)

    @pl.when(step == 0)
    def _():
        for j, slot in enumerate(slots):
            fetch(facts[slot] ^ facts[CHIP], facts[CORE], mine, other, b, j * width, sems.at[j])
        for j in range(len(slots)):
            span = b.at[:, pl.ds(j * width, width)]
            pltpu.make_async_copy(span, span, sems.at[j]).wait()

    acc = jnp.dot(a_ref[...], b[...], preferred_element_type=jnp.float32)
    for j, kind in enumerate(kinds):
        part = acc[:, j * width : (j + 1) * width]
        for form in kind:
            out_ref = outs.pop(0)
            if form != "plain":
                lanes = {"coded": slice(None), "left": slice(width // 2), "right": slice(width // 2, None)}[form]
                encode(part[:, lanes], step, out_ref, codes.pop(0), rows)
            else:
                out_ref[...] = part


def multiply(facts, masked, columns, slots, kinds):
    rows, depth = masked.shape
    columns = [x if isinstance(x, tuple) else (x,) for x in columns]
    sources = tuple(len(parts) for parts in columns)
    columns = [part for parts in columns for part in parts]
    width = columns[0].shape[1] * 2
    packed = (rows + CODE_ROWS, width)
    forms = [form for kind in kinds for form in kind]
    part = (packed[0], width // 2)
    specs = {
        "coded": (pl.BlockSpec(packed, lambda i, c: (0, 0)), jax.ShapeDtypeStruct(packed, jnp.int16)),
        "plain": (pl.BlockSpec((BLOCK_ROWS, width), lambda i, c: (i, 0)), jax.ShapeDtypeStruct((rows, width), jnp.float32)),
    }
    specs["left"] = specs["right"] = (pl.BlockSpec(part, lambda i, c: (0, 0)), jax.ShapeDtypeStruct(part, jnp.int16))
    outs = [specs[form] for form in forms]
    return pl.pallas_call(
        functools.partial(multiply_kernel, slots, kinds, rows, width, sources),
        out_shape=[shape for _, shape in outs],
        grid_spec=pltpu.PrefetchScalarGridSpec(
            num_scalar_prefetch=1,
            grid=(rows // BLOCK_ROWS,),
            in_specs=[pl.BlockSpec((BLOCK_ROWS, depth), lambda i, c: (i, 0))]
            + [pl.BlockSpec(memory_space=pl.ANY)] * len(columns),
            out_specs=[spec for spec, _ in outs],
            scratch_shapes=[pltpu.VMEM((depth, width * len(slots)), masked.dtype), pltpu.SemaphoreType.DMA((len(slots),))]
            + [pltpu.VMEM((CODE_ROWS, specs[form][1].shape[1]), jnp.float32) for form in forms if form != "plain"],
        ),
        compiler_params=pltpu.CompilerParams(vmem_limit_bytes=24 * 1024 * 1024),
        cost_estimate=pl.CostEstimate(flops=3000000000, bytes_accessed=9000000, transcendentals=0),
    )(facts, masked, *columns)


def add_kernel(terms, rows, facts, *refs):
    step = pl.program_id(0)
    count = sum(parts for _, parts in terms)
    blocks, refs = list(refs[:count]), refs[count:]
    acc = None
    for weight, parts in terms:
        share = facts[weight].astype(jnp.float32)
        block, *more = [blocks.pop(0) for _ in range(parts)]
        if block.dtype == jnp.int16:
            value = jnp.concatenate([decode(x, step, rows, ADD_ROWS, share) for x in (block, *more)], axis=1)
        else:
            value = block[...] if weight == ALWAYS else block[...] * share
        acc = value if acc is None else acc + value
    if refs[0].dtype == jnp.int16:
        encode(acc, step, refs[0], refs[1], rows)
    else:
        refs[0][...] = acc.astype(refs[0].dtype)


def add(facts, terms, dtype=jnp.int16):
    rows, width = terms[0][0].shape
    terms = [(x if isinstance(x, tuple) else (x,), weight) for x, weight in terms]
    blocks = [part for x, _ in terms for part in x]
    packed = (rows + CODE_ROWS, width)
    plain = pl.BlockSpec((ADD_ROWS, width), lambda i, c: (i, 0))
    coded = pl.BlockSpec(packed, lambda i, c: (0, 0))
    if dtype == jnp.int16:
        out_spec, out_shape = coded, jax.ShapeDtypeStruct(packed, dtype)
        scratch = [pltpu.VMEM((CODE_ROWS, width), jnp.float32)]
    else:
        out_spec, out_shape = plain, jax.ShapeDtypeStruct((rows, width), dtype)
        scratch = []
    return pl.pallas_call(
        functools.partial(add_kernel, tuple((weight, len(x)) for x, weight in terms), rows),
        out_shape=out_shape,
        grid_spec=pltpu.PrefetchScalarGridSpec(
            num_scalar_prefetch=1,
            grid=(rows // ADD_ROWS,),
            in_specs=[pl.BlockSpec(x.shape, lambda i, c: (0, 0)) if x.dtype == jnp.int16 else plain for x in blocks],
            out_specs=out_spec,
            scratch_shapes=scratch,
        ),
        compiler_params=pltpu.CompilerParams(vmem_limit_bytes=16 * 1024 * 1024),
        cost_estimate=pl.CostEstimate(flops=3000000000, bytes_accessed=9000000, transcendentals=0),
    )(facts, *blocks)


def plan_of(chip, at):
    end = at in (0, 3)
    far, near = (3, 2) if at < 2 else (0, 1)
    late = chip == (0 if at < 2 else 3)
    passed = (near, far) if late else (far, near)
    home = 0 if at < 2 else 3
    if end:
        first, second, third, relayed = passed[0], passed[1], 3 - near, (chip, chip)
    else:
        straight = chip ^ home != 3
        first, second = (home, chip) if straight else (chip, home)
        third, relayed = chip, passed
    early = chip != (3 if at < 2 else 0)
    return (first, second, third, *relayed, at, 1, int(end and early), int(end and not early), int(not end))


FIRST, SECOND, THIRD, RELAY_ONE, RELAY_TWO, HERE, ALWAYS, EARLY, LATE, INNER, CORE, CHIP = range(12)


def line_pairs(choose):
    return [(row * 4 + a, row * 4 + b) for row in range(8) for a, b in choose(row // 2)]


def line_of_four(amplitudes, integrals, tile_mask):
    row = lax.axis_index("row")
    at = lax.axis_index("col")
    core, chip = row % 2, row // 2

    def after(value, *others):
        return lax.optimization_barrier((value, *others))[0]

    def across(block, bit):
        return lax.ppermute(block, "row", [(i, i ^ bit) for i in range(8)])

    def along(block, choose):
        return lax.ppermute(block, ("row", "col"), line_pairs(choose))

    def pairs(p):
        return [(0, 1), (1, 0), (2, 3), (3, 2)]

    inward = [(0, 1), (3, 2)]

    def second_pairs(p):
        return inward + [(1, 0)] * (p == 3) + [(2, 3)] * (p == 0)

    def relay_one(p):
        return [(1, 2 if p == 0 else 3), (2, 1 if p == 3 else 0)]

    def relay_two(p):
        return [(1, 3 if p == 0 else 2), (2, 0 if p == 3 else 1)]

    by_x, by_y = across(integrals, 2), across(integrals, 4)
    plans = jnp.asarray([plan_of(p, z) for p in range(4) for z in range(4)], jnp.int32)
    planned = lax.dynamic_slice_in_dim(plans, chip * 4 + at, 1)[0]
    facts = jnp.concatenate([planned, jnp.stack([core, chip]).astype(jnp.int32)])
    twin = across(after(integrals, facts), 1)
    masked = apply_mask(amplitudes, tile_mask)
    by_x, by_y = after(by_x, masked, facts), after(by_y, masked, facts)
    half = integrals.shape[0] // 2
    by_both = across(by_y[:half], 2), across(by_x[half:], 4)
    straight = (integrals, by_x, by_y, twin, across(by_x, 1), across(by_y, 1))
    coded, plain = ("coded",), ("plain",)
    out_left, out_right = multiply(facts, masked, straight, (FIRST,), (("left", "right"),))
    one = along(out_left, pairs), along(out_right, pairs)
    (share_one,) = multiply(after(facts, out_right), masked, straight, (RELAY_ONE,), (plain,))
    columns = (*straight[:3], by_both, *straight[3:], tuple(across(after(x, share_one), 1) for x in by_both))
    (out_two,) = multiply(after(facts, share_one, one[0]), masked, columns, (SECOND,), (coded,))
    two = along(out_two, second_pairs)
    out_relay_one = add(after(facts, out_two), [(share_one, ALWAYS), (one, ALWAYS)])
    relayed_one = along(out_relay_one, relay_one)
    out_three, share_two = multiply(
        after(facts, out_relay_one), masked, columns, (THIRD, RELAY_TWO), (coded, plain)
    )
    three = along(out_three, lambda p: inward)
    out_relay_two = add(after(facts, out_three), [(share_two, ALWAYS), (two, ALWAYS)])
    relayed_two = along(out_relay_two, relay_two)
    (own,) = multiply(after(facts, out_relay_two), masked, columns, (HERE,), (plain,))
    most = add(
        facts,
        [(own, ALWAYS), (one, EARLY), (two, LATE), (relayed_one, ALWAYS), (three, INNER)],
        jnp.float32,
    )
    return add(facts, [(most, ALWAYS), (relayed_two, ALWAYS)], jnp.bfloat16)


def solution(mesh):
    body = line_of_four if mesh.shape["col"] == 4 and mesh.shape["row"] == 8 else general
    placed = (P("row", "col"), P("col", "row"), P("row", "col"))
    return jax.shard_map(
        body, mesh=mesh, in_specs=placed, out_specs=P("row", "col"), check_vma=False
    )
```
